512 devices in a mesh: segment: 4 (over x_hi, core), dp: 128 (over z, y, x_lo).
Axes of the slice: x: 4 (x_hi: 2, x_lo: 2; x = x_hi * 2 + x_lo), y: 4, z: 16, core: 2. Of those that a mesh axis runs over, the one named last changes fastest.
Arguments:
- inputs: bfloat16 [4, 128, 4, 16, 256], P(None, 'dp'), may hold values from -6 to 6
- out_grad: bfloat16 [4, 128, 4, 16, 256], P(None, 'dp'), may hold values from -6 to 6
- w_in: bfloat16 [4, 256, 1024], P('segment'), may hold values from -0.375 to 0.375
- w_out: bfloat16 [4, 1024, 256], P('segment'), may hold values from -0.1875 to 0.1875
- vector_params: float32 [4, 58, 256], P('segment'), may hold values from -2 to 2, as said below
Outputs:
- input_grads: bfloat16 [4, 4, 128, 4, 16, 256], P('segment', None, 'dp')
- step_w_in: float32 [4, 256, 1024], P('segment')
- step_w_out: float32 [4, 1024, 256], P('segment')
- step_vectors: float32 [4, 58, 256], P('segment')
The draws below stay inside these ranges and needn't reach their ends.
Inputs may be any that keep to these rules, and one draw needn't show every extreme that they name: `vector_params`: rows 0 to 48 are taps of order 0.2, row 50 lies in 0.5 to 1.5, row 53 in 0.2 to 1, the other rows are biases of order 0.5.
All inputs are finite; a program needn't handle non-finite values.
Results may differ from the reference program's by a relative error of at most 0.0095.
Values may be sent and summed in bfloat16 or wider, within the bound.
A program may use at most 128 MiB of HBM per device.

```python
import jax
import jax.numpy as jnp
from jax import lax

C = 256
H = 4
W = 16
MB = 4
VROWS = 58
SAMPLES = 128
PARAMS = 2156544
N_SEGMENT = 4


def draw_vector_params(key, part):
    shape = (N_SEGMENT, VROWS, C)
    normal_part = jnp.clip(jax.random.normal(jax.random.fold_in(key, 11), shape, jnp.float32), -4.0, 4.0)
    even_part = jax.random.uniform(jax.random.fold_in(key, 12), shape, jnp.float32)
    base = normal_part
    kernel = 0.2 * base
    biases = 0.5 * base
    gains = 0.5 + even_part
    scales = jnp.exp(jnp.log(0.2) + even_part * jnp.log(5.0))
    rows = jnp.arange(VROWS)[None, :, None]
    chosen = jnp.where(rows < 49, kernel, jnp.where(rows == 50, gains, jnp.where(rows == 53, scales, biases)))
    return chosen.astype(jnp.float32)


def steps_of(rng, extent, shards, least, largest):
    loudness = 1.0
    for position, parts in shards:
        heights = jax.random.uniform(jax.random.fold_in(jax.random.fold_in(rng, 6), position), (parts,), jnp.float32, least / len(shards), largest / len(shards))
        loudness = loudness * jnp.repeat(jnp.exp(heights), extent[position] // parts).reshape((-1,) + (1,) * (len(extent) - 1 - position))
    return loudness


def scatter_about(stream_key, extent, scale, reach, cuts=(), kind=jnp.bfloat16):
    level = steps_of(stream_key, extent, cuts, -0.22, 0.18) if cuts else 1.0
    entries = jax.random.normal(stream_key, extent, jnp.float32) * scale * level
    return jnp.minimum(jnp.maximum(entries, -reach), reach).astype(kind)


def setup_inputs(seed: int = 0) -> dict:
    seeds = jax.random.split(jax.random.key(seed), 6)
    inputs = scatter_about(seeds[0], (MB, SAMPLES, H, W, C), 1.0, 6.0, ((1, 128),))
    out_grad = scatter_about(seeds[1], (MB, SAMPLES, H, W, C), 1.0, 6.0, ((1, 128),))
    w_in = scatter_about(seeds[2], (N_SEGMENT, C, 4 * C), C ** -0.5, 0.375, ((0, 4),))
    w_out = scatter_about(seeds[3], (N_SEGMENT, 4 * C, C), (4 * C) ** -0.5, 0.1875, ((0, 4),))
    vector_params = draw_vector_params(jax.random.fold_in(seeds[5], 71), 0)
    return {"inputs": inputs, "out_grad": out_grad, "w_in": w_in, "w_out": w_out, "vector_params": vector_params}


def depthwise(features, vectors):
    height = features.shape[1]
    breadth = features.shape[2]
    padded = jnp.pad(features, ((0, 0), (3, 3), (3, 3), (0, 0)))
    summed = jnp.zeros(features.shape, jnp.float32)
    for row_shift in range(7):
        for col_shift in range(7):
            summed = summed + padded[:, row_shift:row_shift + height, col_shift:col_shift + breadth, :] * vectors[row_shift * 7 + col_shift]
    return summed + vectors[49]

def normalize(features, vectors):
    conv = depthwise(features, vectors)
    average = lax.optimization_barrier(jnp.mean(conv, axis=-1, keepdims=True))
    centered = conv - average
    variance = lax.optimization_barrier(jnp.mean(centered * centered, axis=-1, keepdims=True))
    return centered * lax.rsqrt(variance + 1e-06) * vectors[50] + vectors[51]

def gelu_slope(preact):
    cumulative = 0.5 * (1.0 + jax.scipy.special.erf(preact * 0.7071067811865476))
    return cumulative + preact * jnp.exp(-0.5 * preact * preact) * 0.3989422804014327

def forward_block(features, first_weight, second_weight, vectors):
    width = features.shape[-1]
    normed = normalize(features.astype(jnp.float32), vectors).astype(jnp.bfloat16).reshape(-1, width)
    preact = jnp.dot(normed, first_weight, preferred_element_type=jnp.float32) + vectors[54:58].reshape(-1)
    activated = jax.nn.gelu(preact, approximate=False).astype(jnp.bfloat16)
    projected = jnp.dot(activated, second_weight, preferred_element_type=jnp.float32) + vectors[52]
    output = (features.astype(jnp.float32) + vectors[53] * projected.reshape(features.shape)).astype(jnp.bfloat16)
    return (output, normed, preact, activated, projected)

def backward_block(features, upstream, first_weight, second_weight, vectors, normed, preact, activated, projected):
    width = features.shape[-1]
    flat_up = upstream.astype(jnp.float32).reshape(-1, width)
    grad_scale = lax.optimization_barrier(jnp.sum(flat_up * projected, axis=0))
    dproj = flat_up * vectors[53]
    grad_bias_out = lax.optimization_barrier(jnp.sum(dproj, axis=0))
    dproj_b = dproj.astype(jnp.bfloat16)
    grad_second = lax.dot_general(activated, dproj_b, (((0,), (0,)), ((), ())), preferred_element_type=jnp.float32)
    dact = lax.dot_general(dproj_b, second_weight, (((1,), (1,)), ((), ())), preferred_element_type=jnp.float32)
    dpre = dact * gelu_slope(preact)
    grad_bias_in = lax.optimization_barrier(jnp.sum(dpre, axis=0))
    dpre_b = dpre.astype(jnp.bfloat16)
    grad_first = lax.dot_general(normed, dpre_b, (((0,), (0,)), ((), ())), preferred_element_type=jnp.float32)
    dnormed = lax.dot_general(dpre_b, first_weight, (((1,), (1,)), ((), ())), preferred_element_type=jnp.float32)
    unused, pullback = jax.vjp(normalize, features.astype(jnp.float32), vectors)
    grad_field, grad_small = pullback(dnormed.reshape(features.shape))
    grad_small = grad_small.at[52].add(grad_bias_out).at[53].add(grad_scale).at[54:58].add(grad_bias_in.reshape(4, width))
    down_grad = (grad_field + flat_up.reshape(features.shape)).astype(jnp.bfloat16)
    return (down_grad, grad_first, grad_second, grad_small)

def reference(inputs, out_grad, w_in, w_out, vector_params):
    sections = w_in.shape[0]
    sums_first = [jnp.zeros(w_in.shape[1:], jnp.float32) for index in range(sections)]
    sums_second = [jnp.zeros(w_out.shape[1:], jnp.float32) for index in range(sections)]
    sums_small = [jnp.zeros(vector_params.shape[1:], jnp.float32) for index in range(sections)]
    per_micro = []
    for micro_index in range(inputs.shape[0]):
        features = inputs[micro_index]
        kept = []
        for section in range(sections):
            kept.append(features)
            features = forward_block(features, w_in[section], w_out[section], vector_params[section])[0]
        upstream = out_grad[micro_index]
        segment_grads = [None] * sections
        for section in reversed(range(sections)):
            stash = forward_block(kept[section], w_in[section], w_out[section], vector_params[section])[1:]
            down_grad, grad_first, grad_second, grad_small = backward_block(kept[section], upstream, w_in[section], w_out[section], vector_params[section], *stash)
            sums_first[section] = sums_first[section] + grad_first
            sums_second[section] = sums_second[section] + grad_second
            sums_small[section] = sums_small[section] + grad_small
            segment_grads[section] = down_grad
            upstream = down_grad
        per_micro.append(jnp.stack(segment_grads))
    input_grads = jnp.stack(per_micro, axis=1)
    first_all = jnp.stack(sums_first)
    second_all = jnp.stack(sums_second)
    small_all = jnp.stack(sums_small)
    squares = jnp.sum(first_all * first_all) + jnp.sum(second_all * second_all) + jnp.sum(small_all * small_all)
    factor = jnp.minimum(1.0, jnp.sqrt(jnp.float32(PARAMS)) * lax.rsqrt(squares + 1e-06))
    return (input_grads, factor * first_all, factor * second_all, factor * small_all)
```

```python
import functools

import jax
import jax.numpy as jnp
from jax import lax
from jax.experimental import pallas as pl
from jax.experimental.pallas import tpu as pltpu
from jax.sharding import Mesh
from jax.sharding import PartitionSpec as P

F32 = jnp.float32
BF16 = jnp.bfloat16
VTILE = 16
VPAD = 64


def dot(a, b):
    return jnp.dot(a, b, preferred_element_type=F32)


def dot_nt(a, b):
    return lax.dot_general(a, b, (((1,), (1,)), ((), ())), preferred_element_type=F32)


def dot_tn(a, b):
    return lax.dot_general(a, b, (((0,), (0,)), ((), ())), preferred_element_type=F32)


def over_rows(a):
    return jnp.sum(a, axis=0, keepdims=True)


def relay_kernel(
    dims, x_ref, g_ref, win_ref, wout_ref, vec_ref, gath_ref, fac_ref, ig_ref,
    win, wout, vec, X, G, xpad, cv, XH, RSTD, NB, ACT, SL, PJ,
    PIN, POUT, GV, RIN, ROUT, RV, IG, S, RB, ZB, VZ, GATH, SQ,
    load_sem, wsend, wrecv, hsend, hrecv, isend, irecv, csend, crecv,
    psend, precv, zsend, zrecv, vsend, vrecv, bsend, brecv, asend, arecv, gsend, grecv,
    qsend, qrecv,
):
    nz, ny, nx, params = dims
    nplane = ny * nx
    core = lax.axis_index("core")
    sx = lax.axis_index("sx")
    z = lax.axis_index("z")
    y = lax.axis_index("y")
    xl = lax.axis_index("xl")
    plane = y * nx + xl
    pair, height, width, chans = X.shape[1:]
    rows = pair * height * width
    hidden = win.shape[2]
    quarters = hidden // chans
    in_rows = chans // nplane
    out_rows = hidden // nplane
    part = in_rows * quarters + out_rows
    zrows = part // nz
    vlanes = VPAD * chans // nplane // VTILE
    vcols = chans // vlanes
    owner = lax.rem(2 * plane + core, nz)

    def copy(src, dst, ss, rs, dev):
        return pltpu.make_async_remote_copy(
            src_ref=src, dst_ref=dst, send_sem=ss, recv_sem=rs,
            device_id=dev, device_id_type=pl.DeviceIdType.MESH,
        )

    sib = {"core": 1 - core}
    far = {"sx": 1 - sx}
    diag = {"core": 1 - core, "sx": 1 - sx}

    def plane_dev(r):
        q = lax.rem(plane + r, nplane)
        return q, {"y": q // nx, "xl": lax.rem(q, nx)}

    def z_dev(r):
        q = lax.rem(z + r, nz)
        return q, {"z": q}

    loads = [
        pltpu.make_async_copy(vec_ref, vec.at[core], load_sem.at[0]),
        pltpu.make_async_copy(win_ref, win.at[core], load_sem.at[1]),
        pltpu.make_async_copy(wout_ref, wout.at[core], load_sem.at[2]),
    ]
    for c in loads:
        c.start()

    barrier = pltpu.get_barrier_semaphore()

    def hello(dev):
        pl.semaphore_signal(barrier, inc=1, device_id=dev, device_id_type=pl.DeviceIdType.MESH)

    hello(sib)
    hello(far)
    hello(diag)

    @pl.loop(1, nplane)
    def _(r):
        hello(plane_dev(r)[1])

    @pl.loop(1, nz)
    def _(r):
        hello(z_dev(r)[1])

    zero_side = jnp.zeros((pair, height, 8, chans), F32)
    xpad[:, :, 0:8, :] = zero_side
    xpad[:, :, 8 + width : 16 + width, :] = zero_side
    GV[...] = jnp.zeros(GV.shape, F32)
    GATH[plane, part:, :] = jnp.zeros((VTILE, chans), BF16)

    @pl.when(sx == 0)
    def _():
        X[0] = x_ref[pl.ds(core * pair, pair)]

    @pl.when(sx == 1)
    def _():
        G[2] = g_ref[pl.ds(core * pair, pair)]

    pl.semaphore_wait(barrier, 3 + (nplane - 1) + (nz - 1))

    wcopies = [
        copy(vec_ref, vec.at[core], wsend.at[0], wrecv.at[0], sib),
        copy(win_ref, win.at[core], wsend.at[1], wrecv.at[1], sib),
        copy(wout_ref, wout.at[core], wsend.at[2], wrecv.at[2], sib),
    ]
    for c in wcopies:
        c.start()

    def hop_x():
        return copy(X.at[2], X.at[0], hsend, hrecv, far)

    def hop_g():
        return copy(G.at[0], G.at[2], hsend, hrecv, far)

    @pl.when(sx == 1)
    def _():
        hop_x().wait_recv()

    def row(k, t):
        return vec[k, t : t + 1, :]

    def forward(k, carry):
        @pl.when(core == k)
        def _():
            for c in loads:
                c.wait()

        @pl.when(core != k)
        def _():
            for c in wcopies:
                c.wait_recv()

        xpad[:, :, 8 : 8 + width, :] = X[k].astype(F32)
        for half in range(chans // 128):
            lanes = slice(half * 128, half * 128 + 128)
            acc = [None] * height
            for j in range(7):
                shifted = [xpad[:, h, 5 + j : 5 + j + width, lanes] for h in range(height)]
                for i in range(7):
                    tap = vec[k, 7 * i + j : 7 * i + j + 1, lanes][None]
                    for h in range(height):
                        if 0 <= h + i - 3 < height:
                            term = shifted[h + i - 3] * tap
                            acc[h] = term if acc[h] is None else acc[h] + term
            bias = vec[k, 49:50, lanes][None]
            for h in range(height):
                cv[:, h, :, lanes] = acc[h] + bias
        conv = cv[...].reshape(rows, chans)
        mean = jnp.sum(conv, axis=1, keepdims=True) * (1.0 / chans)
        centered = conv - mean
        var = jnp.sum(centered * centered, axis=1, keepdims=True) * (1.0 / chans)
        rstd = lax.rsqrt(var + 1e-06)
        xhat = centered * rstd
        XH[k] = xhat
        RSTD[k] = jnp.broadcast_to(rstd, (rows, 128))
        normed = (xhat * row(k, 50) + row(k, 51)).astype(BF16)
        NB[k] = normed
        proj = jnp.zeros((rows, chans), F32)
        for q in range(quarters):
            cols = slice(q * chans, (q + 1) * chans)
            pre = dot(normed, win[k, :, cols]) + row(k, 54 + q)
            cumulative = 0.5 * (1.0 + lax.erf(pre * 0.7071067811865476))
            act = (pre * cumulative).astype(BF16)
            ACT[k, :, cols] = act
            SL[k, :, cols] = cumulative + pre * jnp.exp(-0.5 * pre * pre) * 0.3989422804014327
            proj = proj + dot(act, wout[k, cols, :])
        proj = proj + row(k, 52)
        PJ[k] = proj
        out = X[k].astype(F32).reshape(rows, chans) + row(k, 53) * proj
        X[k + 1] = out.astype(BF16).reshape(pair, height, width, chans)
        return carry

    lax.fori_loop(0, 2, forward, 0)

    @pl.when(sx == 0)
    def _():
        hop_x().start()
        hop_g().wait_recv()

    def grad_copies(k):
        return [
            copy(POUT.at[k], ROUT, csend.at[0], crecv.at[0], sib),
            copy(PIN.at[k], RIN, csend.at[1], crecv.at[1], sib),
            copy(GV.at[k], RV, csend.at[2], crecv.at[2], sib),
        ]

    def ig_copy(k):
        return copy(G.at[k], IG.at[pl.ds(core * pair, pair)], isend, irecv, sib)

    def plane_copy(r):
        q, dev = plane_dev(r)
        return copy(S.at[q], RB.at[r], psend.at[r], precv.at[r], dev)

    def chip_sum(k):
        for c in grad_copies(k):
            c.wait_recv()

        for t in range(nplane):
            at_row, at_col = (t // vcols) * VTILE, (t % vcols) * vlanes
            tile = (slice(at_row, at_row + VTILE), slice(at_col, at_col + vlanes))
            S[t, part:, :] = jnp.zeros((VTILE, chans), BF16)
            S[t, part:, 0:vlanes] = (GV[(k,) + tile] + RV[tile]).astype(BF16)

        @pl.loop(1, nplane + 1)
        def _(r):
            q = lax.rem(plane + r, nplane)
            at = pl.ds(pl.multiple_of(q * in_rows, in_rows), in_rows)
            for t in range(quarters):
                cols = slice(t * chans, (t + 1) * chans)
                S[q, t * in_rows : (t + 1) * in_rows, :] = (
                    PIN[k, at, cols].astype(F32) + RIN[at, cols].astype(F32)
                ).astype(BF16)
            at = pl.ds(pl.multiple_of(q * out_rows, out_rows), out_rows)
            S[q, quarters * in_rows : part, :] = (
                POUT[k, at, :].astype(F32) + ROUT[at, :].astype(F32)
            ).astype(BF16)

            @pl.when(r < nplane)
            def _():
                plane_copy(r).start()

    def backward(step, carry):
        k = 1 - step
        gf = G[k + 1].astype(F32).reshape(rows, chans)
        GV[k, 53:54, :] = over_rows(gf * PJ[k])
        dproj = gf * row(k, 53)
        GV[k, 52:53, :] = over_rows(dproj)
        dproj_b = dproj.astype(BF16)
        normed = NB[k]
        dn = jnp.zeros((rows, chans), F32)
        for q in range(quarters):
            cols = slice(q * chans, (q + 1) * chans)
            dact = dot_nt(dproj_b, wout[k, cols, :])
            POUT[k, cols, :] = dot_tn(ACT[k, :, cols], dproj_b).astype(BF16)
            dpre = dact * SL[k, :, cols]
            GV[k, 54 + q : 55 + q, :] = over_rows(dpre)
            dpre_b = dpre.astype(BF16)
            PIN[k, :, cols] = dot_tn(normed, dpre_b).astype(BF16)
            dn = dn + dot_nt(dpre_b, win[k, :, cols])

        @pl.when(core != k)
        def _():
            for c in grad_copies(k)[:2]:
                c.start()

        @pl.when((core == 1) & (k == 0))
        def _():
            chip_sum(1)

        xhat = XH[k]
        GV[k, 50:51, :] = over_rows(dn * xhat)
        GV[k, 51:52, :] = over_rows(dn)
        dxh = dn * row(k, 50)
        m1 = jnp.sum(dxh, axis=1, keepdims=True) * (1.0 / chans)
        m2 = jnp.sum(dxh * xhat, axis=1, keepdims=True) * (1.0 / chans)
        rstd = RSTD[k][:, 0:1]
        dconv = (dxh - m1 - xhat * m2) * rstd
        GV[k, 49:50, :] = over_rows(dconv)
        xpad[:, :, 8 : 8 + width, :] = dconv.reshape(pair, height, width, chans)
        for half in range(chans // 128):
            lanes = slice(half * 128, half * 128 + 128)
            acc = [G[k + 1, :, h, :, lanes].astype(F32) for h in range(height)]
            xs = [X[k, :, h, :, lanes].astype(F32) for h in range(height)]
            for j in range(7):
                shifted = [xpad[:, h, 11 - j : 11 - j + width, lanes] for h in range(height)]
                for i in range(7):
                    t = 7 * i + j
                    tap = vec[k, t : t + 1, lanes][None]
                    total = None
                    for h in range(height):
                        if 0 <= h - i + 3 < height:
                            acc[h] = acc[h] + shifted[h - i + 3] * tap
                            term = xs[h] * shifted[h - i + 3]
                            total = term if total is None else total + term
                    GV[k, t : t + 1, lanes] = over_rows(total.reshape(pair * width, 128))
            for h in range(height):
                G[k, :, h, :, lanes] = acc[h].astype(BF16)

        @pl.when(core != k)
        def _():
            grad_copies(k)[2].start()
            ig_copy(k).start()

        @pl.when(core == k)
        def _():
            IG[pl.ds(core * pair, pair)] = G[k]

        return carry

    lax.fori_loop(0, 2, backward, 0)

    @pl.when(sx == 1)
    def _():
        hop_g().start()

    @pl.when(core == 0)
    def _():
        chip_sum(0)

    def z_copy(r):
        q, dev = z_dev(r)
        src = S.at[plane, pl.ds(pl.multiple_of(q * zrows, zrows), zrows)]
        return copy(src, ZB.at[r], zsend.at[r], zrecv.at[r], dev)

    @pl.loop(1, nplane)
    def _(r):
        plane_copy(r).wait_recv()

    def vec_up():
        r = lax.rem(owner - z + nz, nz)
        src = S.at[plane, pl.ds(part, VTILE), pl.ds(0, vlanes)]
        return copy(src, VZ.at[r], vsend, vrecv.at[r], {"z": owner})

    vacc = S[plane, part:, 0:vlanes].astype(F32)
    for r in range(1, nplane):
        vacc = vacc + RB[r, part:, 0:vlanes].astype(F32)
    S[plane, part:, 0:vlanes] = vacc.astype(BF16)

    @pl.when(z != owner)
    def _():
        vec_up().start()

    @pl.loop(1, nz + 1)
    def _(r):
        q = lax.rem(z + r, nz)
        at = pl.ds(pl.multiple_of(q * zrows, zrows), zrows)
        acc = S[plane, at, :].astype(F32)
        for t in range(1, nplane):
            acc = acc + RB[t, at, :].astype(F32)
        S[plane, at, :] = acc.astype(BF16)

        @pl.when(r < nz)
        def _():
            z_copy(r).start()

    mine = pl.ds(pl.multiple_of(z * zrows, zrows), zrows)

    def share_copy(r):
        _, dev = z_dev(r)
        return copy(GATH.at[plane, mine], GATH.at[plane, mine], asend.at[r], arecv.at[r], dev)

    @pl.loop(1, nz)
    def _(r):
        z_copy(r).wait_recv()

    acc = S[plane, mine, :].astype(F32)
    for r in range(1, nz):
        acc = acc + ZB[r].astype(F32)
    GATH[plane, mine, :] = acc.astype(BF16)

    @pl.loop(1, nz)
    def _(r):
        share_copy(r).start()

    vtile = (plane, pl.ds(part, VTILE), pl.ds(0, vlanes))

    def vec_down(r):
        _, dev = z_dev(r)
        return copy(GATH.at[vtile], GATH.at[vtile], bsend.at[r], brecv, dev)

    @pl.when(z == owner)
    def _():
        @pl.loop(1, nz)
        def _(r):
            copy(VZ.at[r], VZ.at[r], vsend, vrecv.at[r], {"z": owner}).wait_recv()

        total = S[plane, part:, 0:vlanes].astype(F32)
        for r in range(1, nz):
            total = total + VZ[r].astype(F32)
        GATH[plane, part:, 0:vlanes] = total.astype(BF16)

        @pl.loop(1, nz)
        def _(r):
            vec_down(r).start()

    @pl.when(z != owner)
    def _():
        vec_down(1).wait_recv()

    @pl.loop(1, nz)
    def _(r):
        q = lax.rem(z - r + nz, nz)
        theirs = pl.ds(pl.multiple_of(q * zrows, zrows), zrows)
        copy(
            GATH.at[plane, theirs], GATH.at[plane, theirs], asend.at[r], arecv.at[r], {"z": q}
        ).wait_recv()

    def whole_copy(r):
        _, dev = plane_dev(r)
        return copy(GATH.at[plane], GATH.at[plane], gsend.at[r], grecv.at[r], dev)

    @pl.loop(1, nplane)
    def _(r):
        whole_copy(r).start()

    @pl.loop(1, nplane)
    def _(r):
        q = lax.rem(plane - r + nplane, nplane)
        copy(GATH.at[q], GATH.at[q], gsend.at[r], grecv.at[r], plane_dev(r)[1]).wait_recv()

    def squares(q, carry):
        a, b = carry
        v = GATH[q, 0:part, :].astype(F32)
        u = GATH[q, part:, 0:vlanes].astype(F32)
        return (
            a + jnp.sum((v * v).reshape(part // 8, 8, chans), axis=0),
            b + jnp.sum((u * u).reshape(VTILE // 8, 8, vlanes), axis=0),
        )

    a, b = lax.fori_loop(
        0, nplane, squares, (jnp.zeros((8, chans), F32), jnp.zeros((8, vlanes), F32))
    )
    seg = sx * 2 + core
    SQ[seg] = jnp.broadcast_to(jnp.sum(a) + jnp.sum(b), (8, 128))
    mates = [sib, far, diag]
    sq_copies = [
        copy(SQ.at[seg], SQ.at[seg], qsend.at[t], qrecv.at[t], dev) for t, dev in enumerate(mates)
    ]
    for c in sq_copies:
        c.start()
    ig_copy(0).wait_recv()
    ig_ref[...] = IG[...]
    gath_ref[...] = GATH[...]
    mate_seg = [sx * 2 + 1 - core, (1 - sx) * 2 + core, (1 - sx) * 2 + 1 - core]
    for t, dev in enumerate(mates):
        copy(
            SQ.at[mate_seg[t]], SQ.at[mate_seg[t]], qsend.at[t], qrecv.at[t], dev
        ).wait_recv()
    total = (SQ[0] + SQ[1]) + (SQ[2] + SQ[3])
    fac_ref[...] = jnp.minimum(1.0, (params**0.5) * lax.rsqrt(total + 1e-06))

    for c in wcopies:
        c.wait_send()
    hop_x().wait_send()
    ig_copy(0).wait_send()
    for c in grad_copies(0):
        c.wait_send()

    @pl.loop(1, nplane)
    def _(r):
        plane_copy(r).wait_send()
        whole_copy(r).wait_send()

    @pl.loop(1, nz)
    def _(r):
        z_copy(r).wait_send()
        share_copy(r).wait_send()

    @pl.when(z != owner)
    def _():
        vec_up().wait_send()

    @pl.when(z == owner)
    def _():
        @pl.loop(1, nz)
        def _(r):
            vec_down(r).wait_send()

    for c in sq_copies:
        c.wait_send()


def scale_kernel(gath, fac, ig, o_in, o_out, o_vec, o_ig):
    nplane, rows, chans = gath.shape
    part = rows - VTILE
    quarters = o_in.shape[1] // chans
    in_rows = chans // nplane
    out_rows = o_out.shape[0] // nplane
    vlanes = VPAD * chans // nplane // VTILE
    vcols = chans // vlanes
    f = fac[0:1, 0:1]
    for p in range(nplane):
        for q in range(quarters):
            o_in[p * in_rows : (p + 1) * in_rows, q * chans : (q + 1) * chans] = (
                gath[p, q * in_rows : (q + 1) * in_rows, :].astype(F32) * f
            )
        o_out[p * out_rows : (p + 1) * out_rows, :] = gath[p, quarters * in_rows : part, :].astype(F32) * f
        at_row, at_col = (p // vcols) * VTILE, (p % vcols) * vlanes
        size = min(VTILE, o_vec.shape[0] - at_row)
        o_vec[at_row : at_row + size, at_col : at_col + vlanes] = (
            gath[p, part:, 0:vlanes].astype(F32) * f
        )[0:size]
    o_ig[...] = ig[...]


def per_device(dims, inputs, out_grad, w_in, w_out, vector_params):
    nz, ny, nx, params = dims
    nplane = ny * nx
    micros, _, height, width, chans = inputs.shape
    hidden = w_in.shape[2]
    vrows = vector_params.shape[1]
    pair = micros // 2
    rows = pair * height * width
    part = (chans * hidden * 2) // chans // nplane
    zrows = part // nz
    vlanes = VPAD * chans // nplane // VTILE
    maps = (micros, height, width, chans)
    small = (pair, height, width, chans)
    vm = pltpu.VMEM
    dma = pltpu.SemaphoreType.DMA
    in_vmem = pl.BlockSpec(memory_space=pltpu.VMEM)
    anywhere = pl.BlockSpec(memory_space=pl.ANY)
    gath, fac, ig = pl.pallas_call(
        functools.partial(relay_kernel, dims),
        out_shape=(
            jax.ShapeDtypeStruct((nplane, part + VTILE, chans), BF16),
            jax.ShapeDtypeStruct((8, 128), F32),
            jax.ShapeDtypeStruct(maps, BF16),
        ),
        in_specs=[in_vmem, in_vmem, anywhere, anywhere, anywhere],
        out_specs=(in_vmem, in_vmem, in_vmem),
        scratch_shapes=[
            vm((2, chans, hidden), BF16),
            vm((2, hidden, chans), BF16),
            vm((2, vrows, chans), F32),
            vm((3,) + small, BF16),
            vm((3,) + small, BF16),
            vm((pair, height, width + 16, chans), F32),
            vm(small, F32),
            vm((2, rows, chans), F32),
            vm((2, rows, 128), F32),
            vm((2, rows, chans), BF16),
            vm((2, rows, hidden), BF16),
            vm((2, rows, hidden), F32),
            vm((2, rows, chans), F32),
            vm((2, chans, hidden), BF16),
            vm((2, hidden, chans), BF16),
            vm((2, VPAD, chans), F32),
            vm((chans, hidden), BF16),
            vm((hidden, chans), BF16),
            vm((VPAD, chans), F32),
            vm(maps, BF16),
            vm((nplane, part + VTILE, chans), BF16),
            vm((nplane, part + VTILE, chans), BF16),
            vm((nz, zrows, chans), BF16),
            vm((nz, VTILE, vlanes), BF16),
            vm((nplane, part + VTILE, chans), BF16),
            vm((4, 8, 128), F32),
            dma((3,)),
            dma((3,)), dma((3,)),
            dma, dma,
            dma, dma,
            dma((3,)), dma((3,)),
            dma((nplane,)), dma((nplane,)),
            dma((nz,)), dma((nz,)),
            dma, dma((nz,)),
            dma((nz,)), dma,
            dma((nz,)), dma((nz,)),
            dma((nplane,)), dma((nplane,)),
            dma((3,)), dma((3,)),
        ],
        compiler_params=pltpu.CompilerParams(
            collective_id=0, has_side_effects=True, vmem_limit_bytes=40 * 1024 * 1024
        ),
        name="relay",
    )(
        inputs.reshape(maps), out_grad.reshape(maps), w_in[0], w_out[0], vector_params[0]
    )
    o_in, o_out, o_vec, o_ig = pl.pallas_call(
        scale_kernel,
        out_shape=(
            jax.ShapeDtypeStruct((chans, hidden), F32),
            jax.ShapeDtypeStruct((hidden, chans), F32),
            jax.ShapeDtypeStruct((vrows, chans), F32),
            jax.ShapeDtypeStruct(maps, BF16),
        ),
        in_specs=[in_vmem] * 3,
        out_specs=(in_vmem,) * 4,
        compiler_params=pltpu.CompilerParams(vmem_limit_bytes=24 * 1024 * 1024),
        name="scale",
    )(gath, fac, ig)
    return (
        o_ig.reshape((1, micros, 1, height, width, chans)), o_in[None], o_out[None], o_vec[None]
    )


def solution(mesh):
    nx = 2
    ny = 4
    nz = mesh.shape["dp"] // (nx * ny)
    return program_on(mesh, nz, ny, nx)


def program_on(mesh, nz, ny, nx, params=2156544):
    split = Mesh(mesh.devices.reshape(2, 2, nz, ny, nx), ("sx", "core", "z", "y", "xl"))
    dp = ("z", "y", "xl")
    seg = ("sx", "core")
    in_specs = (
        P(None, dp, None, None, None),
        P(None, dp, None, None, None),
        P(seg, None, None),
        P(seg, None, None),
        P(seg, None, None),
    )
    out_specs = (
        P(seg, None, dp, None, None, None),
        P(seg, None, None),
        P(seg, None, None),
        P(seg, None, None),
    )
    return jax.shard_map(
        functools.partial(per_device, (nz, ny, nx, params)),
        mesh=split, in_specs=in_specs, out_specs=out_specs, check_vma=False,
    )
```

```python
import functools

import jax
import jax.numpy as jnp
from jax import lax
from jax.experimental import pallas as pl
from jax.experimental.pallas import tpu as pltpu
from jax.sharding import Mesh
from jax.sharding import PartitionSpec as P

F32 = jnp.float32
BF16 = jnp.bfloat16
VTILE = 16
VPAD = 64


def dot(a, b):
    return jnp.dot(a, b, preferred_element_type=F32)


def dot_nt(a, b):
    return lax.dot_general(a, b, (((1,), (1,)), ((), ())), preferred_element_type=F32)


def dot_tn(a, b):
    return lax.dot_general(a, b, (((0,), (0,)), ((), ())), preferred_element_type=F32)


def over_rows(a):
    return jnp.sum(a, axis=0, keepdims=True)


def spans(nz):
    if nz == 16:
        return ((11, 16), (6, 11), (0, 6)), ((0, 1), (1, 5), (5, 9), (9, 13), (13, 16))
    return ((1, nz), (0, 1)), ((0, 1), (1, nz))


def offset(s):
    return (s + 1) // 2 if s % 2 else -(s // 2)


def mirror(s, nz):
    if s == 0 or s == nz - 1:
        return s
    return s + 1 if s % 2 else s - 1


def relay_kernel(
    dims, x_ref, g_ref, win_ref, wout_ref, vec_ref, gath_ref, gathv_ref, fac_ref, ig_ref,
    win, wout, vec, X, G, xpad, cv, XH, RSTD, NB, ACT, SL, PJ,
    PG, GV, RG, RV, IG, S, RB, SV, RBV, ZB, VZ, GATH, GATHV, SQS, SQZ, SQP,
    load_sem, wsend, wrecv, hsend, hrecv, isend, irecv, csend, crecv, cvsend, cvrecv,
    psend, precv, pvsend, pvrecv, zsend, zrecv, vsend, vrecv, bsend, brecv, asend, arecv,
    gsend, grecv, gvsend, gvrecv, qsend, qrecv, qzsend, qzrecv, qpsend, qprecv,
):
    nz, ny, nx, params = dims
    nplane = ny * nx
    core = lax.axis_index("core")
    sx = lax.axis_index("sx")
    z = lax.axis_index("z")
    y = lax.axis_index("y")
    xl = lax.axis_index("xl")
    plane = y * nx + xl
    pair, height, width, chans = X.shape[1:]
    rows = pair * height * width
    hidden = win.shape[2]
    quarters = hidden // chans
    part = 2 * hidden // nplane
    zrows = part // nz
    vlanes = SV.shape[2]
    vcols = chans // vlanes
    owner = lax.rem(2 * plane + core, nz)
    chunks, groups = spans(nz)

    def copy(src, dst, ss, rs, dev):
        return pltpu.make_async_remote_copy(
            src_ref=src, dst_ref=dst, send_sem=ss, recv_sem=rs,
            device_id=dev, device_id_type=pl.DeviceIdType.MESH,
        )

    sib = {"core": 1 - core}
    far = {"sx": 1 - sx}
    diag = {"core": 1 - core, "sx": 1 - sx}

    def plane_dev(r):
        q = lax.rem(plane + r, nplane)
        return q, {"y": q // nx, "xl": lax.rem(q, nx)}

    def z_at(by):
        return lax.rem(z + by + nz, nz)

    loads = [
        pltpu.make_async_copy(vec_ref, vec.at[core], load_sem.at[0]),
        pltpu.make_async_copy(win_ref, win.at[core], load_sem.at[1]),
        pltpu.make_async_copy(wout_ref, wout.at[core], load_sem.at[2]),
    ]
    for c in loads:
        c.start()
    my_micros = pl.ds(core * pair, pair)

    def load_x():
        return pltpu.make_async_copy(x_ref.at[my_micros], X.at[0], load_sem.at[3])

    def load_g():
        return pltpu.make_async_copy(g_ref.at[my_micros], G.at[2], load_sem.at[3])

    @pl.when(sx == 0)
    def _():
        load_x().start()

    @pl.when(sx == 1)
    def _():
        load_g().start()

    barrier = pltpu.get_barrier_semaphore()

    def hello(dev):
        pl.semaphore_signal(barrier, inc=1, device_id=dev, device_id_type=pl.DeviceIdType.MESH)

    @pl.loop(1, nz)
    def _(r):
        hello({"z": z_at(r)})

    @pl.loop(1, nplane)
    def _(r):
        hello(plane_dev(r)[1])

    hello(diag)
    hello(far)
    hello(sib)

    zero_side = jnp.zeros((pair, height, 8, chans), F32)
    xpad[:, :, 0:8, :] = zero_side
    xpad[:, :, 8 + width : 16 + width, :] = zero_side
    GV[...] = jnp.zeros(GV.shape, F32)

    @pl.when(sx == 0)
    def _():
        load_x().wait()

    @pl.when(sx == 1)
    def _():
        load_g().wait()

    pl.semaphore_wait(barrier, 3 + (nplane - 1) + (nz - 1))

    wcopies = [
        copy(vec_ref, vec.at[core], wsend.at[0], wrecv.at[0], sib),
        copy(win_ref, win.at[core], wsend.at[1], wrecv.at[1], sib),
        copy(wout_ref, wout.at[core], wsend.at[2], wrecv.at[2], sib),
    ]
    for c in wcopies:
        c.start()

    def hop_x():
        return copy(X.at[2], X.at[0], hsend, hrecv, far)

    def hop_g():
        return copy(G.at[0], G.at[2], hsend, hrecv, far)

    @pl.when(sx == 1)
    def _():
        hop_x().wait_recv()

    def row(k, t):
        return vec[k, t]

    def forward(k, carry):
        @pl.when(core == k)
        def _():
            for c in loads:
                c.wait()

        @pl.when(core != k)
        def _():
            for c in wcopies:
                c.wait_recv()

        xpad[:, :, 8 : 8 + width, :] = X[k].astype(F32)
        for half in range(chans // 128):
            lanes = slice(half * 128, half * 128 + 128)
            acc = [None] * height
            for j in range(7):
                shifted = [xpad[:, h, 5 + j : 5 + j + width, lanes] for h in range(height)]
                for i in range(7):
                    tap = vec[k, 7 * i + j, :, lanes][None]
                    for h in range(height):
                        if 0 <= h + i - 3 < height:
                            term = shifted[h + i - 3] * tap
                            acc[h] = term if acc[h] is None else acc[h] + term
            bias = vec[k, 49, :, lanes][None]
            for h in range(height):
                cv[:, h, :, lanes] = acc[h] + bias
        conv = cv[...].reshape(rows, chans)
        mean = jnp.sum(conv, axis=1, keepdims=True) * (1.0 / chans)
        centered = conv - mean
        var = jnp.sum(centered * centered, axis=1, keepdims=True) * (1.0 / chans)
        rstd = lax.rsqrt(var + 1e-06)
        xhat = centered * rstd
        XH[k] = xhat
        RSTD[k] = jnp.broadcast_to(rstd, (rows, 128))
        normed = (xhat * row(k, 50) + row(k, 51)).astype(BF16)
        NB[k] = normed
        proj = jnp.zeros((rows, chans), F32)
        for q in range(quarters):
            cols = slice(q * chans, (q + 1) * chans)
            pre = dot(normed, win[k, :, cols]) + row(k, 54 + q)
            cumulative = 0.5 * (1.0 + lax.erf(pre * 0.7071067811865476))
            act = (pre * cumulative).astype(BF16)
            ACT[k, :, cols] = act
            SL[k, :, cols] = cumulative + pre * jnp.exp(-0.5 * pre * pre) * 0.3989422804014327
            proj = proj + dot(act, wout[k, cols, :])
        proj = proj + row(k, 52)
        PJ[k] = proj
        out = X[k].astype(F32).reshape(rows, chans) + row(k, 53) * proj
        X[k + 1] = out.astype(BF16).reshape(pair, height, width, chans)
        return carry

    lax.fori_loop(0, 2, forward, 0)

    @pl.when(sx == 0)
    def _():
        hop_x().start()
        hop_g().wait_recv()

    def grad_copy(k, t):
        at = pl.ds(t * chans, chans)
        return copy(PG.at[k, at], RG.at[at], csend.at[t], crecv.at[t], sib)

    def vec_copy(k):
        return copy(GV.at[k], RV, cvsend, cvrecv, sib)

    def ig_copy(k):
        return copy(G.at[k], IG.at[my_micros], isend, irecv, sib)

    def plane_copy(c, r):
        lo, hi = chunks[c]
        q, dev = plane_dev(r)
        at = pl.ds(lo * zrows, (hi - lo) * zrows)
        return copy(S.at[q, at], RB.at[r, at], psend.at[c, r], precv.at[c, r], dev)

    def plane_vec_copy(r):
        q, dev = plane_dev(r)
        return copy(SV.at[q], RBV.at[r], pvsend.at[r], pvrecv.at[r], dev)

    def chip_sum(k):
        for t in range(2 * quarters):
            grad_copy(k, t).wait_recv()
        for c, (lo, hi) in enumerate(chunks):

            @pl.loop(1, nplane + 1)
            def _(r):
                p = lax.rem(plane + r, nplane)
                for s in range(lo, hi):
                    start = p * part + z_at(offset(s)) * zrows
                    at = pl.ds(pl.multiple_of(start, zrows), zrows)
                    S[p, s * zrows : (s + 1) * zrows, :] = (
                        PG[k, at, :].astype(F32) + RG[at, :].astype(F32)
                    ).astype(BF16)

                @pl.when(r < nplane)
                def _():
                    plane_copy(c, r).start()

    def chip_vec_sum(k):
        vec_copy(k).wait_recv()
        for t in range(nplane):
            at_row, at_col = (t // vcols) * VTILE, (t % vcols) * vlanes
            tile = (slice(at_row, at_row + VTILE), slice(at_col, at_col + vlanes))
            SV[t] = (GV[(k,) + tile] + RV[tile]).astype(BF16)

        @pl.loop(1, nplane)
        def _(r):
            plane_vec_copy(r).start()

    def backward(step, carry):
        k = 1 - step
        gf = G[k + 1].astype(F32).reshape(rows, chans)
        GV[k, 53:54, :] = over_rows(gf * PJ[k])
        dproj = gf * row(k, 53)
        GV[k, 52:53, :] = over_rows(dproj)
        dproj_b = dproj.astype(BF16)
        normed = NB[k]
        dn = jnp.zeros((rows, chans), F32)
        for q in range(quarters):
            cols = slice(q * chans, (q + 1) * chans)
            dact = dot_nt(dproj_b, wout[k, cols, :])
            PG[k, hidden + q * chans : hidden + (q + 1) * chans, :] = dot_tn(
                ACT[k, :, cols], dproj_b
            ).astype(BF16)
            dpre = dact * SL[k, :, cols]
            GV[k, 54 + q : 55 + q, :] = over_rows(dpre)
            dpre_b = dpre.astype(BF16)
            PG[k, cols, :] = dot_tn(normed, dpre_b).astype(BF16)

            @pl.when(core != k)
            def _():
                grad_copy(k, quarters + q).start()
                grad_copy(k, q).start()

            dn = dn + dot_nt(dpre_b, win[k, :, cols])

        @pl.when((core == 1) & (k == 0))
        def _():
            chip_sum(1)
            chip_vec_sum(1)

        xhat = XH[k]
        GV[k, 50:51, :] = over_rows(dn * xhat)
        GV[k, 51:52, :] = over_rows(dn)
        dxh = dn * row(k, 50)
        m1 = jnp.sum(dxh, axis=1, keepdims=True) * (1.0 / chans)
        m2 = jnp.sum(dxh * xhat, axis=1, keepdims=True) * (1.0 / chans)
        rstd = RSTD[k][:, 0:1]
        dconv = (dxh - m1 - xhat * m2) * rstd
        GV[k, 49:50, :] = over_rows(dconv)
        xpad[:, :, 8 : 8 + width, :] = dconv.reshape(pair, height, width, chans)
        for half in range(chans // 128):
            lanes = slice(half * 128, half * 128 + 128)
            acc = [G[k + 1, :, h, :, lanes].astype(F32) for h in range(height)]
            xs = [X[k, :, h, :, lanes].astype(F32) for h in range(height)]
            for j in range(7):
                shifted = [xpad[:, h, 11 - j : 11 - j + width, lanes] for h in range(height)]
                for i in range(7):
                    t = 7 * i + j
                    tap = vec[k, t, :, lanes][None]
                    total = None
                    for h in range(height):
                        if 0 <= h - i + 3 < height:
                            acc[h] = acc[h] + shifted[h - i + 3] * tap
                            term = xs[h] * shifted[h - i + 3]
                            total = term if total is None else total + term
                    GV[k, t : t + 1, lanes] = over_rows(total.reshape(pair * width, 128))
            for h in range(height):
                G[k, :, h, :, lanes] = acc[h].astype(BF16)

        @pl.when(core != k)
        def _():
            vec_copy(k).start()
            ig_copy(k).start()

        @pl.when(core == k)
        def _():
            IG[my_micros] = G[k]

        return carry

    lax.fori_loop(0, 2, backward, 0)

    @pl.when(sx == 1)
    def _():
        hop_g().start()

    @pl.when(core == 0)
    def _():
        chip_sum(0)
        chip_vec_sum(0)

    def z_copy(s):
        src = S.at[plane, pl.ds(s * zrows, zrows)]
        return copy(src, ZB.at[s], zsend.at[s], zrecv.at[s], {"z": z_at(offset(s))})

    for c, (lo, hi) in enumerate(chunks):

        @pl.loop(1, nplane)
        def _(r):
            plane_copy(c, r).wait_recv()

        for s in reversed(range(lo, hi)):
            at = slice(s * zrows, (s + 1) * zrows)
            acc = S[plane, at, :].astype(F32)
            for t in range(1, nplane):
                acc = acc + RB[t, at, :].astype(F32)
            if s > 0:
                S[plane, at, :] = acc.astype(BF16)
                z_copy(s).start()
            else:
                ZB[0] = acc.astype(BF16)

    def vec_up():
        r = lax.rem(owner - z + nz, nz)
        return copy(RBV.at[0], VZ.at[r], vsend, vrecv.at[r], {"z": owner})

    @pl.loop(1, nplane)
    def _(r):
        plane_vec_copy(r).wait_recv()

    vacc = SV[plane].astype(F32)
    for r in range(1, nplane):
        vacc = vacc + RBV[r].astype(F32)
    RBV[0] = vacc.astype(BF16)

    @pl.when(z != owner)
    def _():
        vec_up().start()

    def share_copy(s):
        return copy(
            GATH.at[plane, pl.ds(0, zrows)],
            GATH.at[plane, pl.ds(mirror(s, nz) * zrows, zrows)],
            asend.at[s], arecv.at[mirror(s, nz)], {"z": z_at(offset(s))},
        )

    def group_copy(g, r):
        lo, hi = groups[g]
        at = pl.ds(lo * zrows, (hi - lo) * zrows)
        return copy(
            GATH.at[plane, at], GATH.at[plane, at], gsend.at[g, r], grecv.at[g, r],
            plane_dev(r)[1],
        )

    for s in range(1, nz):
        z_copy(s).wait_recv()
    share = ZB[0].astype(F32)
    for s in range(1, nz):
        share = share + ZB[s].astype(F32)
    GATH[plane, 0:zrows, :] = share.astype(BF16)
    for s in reversed(range(1, nz)):
        share_copy(s).start()

    @pl.loop(1, nplane)
    def _(r):
        group_copy(0, r).start()

    SQS[2 * sx + core] = jnp.broadcast_to(jnp.sum(share * share), (1, 128))

    def vec_down(r):
        return copy(
            GATHV.at[plane], GATHV.at[plane], bsend.at[r], brecv, {"z": z_at(r)}
        )

    @pl.when(z == owner)
    def _():
        @pl.loop(1, nz)
        def _(r):
            copy(VZ.at[r], VZ.at[r], vsend, vrecv.at[r], {"z": owner}).wait_recv()

        total = RBV[0].astype(F32)
        for r in range(1, nz):
            total = total + VZ[r].astype(F32)
        GATHV[plane] = total.astype(BF16)

        @pl.loop(1, nz)
        def _(r):
            vec_down(r).start()

        SQS[2 * sx + core] = SQS[2 * sx + core] + jnp.broadcast_to(
            jnp.sum(total * total), (1, 128)
        )

    def sq_block(t):
        at = SQS.at[2 * sx + core]
        return copy(at, at, qsend.at[t], qrecv.at[t], (sib, far, diag)[t])

    def sq_z(r):
        at = SQZ.at[z]
        return copy(at, at, qzsend.at[r], qzrecv.at[r], {"z": z_at(r)})

    def sq_plane(r):
        at = SQP.at[plane]
        return copy(at, at, qpsend.at[r], qprecv.at[r], plane_dev(r)[1])

    for t in range(3):
        sq_block(t).start()

    def forward_group(g):
        lo, hi = groups[g]
        for s in range(lo, hi):
            at = GATH.at[plane, pl.ds(s * zrows, zrows)]
            copy(at, at, asend.at[s], arecv.at[s], sib).wait_recv()

        @pl.loop(1, nplane)
        def _(r):
            group_copy(g, r).start()

    forward_group(1)
    mates = (2 * sx + 1 - core, 2 * (1 - sx) + core, 2 * (1 - sx) + 1 - core)
    for t in range(3):
        at = SQS.at[mates[t]]
        copy(at, at, qsend.at[t], qrecv.at[t], sib).wait_recv()
    SQZ[z] = (SQS[0] + SQS[1]) + (SQS[2] + SQS[3])

    @pl.loop(1, nz)
    def _(r):
        sq_z(r).start()

    for g in range(2, len(groups)):
        forward_group(g)

    def vec_out(r):
        at = GATHV.at[plane]
        return copy(at, at, gvsend.at[r], gvrecv.at[r], plane_dev(r)[1])

    @pl.when(z != owner)
    def _():
        vec_down(1).wait_recv()

    @pl.loop(1, nplane)
    def _(r):
        vec_out(r).start()

    @pl.loop(1, nz)
    def _(r):
        at = SQZ.at[z_at(-r)]
        copy(at, at, qzsend.at[r], qzrecv.at[r], sib).wait_recv()

    total = SQZ[0]
    for t in range(1, nz):
        total = total + SQZ[t]
    SQP[plane] = total

    @pl.loop(1, nplane)
    def _(r):
        sq_plane(r).start()

    ig_copy(0).wait_recv()
    ig_ref[...] = IG[...]

    for c in wcopies:
        c.wait_send()
    hop_x().wait_send()
    ig_copy(0).wait_send()
    for t in range(2 * quarters):
        grad_copy(0, t).wait_send()
    vec_copy(0).wait_send()

    @pl.loop(1, nplane)
    def _(r):
        for c in range(len(chunks)):
            plane_copy(c, r).wait_send()
        plane_vec_copy(r).wait_send()

    for s in range(1, nz):
        z_copy(s).wait_send()
        share_copy(s).wait_send()

    @pl.when(z != owner)
    def _():
        vec_up().wait_send()

    @pl.when(z == owner)
    def _():
        @pl.loop(1, nz)
        def _(r):
            vec_down(r).wait_send()

    for t in range(3):
        sq_block(t).wait_send()

    @pl.loop(1, nz)
    def _(r):
        sq_z(r).wait_send()

    @pl.loop(1, nplane)
    def _(r):
        q = lax.rem(plane - r + nplane, nplane)
        for g, (lo, hi) in enumerate(groups):
            at = GATH.at[q, pl.ds(lo * zrows, (hi - lo) * zrows)]
            copy(at, at, gsend.at[g, r], grecv.at[g, r], sib).wait_recv()
        copy(GATHV.at[q], GATHV.at[q], gvsend.at[r], gvrecv.at[r], sib).wait_recv()
        copy(SQP.at[q], SQP.at[q], qpsend.at[r], qprecv.at[r], sib).wait_recv()

    gath_ref[...] = GATH[...]
    gathv_ref[...] = GATHV[...]
    total = SQP[0]
    for t in range(1, nplane):
        total = total + SQP[t]
    factor = jnp.minimum(1.0, (params**0.5) * lax.rsqrt(total + 1e-06))
    fac_ref[...] = jnp.broadcast_to(factor, fac_ref.shape)

    @pl.loop(1, nplane)
    def _(r):
        for g in range(len(groups)):
            group_copy(g, r).wait_send()
        vec_out(r).wait_send()
        sq_plane(r).wait_send()


def scale_kernel(nz, gath, gathv, fac, ig, o_in, o_out, o_vec, o_ig):
    nplane, part, chans = gath.shape
    hidden = o_in.shape[1]
    quarters = hidden // chans
    zrows = part // nz
    vlanes = gathv.shape[2]
    vcols = chans // vlanes
    z = lax.axis_index("z")
    f = fac[0:1, 0:1]
    per = chans // zrows
    for s in range(nz):
        q = lax.rem(z + offset(s) + nz, nz)
        for p in range(nplane):
            piece = gath[p, s * zrows : (s + 1) * zrows, :].astype(F32) * f
            first = p * part
            if first < hidden:
                if part <= chans:
                    at = pl.ds(pl.multiple_of(first % chans + q * zrows, zrows), zrows)
                    o_in[at, first // chans * chans : first // chans * chans + chans] = piece
                else:
                    for t in range(part // chans):
                        @pl.when(q // per == t)
                        def _():
                            at = pl.ds(pl.multiple_of(lax.rem(q, per) * zrows, zrows), zrows)
                            o_in[at, first + t * chans : first + t * chans + chans] = piece
            else:
                at = pl.ds(pl.multiple_of(first - hidden + q * zrows, zrows), zrows)
                o_out[at, :] = piece
    for p in range(nplane):
        at_row, at_col = (p // vcols) * VTILE, (p % vcols) * vlanes
        tile = gathv[p].astype(F32) * f
        for t in range(min(VTILE, o_vec.shape[0] - at_row)):
            o_vec[at_row + t, :, at_col : at_col + vlanes] = tile[t : t + 1, :]
    o_ig[...] = ig[...]


def per_device(dims, inputs, out_grad, w_in, w_out, vector_params):
    nz, ny, nx, params = dims
    nplane = ny * nx
    micros, _, height, width, chans = inputs.shape
    hidden = w_in.shape[2]
    vrows = vector_params.shape[1]
    pair = micros // 2
    rows = pair * height * width
    part = 2 * hidden // nplane
    zrows = part // nz
    vlanes = VPAD * chans // nplane // VTILE
    chunks, groups = spans(nz)
    maps = (micros, height, width, chans)
    small = (pair, height, width, chans)
    vm = pltpu.VMEM
    dma = pltpu.SemaphoreType.DMA
    in_vmem = pl.BlockSpec(memory_space=pltpu.VMEM)
    in_hbm = pl.BlockSpec(memory_space=pltpu.HBM)
    gath, gathv, fac, ig = pl.pallas_call(
        functools.partial(relay_kernel, dims),
        out_shape=(
            jax.ShapeDtypeStruct((nplane, part, chans), BF16),
            jax.ShapeDtypeStruct((nplane, VTILE, vlanes), BF16),
            jax.ShapeDtypeStruct((8, 128), F32),
            jax.ShapeDtypeStruct(maps, BF16),
        ),
        in_specs=[in_hbm] * 5,
        out_specs=(in_vmem,) * 4,
        scratch_shapes=[
            vm((2, chans, hidden), BF16),
            vm((2, hidden, chans), BF16),
            vm((2, vrows, 1, chans), F32),
            vm((3,) + small, BF16),
            vm((3,) + small, BF16),
            vm((pair, height, width + 16, chans), F32),
            vm(small, F32),
            vm((2, rows, chans), F32),
            vm((2, rows, 128), F32),
            vm((2, rows, chans), BF16),
            vm((2, rows, hidden), BF16),
            vm((2, rows, hidden), F32),
            vm((2, rows, chans), F32),
            vm((2, 2 * hidden, chans), BF16),
            vm((2, VPAD, chans), F32),
            vm((2 * hidden, chans), BF16),
            vm((VPAD, chans), F32),
            vm(maps, BF16),
            vm((nplane, part, chans), BF16),
            vm((nplane, part, chans), BF16),
            vm((nplane, VTILE, vlanes), BF16),
            vm((nplane, VTILE, vlanes), BF16),
            vm((nz, zrows, chans), BF16),
            vm((nz, VTILE, vlanes), BF16),
            vm((nplane, part, chans), BF16),
            vm((nplane, VTILE, vlanes), BF16),
            vm((4, 1, 128), F32),
            vm((nz, 1, 128), F32),
            vm((nplane, 1, 128), F32),
            dma((4,)),
            dma((3,)), dma((3,)),
            dma, dma,
            dma, dma,
            dma((2 * hidden // chans,)), dma((2 * hidden // chans,)),
            dma, dma,
            dma((len(chunks), nplane)), dma((len(chunks), nplane)),
            dma((nplane,)), dma((nplane,)),
            dma((nz,)), dma((nz,)),
            dma, dma((nz,)),
            dma((nz,)), dma,
            dma((nz,)), dma((nz,)),
            dma((len(groups), nplane)), dma((len(groups), nplane)),
            dma((nplane,)), dma((nplane,)),
            dma((3,)), dma((3,)),
            dma((nz,)), dma((nz,)),
            dma((nplane,)), dma((nplane,)),
        ],
        compiler_params=pltpu.CompilerParams(
            collective_id=0, has_side_effects=True, vmem_limit_bytes=60 * 1024 * 1024
        ),
        name="relay",
    )(
        inputs.reshape(maps), out_grad.reshape(maps), w_in[0], w_out[0],
        jnp.swapaxes(vector_params, 0, 1),
    )
    o_in, o_out, o_vec, o_ig = pl.pallas_call(
        functools.partial(scale_kernel, nz),
        out_shape=(
            jax.ShapeDtypeStruct((chans, hidden), F32),
            jax.ShapeDtypeStruct((hidden, chans), F32),
            jax.ShapeDtypeStruct((vrows, 1, chans), F32),
            jax.ShapeDtypeStruct(maps, BF16),
        ),
        in_specs=[in_vmem] * 4,
        out_specs=(in_vmem,) * 4,
        compiler_params=pltpu.CompilerParams(vmem_limit_bytes=60 * 1024 * 1024),
        name="scale",
    )(gath, gathv, fac, ig)
    return (
        o_ig.reshape((1, micros, 1, height, width, chans)),
        o_in[None],
        o_out[None],
        jnp.swapaxes(o_vec, 0, 1),
    )


def solution(mesh):
    nx = 2
    ny = 4
    nz = mesh.shape["dp"] // (nx * ny)
    return program_on(mesh, nz, ny, nx)


def program_on(mesh, nz, ny, nx, params=2156544):
    split = Mesh(mesh.devices.reshape(2, 2, nz, ny, nx), ("sx", "core", "z", "y", "xl"))
    dp = ("z", "y", "xl")
    seg = ("sx", "core")
    in_specs = (
        P(None, dp, None, None, None),
        P(None, dp, None, None, None),
        P(seg, None, None),
        P(seg, None, None),
        P(seg, None, None),
    )
    out_specs = (
        P(seg, None, dp, None, None, None),
        P(seg, None, None),
        P(seg, None, None),
        P(seg, None, None),
    )
    return jax.shard_map(
        functools.partial(per_device, (nz, ny, nx, params)),
        mesh=split, in_specs=in_specs, out_specs=out_specs, check_vma=False,
    )
```

```python
import functools

import jax
import jax.numpy as jnp
from jax import lax
from jax.experimental import pallas as pl
from jax.experimental.pallas import tpu as pltpu
from jax.sharding import Mesh
from jax.sharding import PartitionSpec as P

F32 = jnp.float32
BF16 = jnp.bfloat16
VTILE = 16
VPAD = 64


def dot(a, b):
    return jnp.dot(a, b, preferred_element_type=F32)


def dot_nt(a, b):
    return lax.dot_general(a, b, (((1,), (1,)), ((), ())), preferred_element_type=F32)


def dot_tn(a, b):
    return lax.dot_general(a, b, (((0,), (0,)), ((), ())), preferred_element_type=F32)


def over_rows(a):
    return jnp.sum(a, axis=0, keepdims=True)


def spans(nz):
    if nz == 16:
        return ((11, 16), (6, 11), (0, 6)), ((0, 1), (1, 5), (5, 9), (9, 13), (13, 16))
    return ((1, nz), (0, 1)), ((0, 1), (1, nz))


def offset(s):
    return (s + 1) // 2 if s % 2 else -(s // 2)


def mirror(s, nz):
    if s == 0 or s == nz - 1:
        return s
    return s + 1 if s % 2 else s - 1


def relay_kernel(
    dims, x_ref, g_ref, win_ref, wout_ref, vec_ref, gath_ref, gathv_ref, fac_ref, ig_ref,
    win, wout, vec, X, G, xpad, cv, XH, RSTD, NB, ACT, SL, PJ,
    PG, GV, RG, RV, IG, S, RB, SV, RBV, ZB, VZ, GATH, GATHV, SQS, SQZ, SQP,
    load_sem, wsend, wrecv, hsend, hrecv, isend, irecv, csend, crecv, cvsend, cvrecv,
    psend, precv, pvsend, pvrecv, zsend, zrecv, vsend, vrecv, bsend, brecv, asend, arecv,
    gsend, grecv, gvsend, gvrecv, qsend, qrecv, qzsend, qzrecv, qpsend, qprecv, store_sem,
):
    nz, ny, nx, params = dims
    nplane = ny * nx
    core = lax.axis_index("core")
    sx = lax.axis_index("sx")
    z = lax.axis_index("z")
    y = lax.axis_index("y")
    xl = lax.axis_index("xl")
    plane = y * nx + xl
    pair, height, width, chans = X.shape[1:]
    rows = pair * height * width
    hidden = win.shape[2]
    quarters = hidden // chans
    part = 2 * hidden // nplane
    zrows = part // nz
    vlanes = SV.shape[2]
    vcols = chans // vlanes
    owner = lax.rem(2 * plane + core, nz)
    chunks, groups = spans(nz)

    def copy(src, dst, ss, rs, dev):
        return pltpu.make_async_remote_copy(
            src_ref=src, dst_ref=dst, send_sem=ss, recv_sem=rs,
            device_id=dev, device_id_type=pl.DeviceIdType.MESH,
        )

    sib = {"core": 1 - core}
    far = {"sx": 1 - sx}
    diag = {"core": 1 - core, "sx": 1 - sx}

    def plane_dev(r):
        q = lax.rem(plane + r, nplane)
        return q, {"y": q // nx, "xl": lax.rem(q, nx)}

    def z_at(by):
        return lax.rem(z + by + nz, nz)

    loads = [
        pltpu.make_async_copy(vec_ref, vec.at[core], load_sem.at[0]),
        pltpu.make_async_copy(win_ref, win.at[core], load_sem.at[1]),
        pltpu.make_async_copy(wout_ref, wout.at[core], load_sem.at[2]),
    ]
    for c in loads:
        c.start()
    my_micros = pl.ds(core * pair, pair)

    def load_x():
        return pltpu.make_async_copy(x_ref.at[my_micros], X.at[0], load_sem.at[3])

    def load_g():
        return pltpu.make_async_copy(g_ref.at[my_micros], G.at[2], load_sem.at[3])

    @pl.when(sx == 0)
    def _():
        load_x().start()

    @pl.when(sx == 1)
    def _():
        load_g().start()

    barrier = pltpu.get_barrier_semaphore()

    def hello(dev):
        pl.semaphore_signal(barrier, inc=1, device_id=dev, device_id_type=pl.DeviceIdType.MESH)

    @pl.loop(1, nz)
    def _(r):
        hello({"z": z_at(r)})

    @pl.loop(1, nplane)
    def _(r):
        hello(plane_dev(r)[1])

    hello(diag)
    hello(far)
    hello(sib)

    zero_side = jnp.zeros((pair, height, 8, chans), F32)
    xpad[:, :, 0:8, :] = zero_side
    xpad[:, :, 8 + width : 16 + width, :] = zero_side
    GV[...] = jnp.zeros(GV.shape, F32)

    @pl.when(sx == 0)
    def _():
        load_x().wait()

    @pl.when(sx == 1)
    def _():
        load_g().wait()

    pl.semaphore_wait(barrier, 3 + (nplane - 1) + (nz - 1))

    wcopies = [
        copy(vec_ref, vec.at[core], wsend.at[0], wrecv.at[0], sib),
        copy(win_ref, win.at[core], wsend.at[1], wrecv.at[1], sib),
        copy(wout_ref, wout.at[core], wsend.at[2], wrecv.at[2], sib),
    ]
    for c in wcopies:
        c.start()

    def hop_x():
        return copy(X.at[2], X.at[0], hsend, hrecv, far)

    def hop_g():
        return copy(G.at[0], G.at[2], hsend, hrecv, far)

    @pl.when(sx == 1)
    def _():
        hop_x().wait_recv()

    def row(k, t):
        return vec[k, t]

    def forward(k, carry):
        @pl.when(core == k)
        def _():
            for c in loads:
                c.wait()

        @pl.when(core != k)
        def _():
            for c in wcopies:
                c.wait_recv()

        xpad[:, :, 8 : 8 + width, :] = X[k].astype(F32)
        for half in range(chans // 128):
            lanes = slice(half * 128, half * 128 + 128)
            acc = [None] * height
            for j in range(7):
                shifted = [xpad[:, h, 5 + j : 5 + j + width, lanes] for h in range(height)]
                for i in range(7):
                    tap = vec[k, 7 * i + j, :, lanes][None]
                    for h in range(height):
                        if 0 <= h + i - 3 < height:
                            term = shifted[h + i - 3] * tap
                            acc[h] = term if acc[h] is None else acc[h] + term
            bias = vec[k, 49, :, lanes][None]
            for h in range(height):
                cv[:, h, :, lanes] = acc[h] + bias
        conv = cv[...].reshape(rows, chans)
        mean = jnp.sum(conv, axis=1, keepdims=True) * (1.0 / chans)
        centered = conv - mean
        var = jnp.sum(centered * centered, axis=1, keepdims=True) * (1.0 / chans)
        rstd = lax.rsqrt(var + 1e-06)
        xhat = centered * rstd
        XH[k] = xhat
        RSTD[k] = jnp.broadcast_to(rstd, (rows, 128))
        normed = (xhat * row(k, 50) + row(k, 51)).astype(BF16)
        NB[k] = normed
        proj = jnp.zeros((rows, chans), F32)
        for q in range(quarters):
            cols = slice(q * chans, (q + 1) * chans)
            pre = dot(normed, win[k, :, cols]) + row(k, 54 + q)
            cumulative = 0.5 * (1.0 + lax.erf(pre * 0.7071067811865476))
            act = (pre * cumulative).astype(BF16)
            ACT[k, :, cols] = act
            SL[k, :, cols] = cumulative + pre * jnp.exp(-0.5 * pre * pre) * 0.3989422804014327
            proj = proj + dot(act, wout[k, cols, :])
        proj = proj + row(k, 52)
        PJ[k] = proj
        out = X[k].astype(F32).reshape(rows, chans) + row(k, 53) * proj
        X[k + 1] = out.astype(BF16).reshape(pair, height, width, chans)
        return carry

    lax.fori_loop(0, 2, forward, 0)

    @pl.when(sx == 0)
    def _():
        hop_x().start()
        hop_g().wait_recv()

    def grad_copy(k, t):
        at = pl.ds(t * chans, chans)
        return copy(PG.at[k, at], RG.at[at], csend.at[t], crecv.at[t], sib)

    def vec_copy(k):
        return copy(GV.at[k], RV, cvsend, cvrecv, sib)

    def ig_copy(k):
        return copy(G.at[k], IG.at[my_micros], isend, irecv, sib)

    def plane_copy(c, r):
        lo, hi = chunks[c]
        q, dev = plane_dev(r)
        at = pl.ds(lo * zrows, (hi - lo) * zrows)
        return copy(S.at[q, at], RB.at[r, at], psend.at[c, r], precv.at[c, r], dev)

    def plane_vec_copy(r):
        q, dev = plane_dev(r)
        return copy(SV.at[q], RBV.at[r], pvsend.at[r], pvrecv.at[r], dev)

    def chip_sum(k):
        for t in range(2 * quarters):
            grad_copy(k, t).wait_recv()
        for c, (lo, hi) in enumerate(chunks):

            @pl.loop(1, nplane + 1)
            def _(r):
                p = lax.rem(plane + r, nplane)
                for s in range(lo, hi):
                    start = p * part + z_at(offset(s)) * zrows
                    at = pl.ds(pl.multiple_of(start, zrows), zrows)
                    S[p, s * zrows : (s + 1) * zrows, :] = (
                        PG[k, at, :].astype(F32) + RG[at, :].astype(F32)
                    ).astype(BF16)

                @pl.when(r < nplane)
                def _():
                    plane_copy(c, r).start()

    def chip_vec_sum(k):
        vec_copy(k).wait_recv()
        for t in range(nplane):
            at_row, at_col = (t // vcols) * VTILE, (t % vcols) * vlanes
            tile = (slice(at_row, at_row + VTILE), slice(at_col, at_col + vlanes))
            SV[t] = (GV[(k,) + tile] + RV[tile]).astype(BF16)

        @pl.loop(1, nplane)
        def _(r):
            plane_vec_copy(r).start()

    def backward(step, carry):
        k = 1 - step
        gf = G[k + 1].astype(F32).reshape(rows, chans)
        GV[k, 53:54, :] = over_rows(gf * PJ[k])
        dproj = gf * row(k, 53)
        GV[k, 52:53, :] = over_rows(dproj)
        dproj_b = dproj.astype(BF16)
        normed = NB[k]
        dn = jnp.zeros((rows, chans), F32)
        for q in range(quarters):
            cols = slice(q * chans, (q + 1) * chans)
            dact = dot_nt(dproj_b, wout[k, cols, :])
            PG[k, hidden + q * chans : hidden + (q + 1) * chans, :] = dot_tn(
                ACT[k, :, cols], dproj_b
            ).astype(BF16)
            dpre = dact * SL[k, :, cols]
            GV[k, 54 + q : 55 + q, :] = over_rows(dpre)
            dpre_b = dpre.astype(BF16)
            PG[k, cols, :] = dot_tn(normed, dpre_b).astype(BF16)

            @pl.when(core != k)
            def _():
                grad_copy(k, quarters + q).start()
                grad_copy(k, q).start()

            dn = dn + dot_nt(dpre_b, win[k, :, cols])

        @pl.when((sx == 0) & (core == 1) & (k == 0))
        def _():
            chip_sum(1)
            chip_vec_sum(1)

        xhat = XH[k]
        GV[k, 50:51, :] = over_rows(dn * xhat)
        GV[k, 51:52, :] = over_rows(dn)
        dxh = dn * row(k, 50)
        m1 = jnp.sum(dxh, axis=1, keepdims=True) * (1.0 / chans)
        m2 = jnp.sum(dxh * xhat, axis=1, keepdims=True) * (1.0 / chans)
        rstd = RSTD[k][:, 0:1]
        dconv = (dxh - m1 - xhat * m2) * rstd
        GV[k, 49:50, :] = over_rows(dconv)
        xpad[:, :, 8 : 8 + width, :] = dconv.reshape(pair, height, width, chans)
        for half in range(chans // 128):
            lanes = slice(half * 128, half * 128 + 128)
            acc = [G[k + 1, :, h, :, lanes].astype(F32) for h in range(height)]
            xs = [X[k, :, h, :, lanes].astype(F32) for h in range(height)]
            for j in range(7):
                shifted = [xpad[:, h, 11 - j : 11 - j + width, lanes] for h in range(height)]
                for i in range(7):
                    t = 7 * i + j
                    tap = vec[k, t, :, lanes][None]
                    total = None
                    for h in range(height):
                        if 0 <= h - i + 3 < height:
                            acc[h] = acc[h] + shifted[h - i + 3] * tap
                            term = xs[h] * shifted[h - i + 3]
                            total = term if total is None else total + term
                    GV[k, t : t + 1, lanes] = over_rows(total.reshape(pair * width, 128))
            for h in range(height):
                G[k, :, h, :, lanes] = acc[h].astype(BF16)

        @pl.when(core != k)
        def _():
            vec_copy(k).start()
            ig_copy(k).start()

        @pl.when(core == k)
        def _():
            IG[my_micros] = G[k]

        return carry

    lax.fori_loop(0, 2, backward, 0)

    @pl.when(sx == 1)
    def _():
        hop_g().start()
        hop_g().wait_send()

    @pl.when((core == 0) | (sx == 1))
    def _():
        chip_sum(core)
        chip_vec_sum(core)

    def z_copy(s):
        src = S.at[plane, pl.ds(s * zrows, zrows)]
        return copy(src, ZB.at[s], zsend.at[s], zrecv.at[s], {"z": z_at(offset(s))})

    for c, (lo, hi) in enumerate(chunks):

        @pl.loop(1, nplane)
        def _(r):
            plane_copy(c, r).wait_recv()

        for s in reversed(range(lo, hi)):
            at = slice(s * zrows, (s + 1) * zrows)
            acc = S[plane, at, :].astype(F32)
            for t in range(1, nplane):
                acc = acc + RB[t, at, :].astype(F32)
            if s > 0:
                S[plane, at, :] = acc.astype(BF16)
                z_copy(s).start()
            else:
                ZB[0] = acc.astype(BF16)

    def vec_up():
        r = lax.rem(owner - z + nz, nz)
        return copy(RBV.at[0], VZ.at[r], vsend, vrecv.at[r], {"z": owner})

    @pl.loop(1, nplane)
    def _(r):
        plane_vec_copy(r).wait_recv()

    vacc = SV[plane].astype(F32)
    for r in range(1, nplane):
        vacc = vacc + RBV[r].astype(F32)
    RBV[0] = vacc.astype(BF16)

    @pl.when(z != owner)
    def _():
        vec_up().start()

    def share_copy(s):
        return copy(
            GATH.at[plane, pl.ds(0, zrows)],
            GATH.at[plane, pl.ds(mirror(s, nz) * zrows, zrows)],
            asend.at[s], arecv.at[mirror(s, nz)], {"z": z_at(offset(s))},
        )

    def group_copy(g, r):
        lo, hi = groups[g]
        at = pl.ds(lo * zrows, (hi - lo) * zrows)
        return copy(
            GATH.at[plane, at], GATH.at[plane, at], gsend.at[g, r], grecv.at[g, r],
            plane_dev(r)[1],
        )

    for s in range(1, nz):
        z_copy(s).wait_recv()
    share = ZB[0].astype(F32)
    for s in range(1, nz):
        share = share + ZB[s].astype(F32)
    GATH[plane, 0:zrows, :] = share.astype(BF16)
    for s in reversed(range(1, nz)):
        share_copy(s).start()

    @pl.loop(1, nplane)
    def _(r):
        group_copy(0, r).start()

    SQS[2 * sx + core] = jnp.broadcast_to(jnp.sum(share * share), (1, 128))

    def vec_down(r):
        return copy(
            GATHV.at[plane], GATHV.at[plane], bsend.at[r], brecv, {"z": z_at(r)}
        )

    @pl.when(z == owner)
    def _():
        @pl.loop(1, nz)
        def _(r):
            copy(VZ.at[r], VZ.at[r], vsend, vrecv.at[r], {"z": owner}).wait_recv()

        total = RBV[0].astype(F32)
        for r in range(1, nz):
            total = total + VZ[r].astype(F32)
        GATHV[plane] = total.astype(BF16)

        @pl.loop(1, nz)
        def _(r):
            vec_down(r).start()

        SQS[2 * sx + core] = SQS[2 * sx + core] + jnp.broadcast_to(
            jnp.sum(total * total), (1, 128)
        )

    def sq_block(t):
        at = SQS.at[2 * sx + core]
        return copy(at, at, qsend.at[t], qrecv.at[t], (sib, far, diag)[t])

    def sq_z(r):
        at = SQZ.at[z]
        return copy(at, at, qzsend.at[r], qzrecv.at[r], {"z": z_at(r)})

    def sq_plane(r):
        at = SQP.at[plane]
        return copy(at, at, qpsend.at[r], qprecv.at[r], plane_dev(r)[1])

    for t in range(3):
        sq_block(t).start()

    def forward_group(g):
        lo, hi = groups[g]
        for s in range(lo, hi):
            at = GATH.at[plane, pl.ds(s * zrows, zrows)]
            copy(at, at, asend.at[s], arecv.at[s], sib).wait_recv()

        @pl.loop(1, nplane)
        def _(r):
            group_copy(g, r).start()

    forward_group(1)
    mates = (2 * sx + 1 - core, 2 * (1 - sx) + core, 2 * (1 - sx) + 1 - core)
    for t in range(3):
        at = SQS.at[mates[t]]
        copy(at, at, qsend.at[t], qrecv.at[t], sib).wait_recv()
    SQZ[z] = (SQS[0] + SQS[1]) + (SQS[2] + SQS[3])

    @pl.loop(1, nz)
    def _(r):
        sq_z(r).start()

    for g in range(2, len(groups)):
        forward_group(g)

    def vec_out(r):
        at = GATHV.at[plane]
        return copy(at, at, gvsend.at[r], gvrecv.at[r], plane_dev(r)[1])

    @pl.when(z != owner)
    def _():
        vec_down(1).wait_recv()

    @pl.loop(1, nplane)
    def _(r):
        vec_out(r).start()

    @pl.loop(1, nz)
    def _(r):
        at = SQZ.at[z_at(-r)]
        copy(at, at, qzsend.at[r], qzrecv.at[r], sib).wait_recv()

    total = SQZ[0]
    for t in range(1, nz):
        total = total + SQZ[t]
    SQP[plane] = total

    @pl.loop(1, nplane)
    def _(r):
        sq_plane(r).start()

    def store(q):
        return pltpu.make_async_copy(GATH.at[q], gath_ref.at[q], store_sem.at[q])

    store(plane).start()
    ig_copy(0).wait_recv()
    ig_out = pltpu.make_async_copy(IG, ig_ref, load_sem.at[4])
    ig_out.start()

    for c in wcopies:
        c.wait_send()

    @pl.when(sx == 0)
    def _():
        hop_x().wait_send()

    ig_copy(0).wait_send()
    for t in range(2 * quarters):
        grad_copy(0, t).wait_send()
    vec_copy(0).wait_send()

    @pl.loop(1, nplane)
    def _(r):
        for c in range(len(chunks)):
            plane_copy(c, r).wait_send()
        plane_vec_copy(r).wait_send()

    for s in range(1, nz):
        z_copy(s).wait_send()
        share_copy(s).wait_send()

    @pl.when(z != owner)
    def _():
        vec_up().wait_send()

    @pl.when(z == owner)
    def _():
        @pl.loop(1, nz)
        def _(r):
            vec_down(r).wait_send()

    for t in range(3):
        sq_block(t).wait_send()

    @pl.loop(1, nz)
    def _(r):
        sq_z(r).wait_send()

    @pl.loop(1, nplane)
    def _(r):
        q = lax.rem(plane - r + nplane, nplane)
        for g, (lo, hi) in enumerate(groups):
            at = GATH.at[q, pl.ds(lo * zrows, (hi - lo) * zrows)]
            copy(at, at, gsend.at[g, r], grecv.at[g, r], sib).wait_recv()
        store(q).start()
        copy(GATHV.at[q], GATHV.at[q], gvsend.at[r], gvrecv.at[r], sib).wait_recv()
        copy(SQP.at[q], SQP.at[q], qpsend.at[r], qprecv.at[r], sib).wait_recv()

    gathv_ref[...] = GATHV[...]
    total = SQP[0]
    for t in range(1, nplane):
        total = total + SQP[t]
    factor = jnp.minimum(1.0, (params**0.5) * lax.rsqrt(total + 1e-06))
    fac_ref[...] = jnp.broadcast_to(factor, fac_ref.shape)

    @pl.loop(1, nplane)
    def _(r):
        for g in range(len(groups)):
            group_copy(g, r).wait_send()
        vec_out(r).wait_send()
        sq_plane(r).wait_send()

    @pl.loop(0, nplane)
    def _(q):
        store(q).wait()

    ig_out.wait()


def scale_kernel(nz, gath, gathv, fac, ig, o_in, o_out, o_vec, o_ig):
    nplane, _, vlanes = gathv.shape
    chans = gath.shape[3]
    zrows = gath.shape[2] // nz
    vcols = chans // vlanes
    z = lax.axis_index("z")
    f = fac[0:1, 0:1]
    for s in range(nz):
        q = lax.rem(z + offset(s) + nz, nz)
        at = pl.ds(pl.multiple_of(q * zrows, zrows), zrows)
        o_in[at, :] = gath[0, 0, s * zrows : (s + 1) * zrows, :].astype(F32) * f
        o_out[at, :] = gath[1, 0, s * zrows : (s + 1) * zrows, :].astype(F32) * f

    @pl.when(pl.program_id(0) == 0)
    def _():
        for p in range(nplane):
            at_row, at_col = (p // vcols) * VTILE, (p % vcols) * vlanes
            tile = gathv[p].astype(F32) * f
            for t in range(min(VTILE, o_vec.shape[0] - at_row)):
                o_vec[at_row + t, :, at_col : at_col + vlanes] = tile[t : t + 1, :]

    o_ig[...] = ig[...]


def per_device(dims, inputs, out_grad, w_in, w_out, vector_params):
    nz, ny, nx, params = dims
    nplane = ny * nx
    micros, _, height, width, chans = inputs.shape
    hidden = w_in.shape[2]
    vrows = vector_params.shape[1]
    pair = micros // 2
    rows = pair * height * width
    part = 2 * hidden // nplane
    zrows = part // nz
    vlanes = VPAD * chans // nplane // VTILE
    chunks, groups = spans(nz)
    maps = (micros, height, width, chans)
    small = (pair, height, width, chans)
    vm = pltpu.VMEM
    dma = pltpu.SemaphoreType.DMA
    in_vmem = pl.BlockSpec(memory_space=pltpu.VMEM)
    in_hbm = pl.BlockSpec(memory_space=pltpu.HBM)
    gath, gathv, fac, ig = pl.pallas_call(
        functools.partial(relay_kernel, dims),
        out_shape=(
            jax.ShapeDtypeStruct((nplane, part, chans), BF16),
            jax.ShapeDtypeStruct((nplane, VTILE, vlanes), BF16),
            jax.ShapeDtypeStruct((8, 128), F32),
            jax.ShapeDtypeStruct(maps, BF16),
        ),
        in_specs=[in_hbm] * 5,
        out_specs=(in_hbm, in_vmem, in_vmem, in_hbm),
        scratch_shapes=[
            vm((2, chans, hidden), BF16),
            vm((2, hidden, chans), BF16),
            vm((2, vrows, 1, chans), F32),
            vm((3,) + small, BF16),
            vm((3,) + small, BF16),
            vm((pair, height, width + 16, chans), F32),
            vm(small, F32),
            vm((2, rows, chans), F32),
            vm((2, rows, 128), F32),
            vm((2, rows, chans), BF16),
            vm((2, rows, hidden), BF16),
            vm((2, rows, hidden), F32),
            vm((2, rows, chans), F32),
            vm((2, 2 * hidden, chans), BF16),
            vm((2, VPAD, chans), F32),
            vm((2 * hidden, chans), BF16),
            vm((VPAD, chans), F32),
            vm(maps, BF16),
            vm((nplane, part, chans), BF16),
            vm((nplane, part, chans), BF16),
            vm((nplane, VTILE, vlanes), BF16),
            vm((nplane, VTILE, vlanes), BF16),
            vm((nz, zrows, chans), BF16),
            vm((nz, VTILE, vlanes), BF16),
            vm((nplane, part, chans), BF16),
            vm((nplane, VTILE, vlanes), BF16),
            vm((4, 1, 128), F32),
            vm((nz, 1, 128), F32),
            vm((nplane, 1, 128), F32),
            dma((5,)),
            dma((3,)), dma((3,)),
            dma, dma,
            dma, dma,
            dma((2 * hidden // chans,)), dma((2 * hidden // chans,)),
            dma, dma,
            dma((len(chunks), nplane)), dma((len(chunks), nplane)),
            dma((nplane,)), dma((nplane,)),
            dma((nz,)), dma((nz,)),
            dma, dma((nz,)),
            dma((nz,)), dma,
            dma((nz,)), dma((nz,)),
            dma((len(groups), nplane)), dma((len(groups), nplane)),
            dma((nplane,)), dma((nplane,)),
            dma((3,)), dma((3,)),
            dma((nz,)), dma((nz,)),
            dma((nplane,)), dma((nplane,)),
            dma((nplane,)),
        ],
        compiler_params=pltpu.CompilerParams(
            collective_id=0, has_side_effects=True, vmem_limit_bytes=60 * 1024 * 1024
        ),
        name="relay",
    )(
        inputs.reshape(maps), out_grad.reshape(maps), w_in[0], w_out[0],
        jnp.swapaxes(vector_params, 0, 1),
    )
    quarters = hidden // chans
    o_in, o_out, o_vec, o_ig = pl.pallas_call(
        functools.partial(scale_kernel, nz),
        out_shape=(
            jax.ShapeDtypeStruct((chans, hidden), F32),
            jax.ShapeDtypeStruct((hidden, chans), F32),
            jax.ShapeDtypeStruct((vrows, 1, chans), F32),
            jax.ShapeDtypeStruct(maps, BF16),
        ),
        grid=(quarters,),
        in_specs=[
            pl.BlockSpec((2, 1, chans, chans), lambda t: (0, t, 0, 0)),
            pl.BlockSpec((nplane, VTILE, vlanes), lambda t: (0, 0, 0)),
            pl.BlockSpec((8, 128), lambda t: (0, 0)),
            pl.BlockSpec((1,) + maps[1:], lambda t: (t, 0, 0, 0)),
        ],
        out_specs=(
            pl.BlockSpec((chans, chans), lambda t: (0, t)),
            pl.BlockSpec((chans, chans), lambda t: (t, 0)),
            pl.BlockSpec((vrows, 1, chans), lambda t: (0, 0, 0)),
            pl.BlockSpec((1,) + maps[1:], lambda t: (t, 0, 0, 0)),
        ),
        compiler_params=pltpu.CompilerParams(vmem_limit_bytes=60 * 1024 * 1024),
        name="scale",
    )(gath.reshape(2, quarters, chans, chans), gathv, fac, ig)
    return (
        o_ig.reshape((1, micros, 1, height, width, chans)),
        o_in[None],
        o_out[None],
        jnp.swapaxes(o_vec, 0, 1),
    )


def solution(mesh):
    nx = 2
    ny = 4
    nz = mesh.shape["dp"] // (nx * ny)
    return program_on(mesh, nz, ny, nx)


def program_on(mesh, nz, ny, nx, params=2156544):
    split = Mesh(mesh.devices.reshape(2, 2, nz, ny, nx), ("sx", "core", "z", "y", "xl"))
    dp = ("z", "y", "xl")
    seg = ("sx", "core")
    in_specs = (
        P(None, dp, None, None, None),
        P(None, dp, None, None, None),
        P(seg, None, None),
        P(seg, None, None),
        P(seg, None, None),
    )
    out_specs = (
        P(seg, None, dp, None, None, None),
        P(seg, None, None),
        P(seg, None, None),
        P(seg, None, None),
    )
    return jax.shard_map(
        functools.partial(per_device, (nz, ny, nx, params)),
        mesh=split, in_specs=in_specs, out_specs=out_specs, check_vma=False,
    )
```

```python
import functools

import jax
import jax.numpy as jnp
from jax import lax
from jax.experimental import pallas as pl
from jax.experimental.pallas import tpu as pltpu
from jax.sharding import Mesh
from jax.sharding import PartitionSpec as P

F32 = jnp.float32
BF16 = jnp.bfloat16
VTILE = 16
VPAD = 64


def dot(a, b):
    return jnp.dot(a, b, preferred_element_type=F32)


def dot_nt(a, b):
    return lax.dot_general(a, b, (((1,), (1,)), ((), ())), preferred_element_type=F32)


def dot_tn(a, b):
    return lax.dot_general(a, b, (((0,), (0,)), ((), ())), preferred_element_type=F32)


def over_rows(a):
    return jnp.sum(a, axis=0, keepdims=True)


def spans(nz):
    if nz == 16:
        return ((11, 16), (6, 11), (0, 6)), ((0, 1), (1, 5), (5, 9), (9, 13), (13, 16))
    return ((1, nz), (0, 1)), ((0, 1), (1, nz))


def offset(s):
    return (s + 1) // 2 if s % 2 else -(s // 2)


def mirror(s, nz):
    if s == 0 or s == nz - 1:
        return s
    return s + 1 if s % 2 else s - 1


def relay_kernel(
    dims, x_ref, g_ref, win_ref, wout_ref, vec_ref, gath_ref, gathv_ref, fac_ref, ig_ref,
    win, wout, vec, X, G, xpad, cv, XH, RSTD, NB, ACT, SL, PJ,
    PG, GV, RG, RV, IG, S, RB, SV, RBV, ZB, VZ, GATH, GATHV, SQS, SQZ, SQP,
    load_sem, wsend, wrecv, hsend, hrecv, isend, irecv, csend, crecv, cvsend, cvrecv,
    psend, precv, pvsend, pvrecv, zsend, zrecv, vsend, vrecv, bsend, brecv, asend, arecv,
    gsend, grecv, gvsend, gvrecv, qsend, qrecv, qzsend, qzrecv, qpsend, qprecv, store_sem, known_sem,
):
    nz, ny, nx, params = dims
    nplane = ny * nx
    core = lax.axis_index("core")
    sx = lax.axis_index("sx")
    z = lax.axis_index("z")
    y = lax.axis_index("y")
    xl = lax.axis_index("xl")
    plane = y * nx + xl
    pair, height, width, chans = X.shape[1:]
    rows = pair * height * width
    hidden = win.shape[2]
    quarters = hidden // chans
    part = 2 * hidden // nplane
    zrows = part // nz
    vlanes = SV.shape[2]
    vcols = chans // vlanes
    owner = lax.rem(2 * plane + core, nz)
    chunks, groups = spans(nz)

    def copy(src, dst, ss, rs, dev):
        return pltpu.make_async_remote_copy(
            src_ref=src, dst_ref=dst, send_sem=ss, recv_sem=rs,
            device_id=dev, device_id_type=pl.DeviceIdType.MESH,
        )

    sib = {"core": 1 - core}
    far = {"sx": 1 - sx}
    diag = {"core": 1 - core, "sx": 1 - sx}

    def plane_dev(r):
        q = lax.rem(plane + r, nplane)
        return q, {"y": q // nx, "xl": lax.rem(q, nx)}

    def z_at(by):
        return lax.rem(z + by + nz, nz)

    loads = [
        pltpu.make_async_copy(vec_ref, vec.at[core], load_sem.at[0]),
        pltpu.make_async_copy(win_ref, win.at[core], load_sem.at[1]),
        pltpu.make_async_copy(wout_ref, wout.at[core], load_sem.at[2]),
    ]
    for c in loads:
        c.start()
    my_micros = pl.ds(core * pair, pair)

    def load_x():
        return pltpu.make_async_copy(x_ref.at[my_micros], X.at[0], load_sem.at[3])

    def load_g():
        return pltpu.make_async_copy(g_ref.at[my_micros], G.at[2], load_sem.at[3])

    @pl.when(sx == 0)
    def _():
        load_x().start()

    @pl.when(sx == 1)
    def _():
        load_g().start()

    barrier = pltpu.get_barrier_semaphore()

    def hello(dev):
        pl.semaphore_signal(barrier, inc=1, device_id=dev, device_id_type=pl.DeviceIdType.MESH)

    hello({"z": z_at(1)})
    hello({"z": z_at(-1)})

    @pl.loop(1, nplane)
    def _(r):
        hello(plane_dev(r)[1])

    hello(diag)
    hello(far)
    hello(sib)

    zero_side = jnp.zeros((pair, height, 8, chans), F32)
    xpad[:, :, 0:8, :] = zero_side
    xpad[:, :, 8 + width : 16 + width, :] = zero_side
    GV[...] = jnp.zeros(GV.shape, F32)

    @pl.when(sx == 0)
    def _():
        load_x().wait()

    @pl.when(sx == 1)
    def _():
        load_g().wait()

    pl.semaphore_wait(barrier, 3 + (nplane - 1) + 2)

    wcopies = [
        copy(vec_ref, vec.at[core], wsend.at[0], wrecv.at[0], sib),
        copy(win_ref, win.at[core], wsend.at[1], wrecv.at[1], sib),
        copy(wout_ref, wout.at[core], wsend.at[2], wrecv.at[2], sib),
    ]
    for c in wcopies:
        c.start()

    reaches = [1 << t for t in range(8) if (1 << t) < nz // 2]

    def tell(t):
        for by in (reaches[t], -reaches[t]):
            pl.semaphore_signal(
                known_sem.at[t], inc=1, device_id={"z": z_at(by)},
                device_id_type=pl.DeviceIdType.MESH,
            )

    def heard(t):
        pl.semaphore_wait(known_sem.at[t], 2)

    if reaches:
        tell(0)

    def hop_x():
        return copy(X.at[2], X.at[0], hsend, hrecv, far)

    def hop_g():
        return copy(G.at[0], G.at[2], hsend, hrecv, far)

    @pl.when(sx == 1)
    def _():
        hop_x().wait_recv()

    def row(k, t):
        return vec[k, t]

    def forward(k, carry):
        @pl.when(core == k)
        def _():
            for c in loads:
                c.wait()

        @pl.when(core != k)
        def _():
            for c in wcopies:
                c.wait_recv()

        xpad[:, :, 8 : 8 + width, :] = X[k].astype(F32)
        for half in range(chans // 128):
            lanes = slice(half * 128, half * 128 + 128)
            acc = [None] * height
            for j in range(7):
                shifted = [xpad[:, h, 5 + j : 5 + j + width, lanes] for h in range(height)]
                for i in range(7):
                    tap = vec[k, 7 * i + j, :, lanes][None]
                    for h in range(height):
                        if 0 <= h + i - 3 < height:
                            term = shifted[h + i - 3] * tap
                            acc[h] = term if acc[h] is None else acc[h] + term
            bias = vec[k, 49, :, lanes][None]
            for h in range(height):
                cv[:, h, :, lanes] = acc[h] + bias
        conv = cv[...].reshape(rows, chans)
        mean = jnp.sum(conv, axis=1, keepdims=True) * (1.0 / chans)
        centered = conv - mean
        var = jnp.sum(centered * centered, axis=1, keepdims=True) * (1.0 / chans)
        rstd = lax.rsqrt(var + 1e-06)
        xhat = centered * rstd
        XH[k] = xhat
        RSTD[k] = jnp.broadcast_to(rstd, (rows, 128))
        normed = (xhat * row(k, 50) + row(k, 51)).astype(BF16)
        NB[k] = normed
        proj = jnp.zeros((rows, chans), F32)
        for q in range(quarters):
            cols = slice(q * chans, (q + 1) * chans)
            pre = dot(normed, win[k, :, cols]) + row(k, 54 + q)
            cumulative = 0.5 * (1.0 + lax.erf(pre * 0.7071067811865476))
            act = (pre * cumulative).astype(BF16)
            ACT[k, :, cols] = act
            SL[k, :, cols] = cumulative + pre * jnp.exp(-0.5 * pre * pre) * 0.3989422804014327
            proj = proj + dot(act, wout[k, cols, :])
        proj = proj + row(k, 52)
        PJ[k] = proj
        out = X[k].astype(F32).reshape(rows, chans) + row(k, 53) * proj
        X[k + 1] = out.astype(BF16).reshape(pair, height, width, chans)
        return carry

    lax.fori_loop(0, 2, forward, 0)
    if len(reaches) > 1:
        heard(0)
        tell(1)

    @pl.when(sx == 0)
    def _():
        hop_x().start()
        hop_g().wait_recv()

    def grad_copy(k, t):
        at = pl.ds(t * chans, chans)
        return copy(PG.at[k, at], RG.at[at], csend.at[t], crecv.at[t], sib)

    def vec_copy(k):
        return copy(GV.at[k], RV, cvsend, cvrecv, sib)

    def ig_copy(k):
        return copy(G.at[k], IG.at[my_micros], isend, irecv, sib)

    def plane_copy(c, r):
        lo, hi = chunks[c]
        q, dev = plane_dev(r)
        at = pl.ds(lo * zrows, (hi - lo) * zrows)
        return copy(S.at[q, at], RB.at[r, at], psend.at[c, r], precv.at[c, r], dev)

    def plane_vec_copy(r):
        q, dev = plane_dev(r)
        return copy(SV.at[q], RBV.at[r], pvsend.at[r], pvrecv.at[r], dev)

    def chip_sum(k):
        for t in range(2 * quarters):
            grad_copy(k, t).wait_recv()
        for c, (lo, hi) in enumerate(chunks):

            @pl.loop(1, nplane + 1)
            def _(r):
                p = lax.rem(plane + r, nplane)
                for s in range(lo, hi):
                    start = p * part + z_at(offset(s)) * zrows
                    at = pl.ds(pl.multiple_of(start, zrows), zrows)
                    S[p, s * zrows : (s + 1) * zrows, :] = (
                        PG[k, at, :].astype(F32) + RG[at, :].astype(F32)
                    ).astype(BF16)

                @pl.when(r < nplane)
                def _():
                    plane_copy(c, r).start()

    def chip_vec_sum(k):
        vec_copy(k).wait_recv()
        for t in range(nplane):
            at_row, at_col = (t // vcols) * VTILE, (t % vcols) * vlanes
            tile = (slice(at_row, at_row + VTILE), slice(at_col, at_col + vlanes))
            SV[t] = (GV[(k,) + tile] + RV[tile]).astype(BF16)

        @pl.loop(1, nplane)
        def _(r):
            plane_vec_copy(r).start()

    def backward(step, carry):
        k = 1 - step

        if len(reaches) > 2:

            @pl.when(step == 1)
            def _():
                heard(1)
                tell(2)

        @pl.when((sx == 0) & (core == 1) & (k == 0))
        def _():
            chip_sum(1)

        gf = G[k + 1].astype(F32).reshape(rows, chans)
        GV[k, 53:54, :] = over_rows(gf * PJ[k])
        dproj = gf * row(k, 53)
        GV[k, 52:53, :] = over_rows(dproj)
        dproj_b = dproj.astype(BF16)
        normed = NB[k]
        dn = jnp.zeros((rows, chans), F32)
        for q in range(quarters):
            cols = slice(q * chans, (q + 1) * chans)
            dact = dot_nt(dproj_b, wout[k, cols, :])
            PG[k, hidden + q * chans : hidden + (q + 1) * chans, :] = dot_tn(
                ACT[k, :, cols], dproj_b
            ).astype(BF16)
            dpre = dact * SL[k, :, cols]
            GV[k, 54 + q : 55 + q, :] = over_rows(dpre)
            dpre_b = dpre.astype(BF16)
            PG[k, cols, :] = dot_tn(normed, dpre_b).astype(BF16)

            @pl.when(core != k)
            def _():
                grad_copy(k, quarters + q).start()
                grad_copy(k, q).start()

            dn = dn + dot_nt(dpre_b, win[k, :, cols])

        @pl.when((sx == 0) & (core == 1) & (k == 0))
        def _():
            chip_vec_sum(1)

        xhat = XH[k]
        GV[k, 50:51, :] = over_rows(dn * xhat)
        GV[k, 51:52, :] = over_rows(dn)
        dxh = dn * row(k, 50)
        m1 = jnp.sum(dxh, axis=1, keepdims=True) * (1.0 / chans)
        m2 = jnp.sum(dxh * xhat, axis=1, keepdims=True) * (1.0 / chans)
        rstd = RSTD[k][:, 0:1]
        dconv = (dxh - m1 - xhat * m2) * rstd
        GV[k, 49:50, :] = over_rows(dconv)
        xpad[:, :, 8 : 8 + width, :] = dconv.reshape(pair, height, width, chans)
        for half in range(chans // 128):
            lanes = slice(half * 128, half * 128 + 128)
            acc = [G[k + 1, :, h, :, lanes].astype(F32) for h in range(height)]
            xs = [X[k, :, h, :, lanes].astype(F32) for h in range(height)]
            for j in range(7):
                shifted = [xpad[:, h, 11 - j : 11 - j + width, lanes] for h in range(height)]
                for i in range(7):
                    t = 7 * i + j
                    tap = vec[k, t, :, lanes][None]
                    total = None
                    for h in range(height):
                        if 0 <= h - i + 3 < height:
                            acc[h] = acc[h] + shifted[h - i + 3] * tap
                            term = xs[h] * shifted[h - i + 3]
                            total = term if total is None else total + term
                    GV[k, t : t + 1, lanes] = over_rows(total.reshape(pair * width, 128))
            for h in range(height):
                G[k, :, h, :, lanes] = acc[h].astype(BF16)

        @pl.when(core != k)
        def _():
            vec_copy(k).start()
            ig_copy(k).start()

        @pl.when(core == k)
        def _():
            IG[my_micros] = G[k]

        return carry

    lax.fori_loop(0, 2, backward, 0)

    @pl.when(sx == 1)
    def _():
        hop_g().start()
        hop_g().wait_send()

    @pl.when((core == 0) | (sx == 1))
    def _():
        chip_sum(core)
        chip_vec_sum(core)

    def z_copy(s):
        src = S.at[plane, pl.ds(s * zrows, zrows)]
        return copy(src, ZB.at[s], zsend.at[s], zrecv.at[s], {"z": z_at(offset(s))})

    if reaches:
        heard(len(reaches) - 1)

    for c, (lo, hi) in enumerate(chunks):

        @pl.loop(1, nplane)
        def _(r):
            plane_copy(c, r).wait_recv()

        for s in reversed(range(lo, hi)):
            at = slice(s * zrows, (s + 1) * zrows)
            acc = S[plane, at, :].astype(F32)
            for t in range(1, nplane):
                acc = acc + RB[t, at, :].astype(F32)
            if s > 0:
                S[plane, at, :] = acc.astype(BF16)
                z_copy(s).start()
            else:
                ZB[0] = acc.astype(BF16)

    def vec_up():
        r = lax.rem(owner - z + nz, nz)
        return copy(RBV.at[0], VZ.at[r], vsend, vrecv.at[r], {"z": owner})

    @pl.loop(1, nplane)
    def _(r):
        plane_vec_copy(r).wait_recv()

    vacc = SV[plane].astype(F32)
    for r in range(1, nplane):
        vacc = vacc + RBV[r].astype(F32)
    RBV[0] = vacc.astype(BF16)

    @pl.when(z != owner)
    def _():
        vec_up().start()

    def share_copy(s):
        return copy(
            GATH.at[plane, pl.ds(0, zrows)],
            GATH.at[plane, pl.ds(mirror(s, nz) * zrows, zrows)],
            asend.at[s], arecv.at[mirror(s, nz)], {"z": z_at(offset(s))},
        )

    def group_copy(g, r):
        lo, hi = groups[g]
        at = pl.ds(lo * zrows, (hi - lo) * zrows)
        return copy(
            GATH.at[plane, at], GATH.at[plane, at], gsend.at[g, r], grecv.at[g, r],
            plane_dev(r)[1],
        )

    for s in range(1, nz):
        z_copy(s).wait_recv()
    share = ZB[0].astype(F32)
    for s in range(1, nz):
        share = share + ZB[s].astype(F32)
    GATH[plane, 0:zrows, :] = share.astype(BF16)
    for s in reversed(range(1, nz)):
        share_copy(s).start()

    @pl.loop(1, nplane)
    def _(r):
        group_copy(0, r).start()

    SQS[2 * sx + core] = jnp.broadcast_to(jnp.sum(share * share), (1, 128))

    def vec_down(r):
        return copy(
            GATHV.at[plane], GATHV.at[plane], bsend.at[r], brecv, {"z": z_at(r)}
        )

    @pl.when(z == owner)
    def _():
        @pl.loop(1, nz)
        def _(r):
            copy(VZ.at[r], VZ.at[r], vsend, vrecv.at[r], {"z": owner}).wait_recv()

        total = RBV[0].astype(F32)
        for r in range(1, nz):
            total = total + VZ[r].astype(F32)
        GATHV[plane] = total.astype(BF16)

        @pl.loop(1, nz)
        def _(r):
            vec_down(r).start()

        SQS[2 * sx + core] = SQS[2 * sx + core] + jnp.broadcast_to(
            jnp.sum(total * total), (1, 128)
        )

    def sq_block(t):
        at = SQS.at[2 * sx + core]
        return copy(at, at, qsend.at[t], qrecv.at[t], (sib, far, diag)[t])

    def sq_z(r):
        at = SQZ.at[z]
        return copy(at, at, qzsend.at[r], qzrecv.at[r], {"z": z_at(r)})

    def sq_plane(r):
        at = SQP.at[plane]
        return copy(at, at, qpsend.at[r], qprecv.at[r], plane_dev(r)[1])

    for t in range(3):
        sq_block(t).start()

    def forward_group(g):
        lo, hi = groups[g]
        for s in range(lo, hi):
            at = GATH.at[plane, pl.ds(s * zrows, zrows)]
            copy(at, at, asend.at[s], arecv.at[s], sib).wait_recv()

        @pl.loop(1, nplane)
        def _(r):
            group_copy(g, r).start()

    forward_group(1)
    mates = (2 * sx + 1 - core, 2 * (1 - sx) + core, 2 * (1 - sx) + 1 - core)
    for t in range(3):
        at = SQS.at[mates[t]]
        copy(at, at, qsend.at[t], qrecv.at[t], sib).wait_recv()
    SQZ[z] = (SQS[0] + SQS[1]) + (SQS[2] + SQS[3])

    @pl.loop(1, nz)
    def _(r):
        sq_z(r).start()

    for g in range(2, len(groups)):
        forward_group(g)

    def vec_out(r):
        at = GATHV.at[plane]
        return copy(at, at, gvsend.at[r], gvrecv.at[r], plane_dev(r)[1])

    @pl.when(z != owner)
    def _():
        vec_down(1).wait_recv()

    @pl.loop(1, nplane)
    def _(r):
        vec_out(r).start()

    @pl.loop(1, nz)
    def _(r):
        at = SQZ.at[z_at(-r)]
        copy(at, at, qzsend.at[r], qzrecv.at[r], sib).wait_recv()

    total = SQZ[0]
    for t in range(1, nz):
        total = total + SQZ[t]
    SQP[plane] = total

    @pl.loop(1, nplane)
    def _(r):
        sq_plane(r).start()

    def store(q):
        return pltpu.make_async_copy(GATH.at[q], gath_ref.at[q], store_sem.at[q])

    store(plane).start()
    ig_copy(0).wait_recv()
    ig_out = pltpu.make_async_copy(IG, ig_ref, load_sem.at[4])
    ig_out.start()

    for c in wcopies:
        c.wait_send()

    @pl.when(sx == 0)
    def _():
        hop_x().wait_send()

    ig_copy(0).wait_send()
    for t in range(2 * quarters):
        grad_copy(0, t).wait_send()
    vec_copy(0).wait_send()

    @pl.loop(1, nplane)
    def _(r):
        for c in range(len(chunks)):
            plane_copy(c, r).wait_send()
        plane_vec_copy(r).wait_send()

    for s in range(1, nz):
        z_copy(s).wait_send()
        share_copy(s).wait_send()

    @pl.when(z != owner)
    def _():
        vec_up().wait_send()

    @pl.when(z == owner)
    def _():
        @pl.loop(1, nz)
        def _(r):
            vec_down(r).wait_send()

    for t in range(3):
        sq_block(t).wait_send()

    @pl.loop(1, nz)
    def _(r):
        sq_z(r).wait_send()

    @pl.loop(1, nplane)
    def _(r):
        q = lax.rem(plane - r + nplane, nplane)
        for g, (lo, hi) in enumerate(groups):
            at = GATH.at[q, pl.ds(lo * zrows, (hi - lo) * zrows)]
            copy(at, at, gsend.at[g, r], grecv.at[g, r], sib).wait_recv()
        store(q).start()
        copy(GATHV.at[q], GATHV.at[q], gvsend.at[r], gvrecv.at[r], sib).wait_recv()
        copy(SQP.at[q], SQP.at[q], qpsend.at[r], qprecv.at[r], sib).wait_recv()

    gathv_ref[...] = GATHV[...]
    total = SQP[0]
    for t in range(1, nplane):
        total = total + SQP[t]
    factor = jnp.minimum(1.0, (params**0.5) * lax.rsqrt(total + 1e-06))
    fac_ref[...] = jnp.broadcast_to(factor, fac_ref.shape)

    @pl.loop(1, nplane)
    def _(r):
        for g in range(len(groups)):
            group_copy(g, r).wait_send()
        vec_out(r).wait_send()
        sq_plane(r).wait_send()

    @pl.loop(0, nplane)
    def _(q):
        store(q).wait()

    ig_out.wait()


def scale_kernel(nz, gath, gathv, fac, ig, o_in, o_out, o_vec, o_ig):
    nplane, part, chans = gath.shape
    hidden = o_in.shape[1]
    quarters = hidden // chans
    zrows = part // nz
    vlanes = gathv.shape[2]
    vcols = chans // vlanes
    z = lax.axis_index("z")
    f = fac[0:1, 0:1]
    per = chans // zrows
    for s in range(nz):
        q = lax.rem(z + offset(s) + nz, nz)
        for p in range(nplane):
            piece = gath[p, s * zrows : (s + 1) * zrows, :].astype(F32) * f
            first = p * part
            if first < hidden:
                if part <= chans:
                    at = pl.ds(pl.multiple_of(first % chans + q * zrows, zrows), zrows)
                    o_in[at, first // chans * chans : first // chans * chans + chans] = piece
                else:
                    for t in range(part // chans):
                        @pl.when(q // per == t)
                        def _():
                            at = pl.ds(pl.multiple_of(lax.rem(q, per) * zrows, zrows), zrows)
                            o_in[at, first + t * chans : first + t * chans + chans] = piece
            else:
                at = pl.ds(pl.multiple_of(first - hidden + q * zrows, zrows), zrows)
                o_out[at, :] = piece
    for p in range(nplane):
        at_row, at_col = (p // vcols) * VTILE, (p % vcols) * vlanes
        tile = gathv[p].astype(F32) * f
        for t in range(min(VTILE, o_vec.shape[0] - at_row)):
            o_vec[at_row + t, :, at_col : at_col + vlanes] = tile[t : t + 1, :]
    o_ig[...] = ig[...]


def per_device(dims, inputs, out_grad, w_in, w_out, vector_params):
    nz, ny, nx, params = dims
    nplane = ny * nx
    micros, _, height, width, chans = inputs.shape
    hidden = w_in.shape[2]
    vrows = vector_params.shape[1]
    pair = micros // 2
    rows = pair * height * width
    part = 2 * hidden // nplane
    zrows = part // nz
    vlanes = VPAD * chans // nplane // VTILE
    chunks, groups = spans(nz)
    maps = (micros, height, width, chans)
    small = (pair, height, width, chans)
    vm = pltpu.VMEM
    dma = pltpu.SemaphoreType.DMA
    in_vmem = pl.BlockSpec(memory_space=pltpu.VMEM)
    in_hbm = pl.BlockSpec(memory_space=pltpu.HBM)
    gath, gathv, fac, ig = pl.pallas_call(
        functools.partial(relay_kernel, dims),
        out_shape=(
            jax.ShapeDtypeStruct((nplane, part, chans), BF16),
            jax.ShapeDtypeStruct((nplane, VTILE, vlanes), BF16),
            jax.ShapeDtypeStruct((8, 128), F32),
            jax.ShapeDtypeStruct(maps, BF16),
        ),
        in_specs=[in_hbm] * 5,
        out_specs=(in_hbm, in_vmem, in_vmem, in_hbm),
        scratch_shapes=[
            vm((2, chans, hidden), BF16),
            vm((2, hidden, chans), BF16),
            vm((2, vrows, 1, chans), F32),
            vm((3,) + small, BF16),
            vm((3,) + small, BF16),
            vm((pair, height, width + 16, chans), F32),
            vm(small, F32),
            vm((2, rows, chans), F32),
            vm((2, rows, 128), F32),
            vm((2, rows, chans), BF16),
            vm((2, rows, hidden), BF16),
            vm((2, rows, hidden), F32),
            vm((2, rows, chans), F32),
            vm((2, 2 * hidden, chans), BF16),
            vm((2, VPAD, chans), F32),
            vm((2 * hidden, chans), BF16),
            vm((VPAD, chans), F32),
            vm(maps, BF16),
            vm((nplane, part, chans), BF16),
            vm((nplane, part, chans), BF16),
            vm((nplane, VTILE, vlanes), BF16),
            vm((nplane, VTILE, vlanes), BF16),
            vm((nz, zrows, chans), BF16),
            vm((nz, VTILE, vlanes), BF16),
            vm((nplane, part, chans), BF16),
            vm((nplane, VTILE, vlanes), BF16),
            vm((4, 1, 128), F32),
            vm((nz, 1, 128), F32),
            vm((nplane, 1, 128), F32),
            dma((5,)),
            dma((3,)), dma((3,)),
            dma, dma,
            dma, dma,
            dma((2 * hidden // chans,)), dma((2 * hidden // chans,)),
            dma, dma,
            dma((len(chunks), nplane)), dma((len(chunks), nplane)),
            dma((nplane,)), dma((nplane,)),
            dma((nz,)), dma((nz,)),
            dma, dma((nz,)),
            dma((nz,)), dma,
            dma((nz,)), dma((nz,)),
            dma((len(groups), nplane)), dma((len(groups), nplane)),
            dma((nplane,)), dma((nplane,)),
            dma((3,)), dma((3,)),
            dma((nz,)), dma((nz,)),
            dma((nplane,)), dma((nplane,)),
            dma((nplane,)),
            pltpu.SemaphoreType.REGULAR((3,)),
        ],
        compiler_params=pltpu.CompilerParams(
            collective_id=0, has_side_effects=True, vmem_limit_bytes=60 * 1024 * 1024
        ),
        name="relay",
    )(
        inputs.reshape(maps), out_grad.reshape(maps), w_in[0], w_out[0],
        jnp.swapaxes(vector_params, 0, 1),
    )
    o_in, o_out, o_vec, o_ig = pl.pallas_call(
        functools.partial(scale_kernel, nz),
        out_shape=(
            jax.ShapeDtypeStruct((chans, hidden), F32),
            jax.ShapeDtypeStruct((hidden, chans), F32),
            jax.ShapeDtypeStruct((vrows, 1, chans), F32),
            jax.ShapeDtypeStruct(maps, BF16),
        ),
        in_specs=[in_vmem] * 4,
        out_specs=(in_vmem,) * 4,
        compiler_params=pltpu.CompilerParams(vmem_limit_bytes=60 * 1024 * 1024),
        name="scale",
    )(gath, gathv, fac, ig)
    return (
        o_ig.reshape((1, micros, 1, height, width, chans)),
        o_in[None],
        o_out[None],
        jnp.swapaxes(o_vec, 0, 1),
    )


def solution(mesh):
    nx = 2
    ny = 4
    nz = mesh.shape["dp"] // (nx * ny)
    return program_on(mesh, nz, ny, nx)


def program_on(mesh, nz, ny, nx, params=2156544):
    split = Mesh(mesh.devices.reshape(2, 2, nz, ny, nx), ("sx", "core", "z", "y", "xl"))
    dp = ("z", "y", "xl")
    seg = ("sx", "core")
    in_specs = (
        P(None, dp, None, None, None),
        P(None, dp, None, None, None),
        P(seg, None, None),
        P(seg, None, None),
        P(seg, None, None),
    )
    out_specs = (
        P(seg, None, dp, None, None, None),
        P(seg, None, None),
        P(seg, None, None),
        P(seg, None, None),
    )
    return jax.shard_map(
        functools.partial(per_device, (nz, ny, nx, params)),
        mesh=split, in_specs=in_specs, out_specs=out_specs, check_vma=False,
    )
```

```python
import functools

import jax
import jax.numpy as jnp
from jax import lax
from jax.experimental import pallas as pl
from jax.experimental.pallas import tpu as pltpu
from jax.sharding import Mesh
from jax.sharding import PartitionSpec as P

F32 = jnp.float32
BF16 = jnp.bfloat16
VTILE = 16
VPAD = 64


def dot(a, b):
    return jnp.dot(a, b, preferred_element_type=F32)


def dot_nt(a, b):
    return lax.dot_general(a, b, (((1,), (1,)), ((), ())), preferred_element_type=F32)


def dot_tn(a, b):
    return lax.dot_general(a, b, (((0,), (0,)), ((), ())), preferred_element_type=F32)


def over_rows(a):
    return jnp.sum(a, axis=0, keepdims=True)


def spans(nz):
    if nz == 16:
        return ((13, 16), (10, 13), (7, 10), (4, 7), (0, 4)), ((0, 1), (1, 5), (5, 9), (9, 13), (13, 16))
    return ((1, nz), (0, 1)), ((0, 1), (1, nz))


def offset(s):
    return (s + 1) // 2 if s % 2 else -(s // 2)


def mirror(s, nz):
    if s == 0 or s == nz - 1:
        return s
    return s + 1 if s % 2 else s - 1


def relay_kernel(
    dims, x_ref, g_ref, win_ref, wout_ref, vec_ref, gath_ref, gathv_ref, fac_ref, ig_ref,
    win, wout, vec, X, G, xpad, cv, XH, RSTD, NB, ACT, SL, PJ,
    PG, GV, RG, RV, IG, S, RB, SV, RBV, ZB, VZ, GATH, GATHV, SQS, SQZ, SQP,
    load_sem, wsend, wrecv, hsend, hrecv, isend, irecv, csend, crecv, cvsend, cvrecv,
    psend, precv, pvsend, pvrecv, zsend, zrecv, vsend, vrecv, bsend, brecv, asend, arecv,
    gsend, grecv, gvsend, gvrecv, qsend, qrecv, qzsend, qzrecv, qpsend, qprecv, store_sem, known_sem,
):
    nz, ny, nx, params = dims
    nplane = ny * nx
    core = lax.axis_index("core")
    sx = lax.axis_index("sx")
    z = lax.axis_index("z")
    y = lax.axis_index("y")
    xl = lax.axis_index("xl")
    plane = y * nx + xl
    pair, height, width, chans = X.shape[1:]
    rows = pair * height * width
    hidden = win.shape[2]
    quarters = hidden // chans
    part = 2 * hidden // nplane
    zrows = part // nz
    vlanes = SV.shape[2]
    vcols = chans // vlanes
    owner = lax.rem(2 * plane + core, nz)
    chunks, groups = spans(nz)

    def copy(src, dst, ss, rs, dev):
        return pltpu.make_async_remote_copy(
            src_ref=src, dst_ref=dst, send_sem=ss, recv_sem=rs,
            device_id=dev, device_id_type=pl.DeviceIdType.MESH,
        )

    sib = {"core": 1 - core}
    far = {"sx": 1 - sx}
    diag = {"core": 1 - core, "sx": 1 - sx}

    def plane_dev(r):
        q = lax.rem(plane + r, nplane)
        return q, {"y": q // nx, "xl": lax.rem(q, nx)}

    def z_at(by):
        return lax.rem(z + by + nz, nz)

    loads = [
        pltpu.make_async_copy(vec_ref, vec.at[core], load_sem.at[0]),
        pltpu.make_async_copy(win_ref, win.at[core], load_sem.at[1]),
        pltpu.make_async_copy(wout_ref, wout.at[core], load_sem.at[2]),
    ]
    for c in loads:
        c.start()
    my_micros = pl.ds(core * pair, pair)

    def load_x():
        return pltpu.make_async_copy(x_ref.at[my_micros], X.at[0], load_sem.at[3])

    def load_g():
        return pltpu.make_async_copy(g_ref.at[my_micros], G.at[2], load_sem.at[3])

    @pl.when(sx == 0)
    def _():
        load_x().start()

    @pl.when(sx == 1)
    def _():
        load_g().start()

    barrier = pltpu.get_barrier_semaphore()

    def hello(dev):
        pl.semaphore_signal(barrier, inc=1, device_id=dev, device_id_type=pl.DeviceIdType.MESH)

    hello({"z": z_at(1)})
    hello({"z": z_at(-1)})

    @pl.loop(1, nplane)
    def _(r):
        hello(plane_dev(r)[1])

    hello(diag)
    hello(far)
    hello(sib)

    zero_side = jnp.zeros((pair, height, 8, chans), F32)
    for k in range(2):
        xpad[k, :, :, 0:8, :] = zero_side
        xpad[k, :, :, 8 + width : 16 + width, :] = zero_side
    GV[...] = jnp.zeros(GV.shape, F32)

    @pl.when(sx == 0)
    def _():
        load_x().wait()

    @pl.when(sx == 1)
    def _():
        load_g().wait()

    pl.semaphore_wait(barrier, 3 + (nplane - 1) + 2)

    wcopies = [
        copy(vec_ref, vec.at[core], wsend.at[0], wrecv.at[0], sib),
        copy(win_ref, win.at[core], wsend.at[1], wrecv.at[1], sib),
        copy(wout_ref, wout.at[core], wsend.at[2], wrecv.at[2], sib),
    ]
    for c in wcopies:
        c.start()

    reaches = [1 << t for t in range(8) if (1 << t) < nz // 2]

    def tell(t):
        for by in (reaches[t], -reaches[t]):
            pl.semaphore_signal(
                known_sem.at[t], inc=1, device_id={"z": z_at(by)},
                device_id_type=pl.DeviceIdType.MESH,
            )

    def heard(t):
        pl.semaphore_wait(known_sem.at[t], 2)

    if reaches:
        tell(0)

    def hop_x():
        return copy(X.at[2], X.at[0], hsend, hrecv, far)

    def hop_g():
        return copy(G.at[0], G.at[2], hsend, hrecv, far)

    @pl.when(sx == 1)
    def _():
        hop_x().wait_recv()

    def row(k, t):
        return vec[k, t]

    def forward(k, carry):
        def ready(t):
            @pl.when(core == k)
            def _():
                loads[t].wait()

            @pl.when(core != k)
            def _():
                wcopies[t].wait_recv()

        xpad[k, :, :, 8 : 8 + width, :] = X[k].astype(F32)
        ready(0)
        for half in range(chans // 128):
            lanes = slice(half * 128, half * 128 + 128)
            acc = [None] * height
            for j in range(7):
                shifted = [xpad[k, :, h, 5 + j : 5 + j + width, lanes] for h in range(height)]
                for i in range(7):
                    tap = vec[k, 7 * i + j, :, lanes][None]
                    for h in range(height):
                        if 0 <= h + i - 3 < height:
                            term = shifted[h + i - 3] * tap
                            acc[h] = term if acc[h] is None else acc[h] + term
            bias = vec[k, 49, :, lanes][None]
            for h in range(height):
                cv[:, h, :, lanes] = acc[h] + bias
        conv = cv[...].reshape(rows, chans)
        mean = jnp.sum(conv, axis=1, keepdims=True) * (1.0 / chans)
        centered = conv - mean
        var = jnp.sum(centered * centered, axis=1, keepdims=True) * (1.0 / chans)
        rstd = lax.rsqrt(var + 1e-06)
        xhat = centered * rstd
        XH[k] = xhat
        RSTD[k] = jnp.broadcast_to(rstd, (rows, 128))
        normed = (xhat * row(k, 50) + row(k, 51)).astype(BF16)
        NB[k] = normed
        ready(1)
        ready(2)
        proj = jnp.zeros((rows, chans), F32)
        for q in range(quarters):
            cols = slice(q * chans, (q + 1) * chans)
            pre = dot(normed, win[k, :, cols]) + row(k, 54 + q)
            cumulative = 0.5 * (1.0 + lax.erf(pre * 0.7071067811865476))
            act = (pre * cumulative).astype(BF16)
            ACT[k, :, cols] = act
            SL[k, :, cols] = cumulative + pre * jnp.exp(-0.5 * pre * pre) * 0.3989422804014327
            proj = proj + dot(act, wout[k, cols, :])
        proj = proj + row(k, 52)
        PJ[k] = proj
        out = X[k].astype(F32).reshape(rows, chans) + row(k, 53) * proj
        X[k + 1] = out.astype(BF16).reshape(pair, height, width, chans)
        return carry

    lax.fori_loop(0, 2, forward, 0)
    if len(reaches) > 1:
        heard(0)
        tell(1)

    @pl.when(sx == 0)
    def _():
        hop_x().start()
        hop_g().wait_recv()

    def grad_copy(k, t):
        at = pl.ds(t * chans, chans)
        return copy(PG.at[k, at], RG.at[at], csend.at[t], crecv.at[t], sib)

    def vec_copy(k):
        return copy(GV.at[k], RV, cvsend, cvrecv, sib)

    def ig_copy(k):
        return copy(G.at[k], IG.at[my_micros], isend, irecv, sib)

    def plane_copy(c, r):
        lo, hi = chunks[c]
        q, dev = plane_dev(r)
        at = pl.ds(lo * zrows, (hi - lo) * zrows)
        return copy(S.at[q, at], RB.at[r, at], psend.at[c, r], precv.at[c, r], dev)

    def plane_vec_copy(r):
        q, dev = plane_dev(r)
        return copy(SV.at[q], RBV.at[r], pvsend.at[r], pvrecv.at[r], dev)

    def chip_sum(k):
        for t in range(2 * quarters):
            grad_copy(k, t).wait_recv()
        for c, (lo, hi) in enumerate(chunks):

            @pl.loop(1, nplane + 1)
            def _(r):
                p = lax.rem(plane + r, nplane)
                for s in range(lo, hi):
                    start = p * part + z_at(offset(s)) * zrows
                    at = pl.ds(pl.multiple_of(start, zrows), zrows)
                    S[p, s * zrows : (s + 1) * zrows, :] = (
                        PG[k, at, :].astype(F32) + RG[at, :].astype(F32)
                    ).astype(BF16)

                @pl.when(r < nplane)
                def _():
                    plane_copy(c, r).start()

    def chip_vec_sum(k):
        vec_copy(k).wait_recv()
        for t in range(nplane):
            at_row, at_col = (t // vcols) * VTILE, (t % vcols) * vlanes
            tile = (slice(at_row, at_row + VTILE), slice(at_col, at_col + vlanes))
            SV[t] = (GV[(k,) + tile] + RV[tile]).astype(BF16)

        @pl.loop(1, nplane)
        def _(r):
            plane_vec_copy(r).start()

    def backward(step, carry):
        k = 1 - step

        if len(reaches) > 2:

            @pl.when(step == 1)
            def _():
                heard(1)
                tell(2)

        @pl.when((sx == 0) & (core == 1) & (k == 0))
        def _():
            chip_sum(1)

        gf = G[k + 1].astype(F32).reshape(rows, chans)
        GV[k, 53:54, :] = over_rows(gf * PJ[k])
        dproj = gf * row(k, 53)
        GV[k, 52:53, :] = over_rows(dproj)
        dproj_b = dproj.astype(BF16)
        normed = NB[k]
        dn = jnp.zeros((rows, chans), F32)
        for q in range(quarters):
            cols = slice(q * chans, (q + 1) * chans)
            dact = dot_nt(dproj_b, wout[k, cols, :])
            PG[k, hidden + q * chans : hidden + (q + 1) * chans, :] = dot_tn(
                ACT[k, :, cols], dproj_b
            ).astype(BF16)
            dpre = dact * SL[k, :, cols]
            GV[k, 54 + q : 55 + q, :] = over_rows(dpre)
            dpre_b = dpre.astype(BF16)
            PG[k, cols, :] = dot_tn(normed, dpre_b).astype(BF16)

            @pl.when(core != k)
            def _():
                grad_copy(k, quarters + q).start()
                grad_copy(k, q).start()

            dn = dn + dot_nt(dpre_b, win[k, :, cols])

        xhat = XH[k]
        GV[k, 50:51, :] = over_rows(dn * xhat)
        GV[k, 51:52, :] = over_rows(dn)
        dxh = dn * row(k, 50)
        m1 = jnp.sum(dxh, axis=1, keepdims=True) * (1.0 / chans)
        m2 = jnp.sum(dxh * xhat, axis=1, keepdims=True) * (1.0 / chans)
        rstd = RSTD[k][:, 0:1]
        dconv = (dxh - m1 - xhat * m2) * rstd
        GV[k, 49:50, :] = over_rows(dconv)
        xpad[k, :, :, 8 : 8 + width, :] = dconv.reshape(pair, height, width, chans)
        for half in range(chans // 128):
            lanes = slice(half * 128, half * 128 + 128)
            acc = [G[k + 1, :, h, :, lanes].astype(F32) for h in range(height)]
            for j in range(7):
                shifted = [xpad[k, :, h, 11 - j : 11 - j + width, lanes] for h in range(height)]
                for i in range(7):
                    tap = vec[k, 7 * i + j, :, lanes][None]
                    for h in range(height):
                        if 0 <= h - i + 3 < height:
                            acc[h] = acc[h] + shifted[h - i + 3] * tap
            for h in range(height):
                G[k, :, h, :, lanes] = acc[h].astype(BF16)

        @pl.when(core != k)
        def _():
            ig_copy(k).start()

        @pl.when(core == k)
        def _():
            IG[my_micros] = G[k]

        return carry

    def tap_grads(step, carry):
        k = 1 - step
        for half in range(chans // 128):
            lanes = slice(half * 128, half * 128 + 128)
            xs = [X[k, :, h, :, lanes].astype(F32) for h in range(height)]
            for j in range(7):
                shifted = [xpad[k, :, h, 11 - j : 11 - j + width, lanes] for h in range(height)]
                for i in range(7):
                    t = 7 * i + j
                    total = None
                    for h in range(height):
                        if 0 <= h - i + 3 < height:
                            term = xs[h] * shifted[h - i + 3]
                            total = term if total is None else total + term
                    GV[k, t : t + 1, lanes] = over_rows(total.reshape(pair * width, 128))

        @pl.when(core != k)
        def _():
            vec_copy(k).start()

        return carry

    lax.fori_loop(0, 2, backward, 0)

    @pl.when(sx == 1)
    def _():
        hop_g().start()

    lax.fori_loop(0, 2, tap_grads, 0)

    @pl.when(sx == 1)
    def _():
        hop_g().wait_send()

    @pl.when((core == 0) | (sx == 1))
    def _():
        chip_sum(core)

    chip_vec_sum(core)

    def z_copy(s):
        src = S.at[plane, pl.ds(s * zrows, zrows)]
        return copy(src, ZB.at[s], zsend.at[s], zrecv.at[s], {"z": z_at(offset(s))})

    if reaches:
        heard(len(reaches) - 1)

    for c, (lo, hi) in enumerate(chunks):

        @pl.loop(1, nplane)
        def _(r):
            plane_copy(c, r).wait_recv()

        for s in reversed(range(lo, hi)):
            at = slice(s * zrows, (s + 1) * zrows)
            acc = S[plane, at, :].astype(F32)
            for t in range(1, nplane):
                acc = acc + RB[t, at, :].astype(F32)
            if s > 0:
                S[plane, at, :] = acc.astype(BF16)
                z_copy(s).start()
            else:
                ZB[0] = acc.astype(BF16)

    def vec_up():
        r = lax.rem(owner - z + nz, nz)
        return copy(RBV.at[0], VZ.at[r], vsend, vrecv.at[r], {"z": owner})

    @pl.loop(1, nplane)
    def _(r):
        plane_vec_copy(r).wait_recv()

    vacc = SV[plane].astype(F32)
    for r in range(1, nplane):
        vacc = vacc + RBV[r].astype(F32)
    RBV[0] = vacc.astype(BF16)

    @pl.when(z != owner)
    def _():
        vec_up().start()

    def share_copy(s):
        return copy(
            GATH.at[plane, pl.ds(0, zrows)],
            GATH.at[plane, pl.ds(mirror(s, nz) * zrows, zrows)],
            asend.at[s], arecv.at[mirror(s, nz)], {"z": z_at(offset(s))},
        )

    def group_copy(g, r):
        lo, hi = groups[g]
        at = pl.ds(lo * zrows, (hi - lo) * zrows)
        return copy(
            GATH.at[plane, at], GATH.at[plane, at], gsend.at[g, r], grecv.at[g, r],
            plane_dev(r)[1],
        )

    for s in range(1, nz):
        z_copy(s).wait_recv()
    share = ZB[0].astype(F32)
    for s in range(1, nz):
        share = share + ZB[s].astype(F32)
    GATH[plane, 0:zrows, :] = share.astype(BF16)
    for s in [*range(1, min(5, nz)), *reversed(range(5, nz))]:
        share_copy(s).start()

    @pl.loop(1, nplane)
    def _(r):
        group_copy(0, r).start()

    SQS[2 * sx + core] = jnp.broadcast_to(jnp.sum(share * share), (1, 128))

    def vec_down(r):
        return copy(
            GATHV.at[plane], GATHV.at[plane], bsend.at[r], brecv, {"z": z_at(r)}
        )

    @pl.when(z == owner)
    def _():
        @pl.loop(1, nz)
        def _(r):
            copy(VZ.at[r], VZ.at[r], vsend, vrecv.at[r], {"z": owner}).wait_recv()

        total = RBV[0].astype(F32)
        for r in range(1, nz):
            total = total + VZ[r].astype(F32)
        GATHV[plane] = total.astype(BF16)

        @pl.loop(1, nz)
        def _(r):
            vec_down(r).start()

        SQS[2 * sx + core] = SQS[2 * sx + core] + jnp.broadcast_to(
            jnp.sum(total * total), (1, 128)
        )

    def sq_block(t):
        at = SQS.at[2 * sx + core]
        return copy(at, at, qsend.at[t], qrecv.at[t], (sib, far, diag)[t])

    def sq_z(r):
        at = SQZ.at[z]
        return copy(at, at, qzsend.at[r], qzrecv.at[r], {"z": z_at(r)})

    def sq_plane(r):
        at = SQP.at[plane]
        return copy(at, at, qpsend.at[r], qprecv.at[r], plane_dev(r)[1])

    for t in range(3):
        sq_block(t).start()

    def forward_group(g):
        lo, hi = groups[g]
        for s in range(lo, hi):
            at = GATH.at[plane, pl.ds(s * zrows, zrows)]
            copy(at, at, asend.at[s], arecv.at[s], sib).wait_recv()

        @pl.loop(1, nplane)
        def _(r):
            group_copy(g, r).start()

    forward_group(1)
    mates = (2 * sx + 1 - core, 2 * (1 - sx) + core, 2 * (1 - sx) + 1 - core)
    for t in range(3):
        at = SQS.at[mates[t]]
        copy(at, at, qsend.at[t], qrecv.at[t], sib).wait_recv()
    SQZ[z] = (SQS[0] + SQS[1]) + (SQS[2] + SQS[3])

    @pl.loop(1, nz)
    def _(r):
        sq_z(r).start()

    for g in range(2, len(groups)):
        forward_group(g)

    def vec_out(r):
        at = GATHV.at[plane]
        return copy(at, at, gvsend.at[r], gvrecv.at[r], plane_dev(r)[1])

    @pl.when(z != owner)
    def _():
        vec_down(1).wait_recv()

    @pl.loop(1, nplane)
    def _(r):
        vec_out(r).start()

    @pl.loop(1, nz)
    def _(r):
        at = SQZ.at[z_at(-r)]
        copy(at, at, qzsend.at[r], qzrecv.at[r], sib).wait_recv()

    total = SQZ[0]
    for t in range(1, nz):
        total = total + SQZ[t]
    SQP[plane] = total

    @pl.loop(1, nplane)
    def _(r):
        sq_plane(r).start()

    def store(q):
        return pltpu.make_async_copy(GATH.at[q], gath_ref.at[q], store_sem.at[q])

    store(plane).start()
    ig_copy(0).wait_recv()
    ig_out = pltpu.make_async_copy(IG, ig_ref, load_sem.at[4])
    ig_out.start()

    for c in wcopies:
        c.wait_send()

    @pl.when(sx == 0)
    def _():
        hop_x().wait_send()

    ig_copy(0).wait_send()
    for t in range(2 * quarters):
        grad_copy(0, t).wait_send()
    vec_copy(0).wait_send()

    @pl.loop(1, nplane)
    def _(r):
        for c in range(len(chunks)):
            plane_copy(c, r).wait_send()
        plane_vec_copy(r).wait_send()

    for s in range(1, nz):
        z_copy(s).wait_send()
        share_copy(s).wait_send()

    @pl.when(z != owner)
    def _():
        vec_up().wait_send()

    @pl.when(z == owner)
    def _():
        @pl.loop(1, nz)
        def _(r):
            vec_down(r).wait_send()

    for t in range(3):
        sq_block(t).wait_send()

    @pl.loop(1, nz)
    def _(r):
        sq_z(r).wait_send()

    @pl.loop(1, nplane)
    def _(r):
        q = lax.rem(plane - r + nplane, nplane)
        for g, (lo, hi) in enumerate(groups):
            at = GATH.at[q, pl.ds(lo * zrows, (hi - lo) * zrows)]
            copy(at, at, gsend.at[g, r], grecv.at[g, r], sib).wait_recv()
        store(q).start()
        copy(GATHV.at[q], GATHV.at[q], gvsend.at[r], gvrecv.at[r], sib).wait_recv()
        copy(SQP.at[q], SQP.at[q], qpsend.at[r], qprecv.at[r], sib).wait_recv()

    gathv_ref[...] = GATHV[...]
    total = SQP[0]
    for t in range(1, nplane):
        total = total + SQP[t]
    factor = jnp.minimum(1.0, (params**0.5) * lax.rsqrt(total + 1e-06))
    fac_ref[...] = jnp.broadcast_to(factor, fac_ref.shape)

    @pl.loop(1, nplane)
    def _(r):
        for g in range(len(groups)):
            group_copy(g, r).wait_send()
        vec_out(r).wait_send()
        sq_plane(r).wait_send()

    @pl.loop(0, nplane)
    def _(q):
        store(q).wait()

    ig_out.wait()


def scale_kernel(nz, gath, gathv, fac, ig, o_in, o_out, o_vec, o_ig):
    nplane, part, chans = gath.shape
    hidden = o_in.shape[1]
    quarters = hidden // chans
    zrows = part // nz
    vlanes = gathv.shape[2]
    vcols = chans // vlanes
    z = lax.axis_index("z")
    f = fac[0:1, 0:1]
    per = chans // zrows
    for s in range(nz):
        q = lax.rem(z + offset(s) + nz, nz)
        for p in range(nplane):
            piece = gath[p, s * zrows : (s + 1) * zrows, :].astype(F32) * f
            first = p * part
            if first < hidden:
                if part <= chans:
                    at = pl.ds(pl.multiple_of(first % chans + q * zrows, zrows), zrows)
                    o_in[at, first // chans * chans : first // chans * chans + chans] = piece
                else:
                    for t in range(part // chans):
                        @pl.when(q // per == t)
                        def _():
                            at = pl.ds(pl.multiple_of(lax.rem(q, per) * zrows, zrows), zrows)
                            o_in[at, first + t * chans : first + t * chans + chans] = piece
            else:
                at = pl.ds(pl.multiple_of(first - hidden + q * zrows, zrows), zrows)
                o_out[at, :] = piece
    for p in range(nplane):
        at_row, at_col = (p // vcols) * VTILE, (p % vcols) * vlanes
        tile = gathv[p].astype(F32) * f
        for t in range(min(VTILE, o_vec.shape[0] - at_row)):
            o_vec[at_row + t, :, at_col : at_col + vlanes] = tile[t : t + 1, :]
    o_ig[...] = ig[...]


def per_device(dims, inputs, out_grad, w_in, w_out, vector_params):
    nz, ny, nx, params = dims
    nplane = ny * nx
    micros, _, height, width, chans = inputs.shape
    hidden = w_in.shape[2]
    vrows = vector_params.shape[1]
    pair = micros // 2
    rows = pair * height * width
    part = 2 * hidden // nplane
    zrows = part // nz
    vlanes = VPAD * chans // nplane // VTILE
    chunks, groups = spans(nz)
    maps = (micros, height, width, chans)
    small = (pair, height, width, chans)
    vm = pltpu.VMEM
    dma = pltpu.SemaphoreType.DMA
    in_vmem = pl.BlockSpec(memory_space=pltpu.VMEM)
    in_hbm = pl.BlockSpec(memory_space=pltpu.HBM)
    gath, gathv, fac, ig = pl.pallas_call(
        functools.partial(relay_kernel, dims),
        out_shape=(
            jax.ShapeDtypeStruct((nplane, part, chans), BF16),
            jax.ShapeDtypeStruct((nplane, VTILE, vlanes), BF16),
            jax.ShapeDtypeStruct((8, 128), F32),
            jax.ShapeDtypeStruct(maps, BF16),
        ),
        in_specs=[in_hbm] * 5,
        out_specs=(in_hbm, in_vmem, in_vmem, in_hbm),
        scratch_shapes=[
            vm((2, chans, hidden), BF16),
            vm((2, hidden, chans), BF16),
            vm((2, vrows, 1, chans), F32),
            vm((3,) + small, BF16),
            vm((3,) + small, BF16),
            vm((2, pair, height, width + 16, chans), F32),
            vm(small, F32),
            vm((2, rows, chans), F32),
            vm((2, rows, 128), F32),
            vm((2, rows, chans), BF16),
            vm((2, rows, hidden), BF16),
            vm((2, rows, hidden), F32),
            vm((2, rows, chans), F32),
            vm((2, 2 * hidden, chans), BF16),
            vm((2, VPAD, chans), F32),
            vm((2 * hidden, chans), BF16),
            vm((VPAD, chans), F32),
            vm(maps, BF16),
            vm((nplane, part, chans), BF16),
            vm((nplane, part, chans), BF16),
            vm((nplane, VTILE, vlanes), BF16),
            vm((nplane, VTILE, vlanes), BF16),
            vm((nz, zrows, chans), BF16),
            vm((nz, VTILE, vlanes), BF16),
            vm((nplane, part, chans), BF16),
            vm((nplane, VTILE, vlanes), BF16),
            vm((4, 1, 128), F32),
            vm((nz, 1, 128), F32),
            vm((nplane, 1, 128), F32),
            dma((5,)),
            dma((3,)), dma((3,)),
            dma, dma,
            dma, dma,
            dma((2 * hidden // chans,)), dma((2 * hidden // chans,)),
            dma, dma,
            dma((len(chunks), nplane)), dma((len(chunks), nplane)),
            dma((nplane,)), dma((nplane,)),
            dma((nz,)), dma((nz,)),
            dma, dma((nz,)),
            dma((nz,)), dma,
            dma((nz,)), dma((nz,)),
            dma((len(groups), nplane)), dma((len(groups), nplane)),
            dma((nplane,)), dma((nplane,)),
            dma((3,)), dma((3,)),
            dma((nz,)), dma((nz,)),
            dma((nplane,)), dma((nplane,)),
            dma((nplane,)),
            pltpu.SemaphoreType.REGULAR((3,)),
        ],
        compiler_params=pltpu.CompilerParams(
            collective_id=0, has_side_effects=True, vmem_limit_bytes=60 * 1024 * 1024
        ),
        name="relay",
    )(
        inputs.reshape(maps), out_grad.reshape(maps), w_in[0], w_out[0],
        jnp.swapaxes(vector_params, 0, 1),
    )
    o_in, o_out, o_vec, o_ig = pl.pallas_call(
        functools.partial(scale_kernel, nz),
        out_shape=(
            jax.ShapeDtypeStruct((chans, hidden), F32),
            jax.ShapeDtypeStruct((hidden, chans), F32),
            jax.ShapeDtypeStruct((vrows, 1, chans), F32),
            jax.ShapeDtypeStruct(maps, BF16),
        ),
        in_specs=[in_vmem] * 4,
        out_specs=(in_vmem,) * 4,
        compiler_params=pltpu.CompilerParams(vmem_limit_bytes=60 * 1024 * 1024),
        name="scale",
    )(gath, gathv, fac, ig)
    return (
        o_ig.reshape((1, micros, 1, height, width, chans)),
        o_in[None],
        o_out[None],
        jnp.swapaxes(o_vec, 0, 1),
    )


def solution(mesh):
    nx = 2
    ny = 4
    nz = mesh.shape["dp"] // (nx * ny)
    return program_on(mesh, nz, ny, nx)


def program_on(mesh, nz, ny, nx, params=2156544):
    split = Mesh(mesh.devices.reshape(2, 2, nz, ny, nx), ("sx", "core", "z", "y", "xl"))
    dp = ("z", "y", "xl")
    seg = ("sx", "core")
    in_specs = (
        P(None, dp, None, None, None),
        P(None, dp, None, None, None),
        P(seg, None, None),
        P(seg, None, None),
        P(seg, None, None),
    )
    out_specs = (
        P(seg, None, dp, None, None, None),
        P(seg, None, None),
        P(seg, None, None),
        P(seg, None, None),
    )
    return jax.shard_map(
        functools.partial(per_device, (nz, ny, nx, params)),
        mesh=split, in_specs=in_specs, out_specs=out_specs, check_vma=False,
    )
```

```python
import functools

import jax
import jax.numpy as jnp
from jax import lax
from jax.experimental import pallas as pl
from jax.experimental.pallas import tpu as pltpu
from jax.sharding import Mesh
from jax.sharding import PartitionSpec as P

F32 = jnp.float32
BF16 = jnp.bfloat16
VTILE = 16
VPAD = 64


def dot(a, b):
    return jnp.dot(a, b, preferred_element_type=F32)


def dot_nt(a, b):
    return lax.dot_general(a, b, (((1,), (1,)), ((), ())), preferred_element_type=F32)


def dot_tn(a, b):
    return lax.dot_general(a, b, (((0,), (0,)), ((), ())), preferred_element_type=F32)


def over_rows(a):
    return jnp.sum(a, axis=0, keepdims=True)


def spans(nz):
    if nz == 16:
        return ((13, 16), (10, 13), (7, 10), (4, 7), (0, 4)), ((0, 1), (1, 5), (5, 9), (9, 13), (13, 16))
    return ((1, nz), (0, 1)), ((0, 1), (1, nz))


def offset(s):
    return (s + 1) // 2 if s % 2 else -(s // 2)


def mirror(s, nz):
    if s == 0 or s == nz - 1:
        return s
    return s + 1 if s % 2 else s - 1


def relay_kernel(
    dims, x_ref, g_ref, win_ref, wout_ref, vec_ref, gath_ref, gathv_ref, fac_ref, ig_ref,
    win, wout, vec, X, G, xpad, cv, XH, RSTD, NB, ACT, SL, PJ,
    PG, GV, RG, RV, IG, S, RB, SV, RBV, ZB, VZ, GATH, GATHV, SQS, SQZ, SQP,
    load_sem, wsend, wrecv, hsend, hrecv, isend, irecv, csend, crecv, cvsend, cvrecv,
    psend, precv, pvsend, pvrecv, zsend, zrecv, vsend, vrecv, bsend, brecv, asend, arecv,
    gsend, grecv, gvsend, gvrecv, qsend, qrecv, qzsend, qzrecv, qpsend, qprecv, store_sem, known_sem,
):
    nz, ny, nx, params = dims
    nplane = ny * nx
    core = lax.axis_index("core")
    sx = lax.axis_index("sx")
    z = lax.axis_index("z")
    y = lax.axis_index("y")
    xl = lax.axis_index("xl")
    plane = y * nx + xl
    pair, height, width, chans = X.shape[1:]
    rows = pair * height * width
    hidden = win.shape[2]
    quarters = hidden // chans
    part = 2 * hidden // nplane
    zrows = part // nz
    vlanes = SV.shape[2]
    vcols = chans // vlanes
    owner = lax.rem(2 * plane + core, nz)
    chunks, groups = spans(nz)

    def copy(src, dst, ss, rs, dev):
        return pltpu.make_async_remote_copy(
            src_ref=src, dst_ref=dst, send_sem=ss, recv_sem=rs,
            device_id=dev, device_id_type=pl.DeviceIdType.MESH,
        )

    sib = {"core": 1 - core}
    far = {"sx": 1 - sx}
    diag = {"core": 1 - core, "sx": 1 - sx}

    def plane_dev(r):
        q = lax.rem(plane + r, nplane)
        return q, {"y": q // nx, "xl": lax.rem(q, nx)}

    def z_at(by):
        return lax.rem(z + by + nz, nz)

    loads = [
        pltpu.make_async_copy(vec_ref, vec.at[core], load_sem.at[0]),
        pltpu.make_async_copy(win_ref, win.at[core], load_sem.at[1]),
        pltpu.make_async_copy(wout_ref, wout.at[core], load_sem.at[2]),
    ]
    for c in loads:
        c.start()
    my_micros = pl.ds(core * pair, pair)

    def load_x():
        return pltpu.make_async_copy(x_ref.at[my_micros], X.at[0], load_sem.at[3])

    def load_g():
        return pltpu.make_async_copy(g_ref.at[my_micros], G.at[2], load_sem.at[3])

    @pl.when(sx == 0)
    def _():
        load_x().start()

    @pl.when(sx == 1)
    def _():
        load_g().start()

    barrier = pltpu.get_barrier_semaphore()

    def hello(dev):
        pl.semaphore_signal(barrier, inc=1, device_id=dev, device_id_type=pl.DeviceIdType.MESH)

    hello({"z": z_at(1)})
    hello({"z": z_at(-1)})

    @pl.loop(1, nplane)
    def _(r):
        hello(plane_dev(r)[1])

    hello(diag)
    hello(far)
    hello(sib)

    zero_side = jnp.zeros((pair, height, 8, chans), F32)
    for k in range(2):
        xpad[k, :, :, 0:8, :] = zero_side
        xpad[k, :, :, 8 + width : 16 + width, :] = zero_side
    GV[...] = jnp.zeros(GV.shape, F32)

    @pl.when(sx == 0)
    def _():
        load_x().wait()

    @pl.when(sx == 1)
    def _():
        load_g().wait()

    pl.semaphore_wait(barrier, 3 + (nplane - 1) + 2)

    wcopies = [
        copy(vec_ref, vec.at[core], wsend.at[0], wrecv.at[0], sib),
        copy(win_ref, win.at[core], wsend.at[1], wrecv.at[1], sib),
        copy(wout_ref, wout.at[core], wsend.at[2], wrecv.at[2], sib),
    ]
    for c in wcopies:
        c.start()

    reaches = [1 << t for t in range(8) if (1 << t) < nz // 2]

    def tell(t):
        for by in (reaches[t], -reaches[t]):
            pl.semaphore_signal(
                known_sem.at[t], inc=1, device_id={"z": z_at(by)},
                device_id_type=pl.DeviceIdType.MESH,
            )

    def heard(t):
        pl.semaphore_wait(known_sem.at[t], 2)

    if reaches:
        tell(0)

    def hop_x():
        return copy(X.at[2], X.at[0], hsend, hrecv, far)

    def hop_g():
        return copy(G.at[0], G.at[2], hsend, hrecv, far)

    @pl.when(sx == 1)
    def _():
        hop_x().wait_recv()

    def row(k, t):
        return vec[k, t]

    def forward(k, carry):
        def ready(t):
            @pl.when(core == k)
            def _():
                loads[t].wait()

            @pl.when(core != k)
            def _():
                wcopies[t].wait_recv()

        xpad[k, :, :, 8 : 8 + width, :] = X[k].astype(F32)
        ready(0)
        for half in range(chans // 128):
            lanes = slice(half * 128, half * 128 + 128)
            acc = [None] * height
            for j in range(7):
                shifted = [xpad[k, :, h, 5 + j : 5 + j + width, lanes] for h in range(height)]
                for i in range(7):
                    tap = vec[k, 7 * i + j, :, lanes][None]
                    for h in range(height):
                        if 0 <= h + i - 3 < height:
                            term = shifted[h + i - 3] * tap
                            acc[h] = term if acc[h] is None else acc[h] + term
            bias = vec[k, 49, :, lanes][None]
            for h in range(height):
                cv[:, h, :, lanes] = acc[h] + bias
        conv = cv[...].reshape(rows, chans)
        mean = jnp.sum(conv, axis=1, keepdims=True) * (1.0 / chans)
        centered = conv - mean
        var = jnp.sum(centered * centered, axis=1, keepdims=True) * (1.0 / chans)
        rstd = lax.rsqrt(var + 1e-06)
        xhat = centered * rstd
        XH[k] = xhat
        RSTD[k] = jnp.broadcast_to(rstd, (rows, 128))
        normed = (xhat * row(k, 50) + row(k, 51)).astype(BF16)
        NB[k] = normed
        ready(1)
        ready(2)
        proj = jnp.zeros((rows, chans), F32)
        for q in range(quarters):
            cols = slice(q * chans, (q + 1) * chans)
            pre = dot(normed, win[k, :, cols]) + row(k, 54 + q)
            cumulative = 0.5 * (1.0 + lax.erf(pre * 0.7071067811865476))
            act = (pre * cumulative).astype(BF16)
            ACT[k, :, cols] = act
            SL[k, :, cols] = cumulative + pre * jnp.exp(-0.5 * pre * pre) * 0.3989422804014327
            proj = proj + dot(act, wout[k, cols, :])
        proj = proj + row(k, 52)
        PJ[k] = proj
        out = X[k].astype(F32).reshape(rows, chans) + row(k, 53) * proj
        X[k + 1] = out.astype(BF16).reshape(pair, height, width, chans)
        return carry

    lax.fori_loop(0, 2, forward, 0)
    if len(reaches) > 1:
        heard(0)
        tell(1)

    @pl.when(sx == 0)
    def _():
        hop_x().start()
        hop_g().wait_recv()

    def grad_copy(k, t):
        at = pl.ds(t * chans, chans)
        return copy(PG.at[k, at], RG.at[at], csend.at[t], crecv.at[t], sib)

    def vec_copy(k):
        return copy(GV.at[k], RV, cvsend, cvrecv, sib)

    def ig_copy(k):
        return copy(G.at[k], IG.at[my_micros], isend, irecv, sib)

    def plane_copy(c, r):
        lo, hi = chunks[c]
        q, dev = plane_dev(r)
        at = pl.ds(lo * zrows, (hi - lo) * zrows)
        return copy(S.at[q, at], RB.at[r, at], psend.at[c, r], precv.at[c, r], dev)

    def plane_vec_copy(r):
        q, dev = plane_dev(r)
        return copy(SV.at[q], RBV.at[r], pvsend.at[r], pvrecv.at[r], dev)

    every = range(len(chunks))
    early, late = every[:2], every[2:]

    def chip_sum(k, some):
        if 0 in some:
            for t in range(2 * quarters):
                grad_copy(k, t).wait_recv()
        for c in some:
            lo, hi = chunks[c]

            @pl.loop(1, nplane + 1)
            def _(r):
                p = lax.rem(plane + r, nplane)
                for s in range(lo, hi):
                    start = p * part + z_at(offset(s)) * zrows
                    at = pl.ds(pl.multiple_of(start, zrows), zrows)
                    S[p, s * zrows : (s + 1) * zrows, :] = (
                        PG[k, at, :].astype(F32) + RG[at, :].astype(F32)
                    ).astype(BF16)

                @pl.when(r < nplane)
                def _():
                    plane_copy(c, r).start()

    def chip_vec_sum(k):
        vec_copy(k).wait_recv()
        for t in range(nplane):
            at_row, at_col = (t // vcols) * VTILE, (t % vcols) * vlanes
            tile = (slice(at_row, at_row + VTILE), slice(at_col, at_col + vlanes))
            SV[t] = (GV[(k,) + tile] + RV[tile]).astype(BF16)

        @pl.loop(1, nplane)
        def _(r):
            plane_vec_copy(r).start()

    def backward(step, carry):
        k = 1 - step

        if len(reaches) > 2:

            @pl.when(step == 1)
            def _():
                heard(1)
                tell(2)

        @pl.when((sx == 0) & (core == 1) & (k == 0))
        def _():
            chip_sum(1, every)

        gf = G[k + 1].astype(F32).reshape(rows, chans)
        GV[k, 53:54, :] = over_rows(gf * PJ[k])
        dproj = gf * row(k, 53)
        GV[k, 52:53, :] = over_rows(dproj)
        dproj_b = dproj.astype(BF16)
        normed = NB[k]
        dn = jnp.zeros((rows, chans), F32)
        for q in range(quarters):
            cols = slice(q * chans, (q + 1) * chans)
            dact = dot_nt(dproj_b, wout[k, cols, :])
            PG[k, hidden + q * chans : hidden + (q + 1) * chans, :] = dot_tn(
                ACT[k, :, cols], dproj_b
            ).astype(BF16)
            dpre = dact * SL[k, :, cols]
            GV[k, 54 + q : 55 + q, :] = over_rows(dpre)
            dpre_b = dpre.astype(BF16)
            PG[k, cols, :] = dot_tn(normed, dpre_b).astype(BF16)

            @pl.when(core != k)
            def _():
                grad_copy(k, quarters + q).start()
                grad_copy(k, q).start()

            dn = dn + dot_nt(dpre_b, win[k, :, cols])

        xhat = XH[k]
        GV[k, 50:51, :] = over_rows(dn * xhat)
        GV[k, 51:52, :] = over_rows(dn)
        dxh = dn * row(k, 50)
        m1 = jnp.sum(dxh, axis=1, keepdims=True) * (1.0 / chans)
        m2 = jnp.sum(dxh * xhat, axis=1, keepdims=True) * (1.0 / chans)
        rstd = RSTD[k][:, 0:1]
        dconv = (dxh - m1 - xhat * m2) * rstd
        GV[k, 49:50, :] = over_rows(dconv)
        xpad[k, :, :, 8 : 8 + width, :] = dconv.reshape(pair, height, width, chans)
        for half in range(chans // 128):
            lanes = slice(half * 128, half * 128 + 128)
            acc = [G[k + 1, :, h, :, lanes].astype(F32) for h in range(height)]
            for j in range(7):
                shifted = [xpad[k, :, h, 11 - j : 11 - j + width, lanes] for h in range(height)]
                for i in range(7):
                    tap = vec[k, 7 * i + j, :, lanes][None]
                    for h in range(height):
                        if 0 <= h - i + 3 < height:
                            acc[h] = acc[h] + shifted[h - i + 3] * tap
            for h in range(height):
                G[k, :, h, :, lanes] = acc[h].astype(BF16)

        @pl.when(core != k)
        def _():
            ig_copy(k).start()

        @pl.when(core == k)
        def _():
            IG[my_micros] = G[k]

        return carry

    def tap_grads(step, carry):
        k = 1 - step
        for half in range(chans // 128):
            lanes = slice(half * 128, half * 128 + 128)
            xs = [X[k, :, h, :, lanes].astype(F32) for h in range(height)]
            for j in range(7):
                shifted = [xpad[k, :, h, 11 - j : 11 - j + width, lanes] for h in range(height)]
                for i in range(7):
                    t = 7 * i + j
                    total = None
                    for h in range(height):
                        if 0 <= h - i + 3 < height:
                            term = xs[h] * shifted[h - i + 3]
                            total = term if total is None else total + term
                    GV[k, t : t + 1, lanes] = over_rows(total.reshape(pair * width, 128))

        @pl.when(core != k)
        def _():
            vec_copy(k).start()

        return carry

    lax.fori_loop(0, 2, backward, 0)

    @pl.when(sx == 1)
    def _():
        hop_g().start()

    lax.fori_loop(0, 2, tap_grads, 0)

    @pl.when(sx == 1)
    def _():
        hop_g().wait_send()

    @pl.when((core == 0) | (sx == 1))
    def _():
        chip_sum(core, early)

    chip_vec_sum(core)

    @pl.when((core == 0) | (sx == 1))
    def _():
        chip_sum(core, late)

    def z_copy(s):
        src = S.at[plane, pl.ds(s * zrows, zrows)]
        return copy(src, ZB.at[s], zsend.at[s], zrecv.at[s], {"z": z_at(offset(s))})

    if reaches:
        heard(len(reaches) - 1)

    def vec_up():
        r = lax.rem(owner - z + nz, nz)
        return copy(RBV.at[0], VZ.at[r], vsend, vrecv.at[r], {"z": owner})

    def vec_share():
        @pl.loop(1, nplane)
        def _(r):
            plane_vec_copy(r).wait_recv()

        vacc = SV[plane].astype(F32)
        for r in range(1, nplane):
            vacc = vacc + RBV[r].astype(F32)
        RBV[0] = vacc.astype(BF16)

        @pl.when(z != owner)
        def _():
            vec_up().start()

    for c, (lo, hi) in enumerate(chunks):
        if c == min(2, len(chunks) - 1):
            vec_share()

        @pl.loop(1, nplane)
        def _(r):
            plane_copy(c, r).wait_recv()

        for s in reversed(range(lo, hi)):
            at = slice(s * zrows, (s + 1) * zrows)
            acc = S[plane, at, :].astype(F32)
            for t in range(1, nplane):
                acc = acc + RB[t, at, :].astype(F32)
            if s > 0:
                S[plane, at, :] = acc.astype(BF16)
                z_copy(s).start()
            else:
                ZB[0] = acc.astype(BF16)

    def share_copy(s):
        return copy(
            GATH.at[plane, pl.ds(0, zrows)],
            GATH.at[plane, pl.ds(mirror(s, nz) * zrows, zrows)],
            asend.at[s], arecv.at[mirror(s, nz)], {"z": z_at(offset(s))},
        )

    def group_copy(g, r):
        lo, hi = groups[g]
        at = pl.ds(lo * zrows, (hi - lo) * zrows)
        return copy(
            GATH.at[plane, at], GATH.at[plane, at], gsend.at[g, r], grecv.at[g, r],
            plane_dev(r)[1],
        )

    for s in range(1, nz):
        z_copy(s).wait_recv()
    share = ZB[0].astype(F32)
    for s in range(1, nz):
        share = share + ZB[s].astype(F32)
    GATH[plane, 0:zrows, :] = share.astype(BF16)
    for s in [*range(1, min(5, nz)), *reversed(range(5, nz))]:
        share_copy(s).start()

    @pl.loop(1, nplane)
    def _(r):
        group_copy(0, r).start()

    SQS[2 * sx + core] = jnp.broadcast_to(jnp.sum(share * share), (1, 128))

    def vec_down(r):
        return copy(
            GATHV.at[plane], GATHV.at[plane], bsend.at[r], brecv, {"z": z_at(r)}
        )

    @pl.when(z == owner)
    def _():
        @pl.loop(1, nz)
        def _(r):
            copy(VZ.at[r], VZ.at[r], vsend, vrecv.at[r], {"z": owner}).wait_recv()

        total = RBV[0].astype(F32)
        for r in range(1, nz):
            total = total + VZ[r].astype(F32)
        GATHV[plane] = total.astype(BF16)

        @pl.loop(1, nz)
        def _(r):
            vec_down(r).start()

        SQS[2 * sx + core] = SQS[2 * sx + core] + jnp.broadcast_to(
            jnp.sum(total * total), (1, 128)
        )

    def sq_block(t):
        at = SQS.at[2 * sx + core]
        return copy(at, at, qsend.at[t], qrecv.at[t], (sib, far, diag)[t])

    def sq_z(r):
        at = SQZ.at[z]
        return copy(at, at, qzsend.at[r], qzrecv.at[r], {"z": z_at(r)})

    def sq_plane(r):
        at = SQP.at[plane]
        return copy(at, at, qpsend.at[r], qprecv.at[r], plane_dev(r)[1])

    for t in range(3):
        sq_block(t).start()

    def forward_group(g):
        lo, hi = groups[g]
        for s in range(lo, hi):
            at = GATH.at[plane, pl.ds(s * zrows, zrows)]
            copy(at, at, asend.at[s], arecv.at[s], sib).wait_recv()

        @pl.loop(1, nplane)
        def _(r):
            group_copy(g, r).start()

    forward_group(1)
    mates = (2 * sx + 1 - core, 2 * (1 - sx) + core, 2 * (1 - sx) + 1 - core)
    for t in range(3):
        at = SQS.at[mates[t]]
        copy(at, at, qsend.at[t], qrecv.at[t], sib).wait_recv()
    SQZ[z] = (SQS[0] + SQS[1]) + (SQS[2] + SQS[3])

    @pl.loop(1, nz)
    def _(r):
        sq_z(r).start()

    for g in range(2, len(groups)):
        forward_group(g)

    def vec_out(r):
        at = GATHV.at[plane]
        return copy(at, at, gvsend.at[r], gvrecv.at[r], plane_dev(r)[1])

    @pl.when(z != owner)
    def _():
        vec_down(1).wait_recv()

    @pl.loop(1, nplane)
    def _(r):
        vec_out(r).start()

    @pl.loop(1, nz)
    def _(r):
        at = SQZ.at[z_at(-r)]
        copy(at, at, qzsend.at[r], qzrecv.at[r], sib).wait_recv()

    total = SQZ[0]
    for t in range(1, nz):
        total = total + SQZ[t]
    SQP[plane] = total

    @pl.loop(1, nplane)
    def _(r):
        sq_plane(r).start()

    def store(q):
        return pltpu.make_async_copy(GATH.at[q], gath_ref.at[q], store_sem.at[q])

    store(plane).start()
    ig_copy(0).wait_recv()
    ig_out = pltpu.make_async_copy(IG, ig_ref, load_sem.at[4])
    ig_out.start()

    for c in wcopies:
        c.wait_send()

    @pl.when(sx == 0)
    def _():
        hop_x().wait_send()

    ig_copy(0).wait_send()
    for t in range(2 * quarters):
        grad_copy(0, t).wait_send()
    vec_copy(0).wait_send()

    @pl.loop(1, nplane)
    def _(r):
        for c in range(len(chunks)):
            plane_copy(c, r).wait_send()
        plane_vec_copy(r).wait_send()

    for s in range(1, nz):
        z_copy(s).wait_send()
        share_copy(s).wait_send()

    @pl.when(z != owner)
    def _():
        vec_up().wait_send()

    @pl.when(z == owner)
    def _():
        @pl.loop(1, nz)
        def _(r):
            vec_down(r).wait_send()

    for t in range(3):
        sq_block(t).wait_send()

    @pl.loop(1, nz)
    def _(r):
        sq_z(r).wait_send()

    @pl.loop(1, nplane)
    def _(r):
        q = lax.rem(plane - r + nplane, nplane)
        for g, (lo, hi) in enumerate(groups):
            at = GATH.at[q, pl.ds(lo * zrows, (hi - lo) * zrows)]
            copy(at, at, gsend.at[g, r], grecv.at[g, r], sib).wait_recv()
        store(q).start()
        copy(GATHV.at[q], GATHV.at[q], gvsend.at[r], gvrecv.at[r], sib).wait_recv()
        copy(SQP.at[q], SQP.at[q], qpsend.at[r], qprecv.at[r], sib).wait_recv()

    gathv_ref[...] = GATHV[...]
    total = SQP[0]
    for t in range(1, nplane):
        total = total + SQP[t]
    factor = jnp.minimum(1.0, (params**0.5) * lax.rsqrt(total + 1e-06))
    fac_ref[...] = jnp.broadcast_to(factor, fac_ref.shape)

    @pl.loop(1, nplane)
    def _(r):
        for g in range(len(groups)):
            group_copy(g, r).wait_send()
        vec_out(r).wait_send()
        sq_plane(r).wait_send()

    @pl.loop(0, nplane)
    def _(q):
        store(q).wait()

    ig_out.wait()


def scale_kernel(nz, gath, gathv, fac, ig, o_in, o_out, o_vec, o_ig):
    nplane, part, chans = gath.shape
    hidden = o_in.shape[1]
    quarters = hidden // chans
    zrows = part // nz
    vlanes = gathv.shape[2]
    vcols = chans // vlanes
    z = lax.axis_index("z")
    f = fac[0:1, 0:1]
    per = chans // zrows
    for s in range(nz):
        q = lax.rem(z + offset(s) + nz, nz)
        for p in range(nplane):
            piece = gath[p, s * zrows : (s + 1) * zrows, :].astype(F32) * f
            first = p * part
            if first < hidden:
                if part <= chans:
                    at = pl.ds(pl.multiple_of(first % chans + q * zrows, zrows), zrows)
                    o_in[at, first // chans * chans : first // chans * chans + chans] = piece
                else:
                    for t in range(part // chans):
                        @pl.when(q // per == t)
                        def _():
                            at = pl.ds(pl.multiple_of(lax.rem(q, per) * zrows, zrows), zrows)
                            o_in[at, first + t * chans : first + t * chans + chans] = piece
            else:
                at = pl.ds(pl.multiple_of(first - hidden + q * zrows, zrows), zrows)
                o_out[at, :] = piece
    for p in range(nplane):
        at_row, at_col = (p // vcols) * VTILE, (p % vcols) * vlanes
        tile = gathv[p].astype(F32) * f
        for t in range(min(VTILE, o_vec.shape[0] - at_row)):
            o_vec[at_row + t, :, at_col : at_col + vlanes] = tile[t : t + 1, :]
    o_ig[...] = ig[...]


def per_device(dims, inputs, out_grad, w_in, w_out, vector_params):
    nz, ny, nx, params = dims
    nplane = ny * nx
    micros, _, height, width, chans = inputs.shape
    hidden = w_in.shape[2]
    vrows = vector_params.shape[1]
    pair = micros // 2
    rows = pair * height * width
    part = 2 * hidden // nplane
    zrows = part // nz
    vlanes = VPAD * chans // nplane // VTILE
    chunks, groups = spans(nz)
    maps = (micros, height, width, chans)
    small = (pair, height, width, chans)
    vm = pltpu.VMEM
    dma = pltpu.SemaphoreType.DMA
    in_vmem = pl.BlockSpec(memory_space=pltpu.VMEM)
    in_hbm = pl.BlockSpec(memory_space=pltpu.HBM)
    gath, gathv, fac, ig = pl.pallas_call(
        functools.partial(relay_kernel, dims),
        out_shape=(
            jax.ShapeDtypeStruct((nplane, part, chans), BF16),
            jax.ShapeDtypeStruct((nplane, VTILE, vlanes), BF16),
            jax.ShapeDtypeStruct((8, 128), F32),
            jax.ShapeDtypeStruct(maps, BF16),
        ),
        in_specs=[in_hbm] * 5,
        out_specs=(in_hbm, in_vmem, in_vmem, in_hbm),
        scratch_shapes=[
            vm((2, chans, hidden), BF16),
            vm((2, hidden, chans), BF16),
            vm((2, vrows, 1, chans), F32),
            vm((3,) + small, BF16),
            vm((3,) + small, BF16),
            vm((2, pair, height, width + 16, chans), F32),
            vm(small, F32),
            vm((2, rows, chans), F32),
            vm((2, rows, 128), F32),
            vm((2, rows, chans), BF16),
            vm((2, rows, hidden), BF16),
            vm((2, rows, hidden), F32),
            vm((2, rows, chans), F32),
            vm((2, 2 * hidden, chans), BF16),
            vm((2, VPAD, chans), F32),
            vm((2 * hidden, chans), BF16),
            vm((VPAD, chans), F32),
            vm(maps, BF16),
            vm((nplane, part, chans), BF16),
            vm((nplane, part, chans), BF16),
            vm((nplane, VTILE, vlanes), BF16),
            vm((nplane, VTILE, vlanes), BF16),
            vm((nz, zrows, chans), BF16),
            vm((nz, VTILE, vlanes), BF16),
            vm((nplane, part, chans), BF16),
            vm((nplane, VTILE, vlanes), BF16),
            vm((4, 1, 128), F32),
            vm((nz, 1, 128), F32),
            vm((nplane, 1, 128), F32),
            dma((5,)),
            dma((3,)), dma((3,)),
            dma, dma,
            dma, dma,
            dma((2 * hidden // chans,)), dma((2 * hidden // chans,)),
            dma, dma,
            dma((len(chunks), nplane)), dma((len(chunks), nplane)),
            dma((nplane,)), dma((nplane,)),
            dma((nz,)), dma((nz,)),
            dma, dma((nz,)),
            dma((nz,)), dma,
            dma((nz,)), dma((nz,)),
            dma((len(groups), nplane)), dma((len(groups), nplane)),
            dma((nplane,)), dma((nplane,)),
            dma((3,)), dma((3,)),
            dma((nz,)), dma((nz,)),
            dma((nplane,)), dma((nplane,)),
            dma((nplane,)),
            pltpu.SemaphoreType.REGULAR((3,)),
        ],
        compiler_params=pltpu.CompilerParams(
            collective_id=0, has_side_effects=True, vmem_limit_bytes=60 * 1024 * 1024
        ),
        name="relay",
    )(
        inputs.reshape(maps), out_grad.reshape(maps), w_in[0], w_out[0],
        jnp.swapaxes(vector_params, 0, 1),
    )
    o_in, o_out, o_vec, o_ig = pl.pallas_call(
        functools.partial(scale_kernel, nz),
        out_shape=(
            jax.ShapeDtypeStruct((chans, hidden), F32),
            jax.ShapeDtypeStruct((hidden, chans), F32),
            jax.ShapeDtypeStruct((vrows, 1, chans), F32),
            jax.ShapeDtypeStruct(maps, BF16),
        ),
        in_specs=[in_vmem] * 4,
        out_specs=(in_vmem,) * 4,
        compiler_params=pltpu.CompilerParams(vmem_limit_bytes=60 * 1024 * 1024),
        name="scale",
    )(gath, gathv, fac, ig)
    return (
        o_ig.reshape((1, micros, 1, height, width, chans)),
        o_in[None],
        o_out[None],
        jnp.swapaxes(o_vec, 0, 1),
    )


def solution(mesh):
    nx = 2
    ny = 4
    nz = mesh.shape["dp"] // (nx * ny)
    return program_on(mesh, nz, ny, nx)


def program_on(mesh, nz, ny, nx, params=2156544):
    split = Mesh(mesh.devices.reshape(2, 2, nz, ny, nx), ("sx", "core", "z", "y", "xl"))
    dp = ("z", "y", "xl")
    seg = ("sx", "core")
    in_specs = (
        P(None, dp, None, None, None),
        P(None, dp, None, None, None),
        P(seg, None, None),
        P(seg, None, None),
        P(seg, None, None),
    )
    out_specs = (
        P(seg, None, dp, None, None, None),
        P(seg, None, None),
        P(seg, None, None),
        P(seg, None, None),
    )
    return jax.shard_map(
        functools.partial(per_device, (nz, ny, nx, params)),
        mesh=split, in_specs=in_specs, out_specs=out_specs, check_vma=False,
    )
```

```python
import functools

import jax
import jax.numpy as jnp
from jax import lax
from jax.experimental import pallas as pl
from jax.experimental.pallas import tpu as pltpu
from jax.sharding import Mesh
from jax.sharding import PartitionSpec as P

F32 = jnp.float32
BF16 = jnp.bfloat16
VTILE = 16
VPAD = 64


def dot(a, b):
    return jnp.dot(a, b, preferred_element_type=F32)


def dot_nt(a, b):
    return lax.dot_general(a, b, (((1,), (1,)), ((), ())), preferred_element_type=F32)


def dot_tn(a, b):
    return lax.dot_general(a, b, (((0,), (0,)), ((), ())), preferred_element_type=F32)


def over_rows(a):
    return jnp.sum(a, axis=0, keepdims=True)


def spans(nz):
    if nz == 16:
        return ((13, 16), (10, 13), (7, 10), (4, 7), (2, 4), (0, 2)), ((0, 1), (1, 5), (5, 9), (9, 13), (13, 16))
    return ((1, nz), (0, 1)), ((0, 1), (1, nz))


def offset(s):
    return (s + 1) // 2 if s % 2 else -(s // 2)


def mirror(s, nz):
    if s == 0 or s == nz - 1:
        return s
    return s + 1 if s % 2 else s - 1


def relay_kernel(
    dims, x_ref, g_ref, win_ref, wout_ref, vec_ref, gath_ref, gathv_ref, fac_ref, ig_ref,
    win, wout, vec, X, G, xpad, cv, XH, RSTD, NB, ACT, SL, PJ,
    PG, GV, RG, RV, IG, S, RB, SV, RBV, ZB, VZ, GATH, GATHV, SQS, SQZ, SQP,
    load_sem, wsend, wrecv, hsend, hrecv, isend, irecv, csend, crecv, cvsend, cvrecv,
    psend, precv, pvsend, pvrecv, zsend, zrecv, vsend, vrecv, bsend, brecv, asend, arecv,
    gsend, grecv, gvsend, gvrecv, qsend, qrecv, qzsend, qzrecv, qpsend, qprecv, store_sem, known_sem,
):
    nz, ny, nx, params = dims
    nplane = ny * nx
    core = lax.axis_index("core")
    sx = lax.axis_index("sx")
    z = lax.axis_index("z")
    y = lax.axis_index("y")
    xl = lax.axis_index("xl")
    plane = y * nx + xl
    pair, height, width, chans = X.shape[1:]
    rows = pair * height * width
    hidden = win.shape[2]
    quarters = hidden // chans
    part = 2 * hidden // nplane
    zrows = part // nz
    vlanes = SV.shape[2]
    vcols = chans // vlanes
    owner = lax.rem(2 * plane + core, nz)
    chunks, groups = spans(nz)

    def copy(src, dst, ss, rs, dev):
        return pltpu.make_async_remote_copy(
            src_ref=src, dst_ref=dst, send_sem=ss, recv_sem=rs,
            device_id=dev, device_id_type=pl.DeviceIdType.MESH,
        )

    sib = {"core": 1 - core}
    far = {"sx": 1 - sx}
    diag = {"core": 1 - core, "sx": 1 - sx}

    def plane_dev(r):
        q = lax.rem(plane + r, nplane)
        return q, {"y": q // nx, "xl": lax.rem(q, nx)}

    def z_at(by):
        return lax.rem(z + by + nz, nz)

    loads = [
        pltpu.make_async_copy(vec_ref, vec.at[core], load_sem.at[0]),
        pltpu.make_async_copy(win_ref, win.at[core], load_sem.at[1]),
        pltpu.make_async_copy(wout_ref, wout.at[core], load_sem.at[2]),
    ]
    for c in loads:
        c.start()
    my_micros = pl.ds(core * pair, pair)

    def load_x():
        return pltpu.make_async_copy(x_ref.at[my_micros], X.at[0], load_sem.at[3])

    def load_g():
        return pltpu.make_async_copy(g_ref.at[my_micros], G.at[2], load_sem.at[3])

    @pl.when(sx == 0)
    def _():
        load_x().start()

    @pl.when(sx == 1)
    def _():
        load_g().start()

    barrier = pltpu.get_barrier_semaphore()

    def hello(dev):
        pl.semaphore_signal(barrier, inc=1, device_id=dev, device_id_type=pl.DeviceIdType.MESH)

    hello({"z": z_at(1)})
    hello({"z": z_at(-1)})

    @pl.loop(1, nplane)
    def _(r):
        hello(plane_dev(r)[1])

    hello(diag)
    hello(far)
    hello(sib)

    zero_side = jnp.zeros((pair, height, 8, chans), F32)
    for k in range(2):
        xpad[k, :, :, 0:8, :] = zero_side
        xpad[k, :, :, 8 + width : 16 + width, :] = zero_side
    GV[...] = jnp.zeros(GV.shape, F32)

    @pl.when(sx == 0)
    def _():
        load_x().wait()

    @pl.when(sx == 1)
    def _():
        load_g().wait()

    pl.semaphore_wait(barrier, 3 + (nplane - 1) + 2)

    wcopies = [
        copy(vec_ref, vec.at[core], wsend.at[0], wrecv.at[0], sib),
        copy(win_ref, win.at[core], wsend.at[1], wrecv.at[1], sib),
        copy(wout_ref, wout.at[core], wsend.at[2], wrecv.at[2], sib),
    ]
    for c in wcopies:
        c.start()

    reaches = [1 << t for t in range(8) if (1 << t) < nz // 2]

    def tell(t):
        for by in (reaches[t], -reaches[t]):
            pl.semaphore_signal(
                known_sem.at[t], inc=1, device_id={"z": z_at(by)},
                device_id_type=pl.DeviceIdType.MESH,
            )

    def heard(t):
        pl.semaphore_wait(known_sem.at[t], 2)

    if reaches:
        tell(0)

    def hop_x():
        return copy(X.at[2], X.at[0], hsend, hrecv, far)

    def hop_g():
        return copy(G.at[0], G.at[2], hsend, hrecv, far)

    @pl.when(sx == 1)
    def _():
        hop_x().wait_recv()

    def row(k, t):
        return vec[k, t]

    def forward(k, carry):
        def ready(t):
            @pl.when(core == k)
            def _():
                loads[t].wait()

            @pl.when(core != k)
            def _():
                wcopies[t].wait_recv()

        xpad[k, :, :, 8 : 8 + width, :] = X[k].astype(F32)
        ready(0)
        for half in range(chans // 128):
            lanes = slice(half * 128, half * 128 + 128)
            acc = [None] * height
            for j in range(7):
                shifted = [xpad[k, :, h, 5 + j : 5 + j + width, lanes] for h in range(height)]
                for i in range(7):
                    tap = vec[k, 7 * i + j, :, lanes][None]
                    for h in range(height):
                        if 0 <= h + i - 3 < height:
                            term = shifted[h + i - 3] * tap
                            acc[h] = term if acc[h] is None else acc[h] + term
            bias = vec[k, 49, :, lanes][None]
            for h in range(height):
                cv[:, h, :, lanes] = acc[h] + bias
        conv = cv[...].reshape(rows, chans)
        mean = jnp.sum(conv, axis=1, keepdims=True) * (1.0 / chans)
        centered = conv - mean
        var = jnp.sum(centered * centered, axis=1, keepdims=True) * (1.0 / chans)
        rstd = lax.rsqrt(var + 1e-06)
        xhat = centered * rstd
        XH[k] = xhat
        RSTD[k] = jnp.broadcast_to(rstd, (rows, 128))
        normed = (xhat * row(k, 50) + row(k, 51)).astype(BF16)
        NB[k] = normed
        ready(1)
        ready(2)
        proj = jnp.zeros((rows, chans), F32)
        for q in range(quarters):
            cols = slice(q * chans, (q + 1) * chans)
            pre = dot(normed, win[k, :, cols]) + row(k, 54 + q)
            cumulative = 0.5 * (1.0 + lax.erf(pre * 0.7071067811865476))
            act = (pre * cumulative).astype(BF16)
            ACT[k, :, cols] = act
            SL[k, :, cols] = cumulative + pre * jnp.exp(-0.5 * pre * pre) * 0.3989422804014327
            proj = proj + dot(act, wout[k, cols, :])
        proj = proj + row(k, 52)
        PJ[k] = proj
        out = X[k].astype(F32).reshape(rows, chans) + row(k, 53) * proj
        X[k + 1] = out.astype(BF16).reshape(pair, height, width, chans)
        return carry

    lax.fori_loop(0, 2, forward, 0)
    if len(reaches) > 1:
        heard(0)
        tell(1)

    @pl.when(sx == 0)
    def _():
        hop_x().start()
        hop_g().wait_recv()

    def grad_copy(k, t):
        at = pl.ds(t * chans, chans)
        return copy(PG.at[k, at], RG.at[at], csend.at[t], crecv.at[t], sib)

    def vec_copy(k):
        return copy(GV.at[k], RV, cvsend, cvrecv, sib)

    def ig_copy(k):
        return copy(G.at[k], IG.at[my_micros], isend, irecv, sib)

    def plane_copy(c, r):
        lo, hi = chunks[c]
        q, dev = plane_dev(r)
        at = pl.ds(lo * zrows, (hi - lo) * zrows)
        return copy(S.at[q, at], RB.at[r, at], psend.at[c, r], precv.at[c, r], dev)

    def plane_vec_copy(r):
        q, dev = plane_dev(r)
        return copy(SV.at[q], RBV.at[r], pvsend.at[r], pvrecv.at[r], dev)

    every = range(len(chunks))
    early, late = every[:2], every[2:]

    def chip_sum(k, some):
        if 0 in some:
            for t in range(2 * quarters):
                grad_copy(k, t).wait_recv()
        for c in some:
            lo, hi = chunks[c]

            @pl.loop(1, nplane + 1)
            def _(r):
                p = lax.rem(plane + r, nplane)
                for s in range(lo, hi):
                    start = p * part + z_at(offset(s)) * zrows
                    at = pl.ds(pl.multiple_of(start, zrows), zrows)
                    S[p, s * zrows : (s + 1) * zrows, :] = (
                        PG[k, at, :].astype(F32) + RG[at, :].astype(F32)
                    ).astype(BF16)

                @pl.when(r < nplane)
                def _():
                    plane_copy(c, r).start()

    def chip_vec_sum(k):
        vec_copy(k).wait_recv()
        for t in range(nplane):
            at_row, at_col = (t // vcols) * VTILE, (t % vcols) * vlanes
            tile = (slice(at_row, at_row + VTILE), slice(at_col, at_col + vlanes))
            SV[t] = (GV[(k,) + tile] + RV[tile]).astype(BF16)

        @pl.loop(1, nplane)
        def _(r):
            plane_vec_copy(r).start()

    def backward(step, carry):
        k = 1 - step

        if len(reaches) > 2:

            @pl.when(step == 1)
            def _():
                heard(1)
                tell(2)

        @pl.when((sx == 0) & (core == 1) & (k == 0))
        def _():
            chip_sum(1, every)

        gf = G[k + 1].astype(F32).reshape(rows, chans)
        GV[k, 53:54, :] = over_rows(gf * PJ[k])
        dproj = gf * row(k, 53)
        GV[k, 52:53, :] = over_rows(dproj)
        dproj_b = dproj.astype(BF16)
        normed = NB[k]
        dn = jnp.zeros((rows, chans), F32)
        for q in range(quarters):
            cols = slice(q * chans, (q + 1) * chans)
            dact = dot_nt(dproj_b, wout[k, cols, :])
            PG[k, hidden + q * chans : hidden + (q + 1) * chans, :] = dot_tn(
                ACT[k, :, cols], dproj_b
            ).astype(BF16)
            dpre = dact * SL[k, :, cols]
            GV[k, 54 + q : 55 + q, :] = over_rows(dpre)
            dpre_b = dpre.astype(BF16)
            PG[k, cols, :] = dot_tn(normed, dpre_b).astype(BF16)

            @pl.when(core != k)
            def _():
                grad_copy(k, quarters + q).start()
                grad_copy(k, q).start()

            dn = dn + dot_nt(dpre_b, win[k, :, cols])

        xhat = XH[k]
        GV[k, 50:51, :] = over_rows(dn * xhat)
        GV[k, 51:52, :] = over_rows(dn)
        dxh = dn * row(k, 50)
        m1 = jnp.sum(dxh, axis=1, keepdims=True) * (1.0 / chans)
        m2 = jnp.sum(dxh * xhat, axis=1, keepdims=True) * (1.0 / chans)
        rstd = RSTD[k][:, 0:1]
        dconv = (dxh - m1 - xhat * m2) * rstd
        GV[k, 49:50, :] = over_rows(dconv)
        xpad[k, :, :, 8 : 8 + width, :] = dconv.reshape(pair, height, width, chans)
        for half in range(chans // 128):
            lanes = slice(half * 128, half * 128 + 128)
            acc = [G[k + 1, :, h, :, lanes].astype(F32) for h in range(height)]
            for j in range(7):
                shifted = [xpad[k, :, h, 11 - j : 11 - j + width, lanes] for h in range(height)]
                for i in range(7):
                    tap = vec[k, 7 * i + j, :, lanes][None]
                    for h in range(height):
                        if 0 <= h - i + 3 < height:
                            acc[h] = acc[h] + shifted[h - i + 3] * tap
            for h in range(height):
                G[k, :, h, :, lanes] = acc[h].astype(BF16)

        @pl.when(core != k)
        def _():
            ig_copy(k).start()

        @pl.when(core == k)
        def _():
            IG[my_micros] = G[k]

        return carry

    def tap_grads(step, carry):
        k = 1 - step
        for half in range(chans // 128):
            lanes = slice(half * 128, half * 128 + 128)
            xs = [X[k, :, h, :, lanes].astype(F32) for h in range(height)]
            for j in range(7):
                shifted = [xpad[k, :, h, 11 - j : 11 - j + width, lanes] for h in range(height)]
                for i in range(7):
                    t = 7 * i + j
                    total = None
                    for h in range(height):
                        if 0 <= h - i + 3 < height:
                            term = xs[h] * shifted[h - i + 3]
                            total = term if total is None else total + term
                    GV[k, t : t + 1, lanes] = over_rows(total.reshape(pair * width, 128))

        @pl.when(core != k)
        def _():
            vec_copy(k).start()

        return carry

    lax.fori_loop(0, 2, backward, 0)

    @pl.when(sx == 1)
    def _():
        hop_g().start()

    lax.fori_loop(0, 2, tap_grads, 0)

    @pl.when(sx == 1)
    def _():
        hop_g().wait_send()

    @pl.when((core == 0) | (sx == 1))
    def _():
        chip_sum(core, early)

    chip_vec_sum(core)

    @pl.when((core == 0) | (sx == 1))
    def _():
        chip_sum(core, late)

    def z_copy(s):
        src = S.at[plane, pl.ds(s * zrows, zrows)]
        return copy(src, ZB.at[s], zsend.at[s], zrecv.at[s], {"z": z_at(offset(s))})

    if reaches:
        heard(len(reaches) - 1)

    def vec_up():
        r = lax.rem(owner - z + nz, nz)
        return copy(RBV.at[0], VZ.at[r], vsend, vrecv.at[r], {"z": owner})

    def vec_share():
        @pl.loop(1, nplane)
        def _(r):
            plane_vec_copy(r).wait_recv()

        vacc = SV[plane].astype(F32)
        for r in range(1, nplane):
            vacc = vacc + RBV[r].astype(F32)
        RBV[0] = vacc.astype(BF16)

        @pl.when(z != owner)
        def _():
            vec_up().start()

    for c, (lo, hi) in enumerate(chunks):
        if c == min(2, len(chunks) - 1):
            vec_share()

        @pl.loop(1, nplane)
        def _(r):
            plane_copy(c, r).wait_recv()

        for s in reversed(range(lo, hi)):
            at = slice(s * zrows, (s + 1) * zrows)
            acc = S[plane, at, :].astype(F32)
            for t in range(1, nplane):
                acc = acc + RB[t, at, :].astype(F32)
            if s > 0:
                S[plane, at, :] = acc.astype(BF16)
                z_copy(s).start()
            else:
                ZB[0] = acc.astype(BF16)

    def share_copy(s):
        return copy(
            GATH.at[plane, pl.ds(0, zrows)],
            GATH.at[plane, pl.ds(mirror(s, nz) * zrows, zrows)],
            asend.at[s], arecv.at[mirror(s, nz)], {"z": z_at(offset(s))},
        )

    def group_copy(g, r):
        lo, hi = groups[g]
        at = pl.ds(lo * zrows, (hi - lo) * zrows)
        return copy(
            GATH.at[plane, at], GATH.at[plane, at], gsend.at[g, r], grecv.at[g, r],
            plane_dev(r)[1],
        )

    for s in range(1, nz):
        z_copy(s).wait_recv()
    share = ZB[0].astype(F32)
    for s in range(1, nz):
        share = share + ZB[s].astype(F32)
    GATH[plane, 0:zrows, :] = share.astype(BF16)
    for s in [*range(1, min(5, nz)), *reversed(range(5, nz))]:
        share_copy(s).start()

    @pl.loop(1, nplane)
    def _(r):
        group_copy(0, r).start()

    SQS[2 * sx + core] = jnp.broadcast_to(jnp.sum(share * share), (1, 128))

    def vec_down(r):
        return copy(
            GATHV.at[plane], GATHV.at[plane], bsend.at[r], brecv, {"z": z_at(r)}
        )

    @pl.when(z == owner)
    def _():
        @pl.loop(1, nz)
        def _(r):
            copy(VZ.at[r], VZ.at[r], vsend, vrecv.at[r], {"z": owner}).wait_recv()

        total = RBV[0].astype(F32)
        for r in range(1, nz):
            total = total + VZ[r].astype(F32)
        GATHV[plane] = total.astype(BF16)

        @pl.loop(1, nz)
        def _(r):
            vec_down(r).start()

        SQS[2 * sx + core] = SQS[2 * sx + core] + jnp.broadcast_to(
            jnp.sum(total * total), (1, 128)
        )

    def sq_block(t):
        at = SQS.at[2 * sx + core]
        return copy(at, at, qsend.at[t], qrecv.at[t], (sib, far, diag)[t])

    def sq_z(r):
        at = SQZ.at[z]
        return copy(at, at, qzsend.at[r], qzrecv.at[r], {"z": z_at(r)})

    def sq_plane(r):
        at = SQP.at[plane]
        return copy(at, at, qpsend.at[r], qprecv.at[r], plane_dev(r)[1])

    for t in range(3):
        sq_block(t).start()

    def forward_group(g):
        lo, hi = groups[g]
        for s in range(lo, hi):
            at = GATH.at[plane, pl.ds(s * zrows, zrows)]
            copy(at, at, asend.at[s], arecv.at[s], sib).wait_recv()

        @pl.loop(1, nplane)
        def _(r):
            group_copy(g, r).start()

    forward_group(1)
    mates = (2 * sx + 1 - core, 2 * (1 - sx) + core, 2 * (1 - sx) + 1 - core)
    for t in range(3):
        at = SQS.at[mates[t]]
        copy(at, at, qsend.at[t], qrecv.at[t], sib).wait_recv()
    SQZ[z] = (SQS[0] + SQS[1]) + (SQS[2] + SQS[3])

    @pl.loop(1, nz)
    def _(r):
        sq_z(r).start()

    for g in range(2, len(groups)):
        forward_group(g)

    def vec_out(r):
        at = GATHV.at[plane]
        return copy(at, at, gvsend.at[r], gvrecv.at[r], plane_dev(r)[1])

    @pl.when(z != owner)
    def _():
        vec_down(1).wait_recv()

    @pl.loop(1, nplane)
    def _(r):
        vec_out(r).start()

    @pl.loop(1, nz)
    def _(r):
        at = SQZ.at[z_at(-r)]
        copy(at, at, qzsend.at[r], qzrecv.at[r], sib).wait_recv()

    total = SQZ[0]
    for t in range(1, nz):
        total = total + SQZ[t]
    SQP[plane] = total

    @pl.loop(1, nplane)
    def _(r):
        sq_plane(r).start()

    def store(q):
        return pltpu.make_async_copy(GATH.at[q], gath_ref.at[q], store_sem.at[q])

    store(plane).start()
    ig_copy(0).wait_recv()
    ig_out = pltpu.make_async_copy(IG, ig_ref, load_sem.at[4])
    ig_out.start()

    for c in wcopies:
        c.wait_send()

    @pl.when(sx == 0)
    def _():
        hop_x().wait_send()

    ig_copy(0).wait_send()
    for t in range(2 * quarters):
        grad_copy(0, t).wait_send()
    vec_copy(0).wait_send()

    @pl.loop(1, nplane)
    def _(r):
        for c in range(len(chunks)):
            plane_copy(c, r).wait_send()
        plane_vec_copy(r).wait_send()

    for s in range(1, nz):
        z_copy(s).wait_send()
        share_copy(s).wait_send()

    @pl.when(z != owner)
    def _():
        vec_up().wait_send()

    @pl.when(z == owner)
    def _():
        @pl.loop(1, nz)
        def _(r):
            vec_down(r).wait_send()

    for t in range(3):
        sq_block(t).wait_send()

    @pl.loop(1, nz)
    def _(r):
        sq_z(r).wait_send()

    @pl.loop(1, nplane)
    def _(r):
        q = lax.rem(plane - r + nplane, nplane)
        for g, (lo, hi) in enumerate(groups):
            at = GATH.at[q, pl.ds(lo * zrows, (hi - lo) * zrows)]
            copy(at, at, gsend.at[g, r], grecv.at[g, r], sib).wait_recv()
        store(q).start()
        copy(GATHV.at[q], GATHV.at[q], gvsend.at[r], gvrecv.at[r], sib).wait_recv()
        copy(SQP.at[q], SQP.at[q], qpsend.at[r], qprecv.at[r], sib).wait_recv()

    gathv_ref[...] = GATHV[...]
    total = SQP[0]
    for t in range(1, nplane):
        total = total + SQP[t]
    factor = jnp.minimum(1.0, (params**0.5) * lax.rsqrt(total + 1e-06))
    fac_ref[...] = jnp.broadcast_to(factor, fac_ref.shape)

    @pl.loop(1, nplane)
    def _(r):
        for g in range(len(groups)):
            group_copy(g, r).wait_send()
        vec_out(r).wait_send()
        sq_plane(r).wait_send()

    @pl.loop(0, nplane)
    def _(q):
        store(q).wait()

    ig_out.wait()


def scale_kernel(nz, gath, gathv, fac, ig, o_in, o_out, o_vec, o_ig):
    nplane, part, chans = gath.shape
    hidden = o_in.shape[1]
    quarters = hidden // chans
    zrows = part // nz
    vlanes = gathv.shape[2]
    vcols = chans // vlanes
    z = lax.axis_index("z")
    f = fac[0:1, 0:1]
    per = chans // zrows
    for s in range(nz):
        q = lax.rem(z + offset(s) + nz, nz)
        for p in range(nplane):
            piece = gath[p, s * zrows : (s + 1) * zrows, :].astype(F32) * f
            first = p * part
            if first < hidden:
                if part <= chans:
                    at = pl.ds(pl.multiple_of(first % chans + q * zrows, zrows), zrows)
                    o_in[at, first // chans * chans : first // chans * chans + chans] = piece
                else:
                    for t in range(part // chans):
                        @pl.when(q // per == t)
                        def _():
                            at = pl.ds(pl.multiple_of(lax.rem(q, per) * zrows, zrows), zrows)
                            o_in[at, first + t * chans : first + t * chans + chans] = piece
            else:
                at = pl.ds(pl.multiple_of(first - hidden + q * zrows, zrows), zrows)
                o_out[at, :] = piece
    for p in range(nplane):
        at_row, at_col = (p // vcols) * VTILE, (p % vcols) * vlanes
        tile = gathv[p].astype(F32) * f
        for t in range(min(VTILE, o_vec.shape[0] - at_row)):
            o_vec[at_row + t, :, at_col : at_col + vlanes] = tile[t : t + 1, :]
    o_ig[...] = ig[...]


def per_device(dims, inputs, out_grad, w_in, w_out, vector_params):
    nz, ny, nx, params = dims
    nplane = ny * nx
    micros, _, height, width, chans = inputs.shape
    hidden = w_in.shape[2]
    vrows = vector_params.shape[1]
    pair = micros // 2
    rows = pair * height * width
    part = 2 * hidden // nplane
    zrows = part // nz
    vlanes = VPAD * chans // nplane // VTILE
    chunks, groups = spans(nz)
    maps = (micros, height, width, chans)
    small = (pair, height, width, chans)
    vm = pltpu.VMEM
    dma = pltpu.SemaphoreType.DMA
    in_vmem = pl.BlockSpec(memory_space=pltpu.VMEM)
    in_hbm = pl.BlockSpec(memory_space=pltpu.HBM)
    gath, gathv, fac, ig = pl.pallas_call(
        functools.partial(relay_kernel, dims),
        out_shape=(
            jax.ShapeDtypeStruct((nplane, part, chans), BF16),
            jax.ShapeDtypeStruct((nplane, VTILE, vlanes), BF16),
            jax.ShapeDtypeStruct((8, 128), F32),
            jax.ShapeDtypeStruct(maps, BF16),
        ),
        in_specs=[in_hbm] * 5,
        out_specs=(in_hbm, in_vmem, in_vmem, in_hbm),
        scratch_shapes=[
            vm((2, chans, hidden), BF16),
            vm((2, hidden, chans), BF16),
            vm((2, vrows, 1, chans), F32),
            vm((3,) + small, BF16),
            vm((3,) + small, BF16),
            vm((2, pair, height, width + 16, chans), F32),
            vm(small, F32),
            vm((2, rows, chans), F32),
            vm((2, rows, 128), F32),
            vm((2, rows, chans), BF16),
            vm((2, rows, hidden), BF16),
            vm((2, rows, hidden), F32),
            vm((2, rows, chans), F32),
            vm((2, 2 * hidden, chans), BF16),
            vm((2, VPAD, chans), F32),
            vm((2 * hidden, chans), BF16),
            vm((VPAD, chans), F32),
            vm(maps, BF16),
            vm((nplane, part, chans), BF16),
            vm((nplane, part, chans), BF16),
            vm((nplane, VTILE, vlanes), BF16),
            vm((nplane, VTILE, vlanes), BF16),
            vm((nz, zrows, chans), BF16),
            vm((nz, VTILE, vlanes), BF16),
            vm((nplane, part, chans), BF16),
            vm((nplane, VTILE, vlanes), BF16),
            vm((4, 1, 128), F32),
            vm((nz, 1, 128), F32),
            vm((nplane, 1, 128), F32),
            dma((5,)),
            dma((3,)), dma((3,)),
            dma, dma,
            dma, dma,
            dma((2 * hidden // chans,)), dma((2 * hidden // chans,)),
            dma, dma,
            dma((len(chunks), nplane)), dma((len(chunks), nplane)),
            dma((nplane,)), dma((nplane,)),
            dma((nz,)), dma((nz,)),
            dma, dma((nz,)),
            dma((nz,)), dma,
            dma((nz,)), dma((nz,)),
            dma((len(groups), nplane)), dma((len(groups), nplane)),
            dma((nplane,)), dma((nplane,)),
            dma((3,)), dma((3,)),
            dma((nz,)), dma((nz,)),
            dma((nplane,)), dma((nplane,)),
            dma((nplane,)),
            pltpu.SemaphoreType.REGULAR((3,)),
        ],
        compiler_params=pltpu.CompilerParams(
            collective_id=0, has_side_effects=True, vmem_limit_bytes=60 * 1024 * 1024
        ),
        name="relay",
    )(
        inputs.reshape(maps), out_grad.reshape(maps), w_in[0], w_out[0],
        jnp.swapaxes(vector_params, 0, 1),
    )
    o_in, o_out, o_vec, o_ig = pl.pallas_call(
        functools.partial(scale_kernel, nz),
        out_shape=(
            jax.ShapeDtypeStruct((chans, hidden), F32),
            jax.ShapeDtypeStruct((hidden, chans), F32),
            jax.ShapeDtypeStruct((vrows, 1, chans), F32),
            jax.ShapeDtypeStruct(maps, BF16),
        ),
        in_specs=[in_vmem] * 4,
        out_specs=(in_vmem,) * 4,
        compiler_params=pltpu.CompilerParams(vmem_limit_bytes=60 * 1024 * 1024),
        name="scale",
    )(gath, gathv, fac, ig)
    return (
        o_ig.reshape((1, micros, 1, height, width, chans)),
        o_in[None],
        o_out[None],
        jnp.swapaxes(o_vec, 0, 1),
    )


def solution(mesh):
    nx = 2
    ny = 4
    nz = mesh.shape["dp"] // (nx * ny)
    return program_on(mesh, nz, ny, nx)


def program_on(mesh, nz, ny, nx, params=2156544):
    split = Mesh(mesh.devices.reshape(2, 2, nz, ny, nx), ("sx", "core", "z", "y", "xl"))
    dp = ("z", "y", "xl")
    seg = ("sx", "core")
    in_specs = (
        P(None, dp, None, None, None),
        P(None, dp, None, None, None),
        P(seg, None, None),
        P(seg, None, None),
        P(seg, None, None),
    )
    out_specs = (
        P(seg, None, dp, None, None, None),
        P(seg, None, None),
        P(seg, None, None),
        P(seg, None, None),
    )
    return jax.shard_map(
        functools.partial(per_device, (nz, ny, nx, params)),
        mesh=split, in_specs=in_specs, out_specs=out_specs, check_vma=False,
    )
```
